128 devices in a mesh: comp: 2 (over x_hi), gx: 8 (over z, core), gy: 8 (over x_lo, y).
Axes of the slice: x: 4 (x_hi: 2, x_lo: 2; x = x_hi * 2 + x_lo), y: 4, z: 4, core: 2. Of those that a mesh axis runs over, the one named last changes fastest.
Arguments:
- state: float32 [2, 4, 16, 1024, 1024], P('comp', None, None, 'gx', 'gy'), may hold values from -6 to 6
- horiz_coef: float32 [2, 4], P('comp'), may hold values from 0.03 to 0.12
- vert_coef: float32 [2, 1024, 1024], P('comp', 'gx', 'gy'), may hold values from 0.02 to 0.3
- couple_rate: float32 [2, 4], P('comp'), may hold values from 0.2 to 0.8
- sea_mask: int32 [2, 1024, 1024], P('comp', 'gx', 'gy'), may hold values 0 or 1
- dest_block: int32 [2, 1024, 8, 4], P('comp', 'gx', 'gy'), may hold values from 0 to 8191, as said below
- entry_count: int32 [2, 1024, 8], P('comp', 'gx', 'gy'), may hold values from 1 to 4
- remap_weight: bfloat16 [2, 1024, 8, 4, 128, 128], P('comp', 'gx', 'gy'), may hold values from -0.375 to 0.375
Outputs:
- advanced: float32 [2, 4, 16, 1024, 1024], P('comp', None, None, 'gx', 'gy')
The draws below stay inside these ranges and needn't reach their ends.
Inputs may be any that keep to these rules, and one draw needn't show every extreme that they name: `dest_block`: each list entry names a block of the other component: id // 128 is a device of that component's 8 x 8 tiles in row-major order and id % 128 a tile row on it. Over the live entries of one device, at most 8 name blocks of any one device of the other component, and in every draw some pair of devices has exactly 8. Padded entries hold arbitrary ids.
All inputs are finite; a program needn't handle non-finite values. No bound on the sum of `sea_mask` on one device may be relied on, other than what follows from the above.
Results may differ from the reference program's by a relative error of at most 0.0011.
Values sent between devices are 32-bit elements; how exact they have to be, the bound alone decides.
No kernel may reach another device: no remote copies, remote signals or barrier semaphores. Data moves between devices by JAX's collectives and lax.ppermute only.
A program may use at most 128 MiB of HBM per device.

```python
import math
import jax
import jax.numpy as jnp
from jax import lax

NV = 4
LEV = 16
BLK = 128
FAN = 4
STEPS = 2
TX = 128
NX = 1024
NY = 1024
CAP = 8
N_GX = 8
N_GY = 8


def draw_lists(key):

    def one_device(device_key):
        subkeys = jax.random.split(device_key, 6)
        entries_all = TX * FAN
        peer_count = N_GX * N_GY
        counts = jax.random.randint(subkeys[0], (TX,), 1, FAN + 1)
        usable = (jnp.arange(FAN)[None, :] < counts[:, None]).reshape(entries_all)
        shuffled = jax.random.permutation(subkeys[1], entries_all)
        scores = jnp.where(usable, shuffled, shuffled + entries_all)
        ranking = jnp.argsort(jnp.argsort(scores))
        leading = jax.random.randint(subkeys[2], (), 0, peer_count)
        slot_labels = (jnp.arange(peer_count * CAP) // CAP + leading) % peer_count
        remainder = jax.random.permutation(subkeys[3], slot_labels[CAP:])
        slot_table = jnp.concatenate([slot_labels[:CAP], remainder])
        filler = jax.random.randint(subkeys[4], (entries_all,), 0, peer_count)
        chosen = slot_table[jnp.minimum(ranking, peer_count * CAP - 1)]
        target_dev = jnp.where(usable, chosen, filler)
        target_row = jax.random.randint(subkeys[5], (entries_all,), 0, TX)
        return ((target_dev * TX + target_row).reshape(TX, FAN), counts)
    device_keys = jax.random.split(key, 2 * N_GX * N_GY)
    targets, counts = jax.vmap(one_device)(device_keys)
    targets = targets.reshape(2, N_GX, N_GY, TX, FAN).transpose(0, 1, 3, 2, 4).reshape(2, TX * N_GX, N_GY, FAN)
    counts = counts.reshape(2, N_GX, N_GY, TX).transpose(0, 1, 3, 2).reshape(2, TX * N_GX, N_GY)
    return (targets.astype(jnp.int32), counts.astype(jnp.int32))


def draw_dest_block(key, part):
    shared = draw_lists(key)
    return shared[0]


def draw_entry_count(key, part):
    shared = draw_lists(key)
    return shared[1]


def place_ends(result, key, smallest, top_value):
    longest = result.shape.index(max(result.shape))
    spots = []
    for shift in (0, 1):
        where = [jax.random.randint(jax.random.fold_in(key, axis), (), 0, length) for axis, length in enumerate(result.shape)]
        where[longest] = (where[longest] + shift) % result.shape[longest]
        spots.append(tuple(where))
    return result.at[spots[0]].set(smallest).at[spots[1]].set(top_value)


def shard_levels(rng, dims, cuts, low, high):
    def one(axis_at, parts):
        heights = jax.random.uniform(jax.random.fold_in(jax.random.fold_in(rng, 6), axis_at), (parts,), jnp.float32, low / len(cuts), high / len(cuts))
        return jnp.repeat(jnp.exp(heights), dims[axis_at] // parts).reshape((-1,) + (1,) * (len(dims) - axis_at - 1))

    loudness = one(*cuts[0])
    for cut in cuts[1:]:
        loudness = loudness * one(*cut)
    return loudness


def bell_draw(key, dims, deviation, most, cuts=(), kind=jnp.bfloat16):
    values = deviation * jax.random.normal(key, dims, jnp.float32)
    if cuts:
        values = values * shard_levels(key, dims, cuts, -0.22, 0.18)
    return jnp.clip(values, -most, most).astype(kind)


def setup_inputs(seed: int = 0) -> dict:
    splits = jax.random.split(jax.random.key(seed), 9)
    state = bell_draw(splits[0], (2, NV, LEV, NX, NY), 1.0, 6.0, ((0, 2), (3, 8), (4, 8)), jnp.float32)
    horiz_coef = jnp.clip(0.03 + 0.089999998 * jax.random.uniform(splits[1], (2, NV), jnp.float32) ** shard_levels(splits[1], (2, NV), ((0, 2),), -0.2, 0.2), 0.03, 0.12)
    vert_coef = jnp.clip(jnp.exp(math.log(0.3) - 2.7080503 * jax.random.uniform(splits[2], (2, NX, NY), jnp.float32) ** shard_levels(splits[2], (2, NX, NY), ((0, 2), (1, 8), (2, 8)), -0.2, 0.2)), 0.02, 0.3)
    couple_rate = jnp.clip(0.2 + 0.6 * jax.random.uniform(splits[3], (2, NV), jnp.float32) ** shard_levels(splits[3], (2, NV), ((0, 2),), -0.2, 0.2), 0.2, 0.8)
    sea_mask = place_ends((jax.random.randint(splits[4], (2, NX, NY), 0, 4) < 3).astype(jnp.int32), jax.random.fold_in(splits[4], 1), 0, 1)
    dest_block = draw_dest_block(jax.random.fold_in(splits[8], 71), 0)
    entry_count = draw_entry_count(jax.random.fold_in(splits[8], 71), 0)
    remap_weight = bell_draw(splits[7], (2, NX, N_GY, FAN, BLK, BLK), (2 * BLK) ** -0.5, 0.375, ((0, 2), (1, 8), (2, 8)))
    return {"state": state, "horiz_coef": horiz_coef, "vert_coef": vert_coef, "couple_rate": couple_rate, "sea_mask": sea_mask, "dest_block": dest_block, "entry_count": entry_count, "remap_weight": remap_weight}


def mix_levels(values, coef, axis):
    count = values.shape[axis]
    upper = lax.slice_in_dim(values, 1, count, axis=axis)
    lower = lax.slice_in_dim(values, 0, count - 1, axis=axis)
    zero_plane = jnp.zeros_like(lax.slice_in_dim(values, 0, 1, axis=axis))
    from_above = jnp.concatenate([upper - lower, zero_plane], axis=axis)
    from_below = jnp.concatenate([zero_plane, lower - upper], axis=axis)
    return values + coef * (from_above + from_below)


def reference(state, horiz_coef, vert_coef, couple_rate, sea_mask, dest_block, entry_count, remap_weight):
    surface = state[:, :, 0].astype(jnp.bfloat16)
    blocks = surface.reshape(2, NV, NX, N_GY, BLK).transpose(0, 2, 3, 1, 4).reshape(2 * NX, N_GY, NV, BLK)
    weights = remap_weight.reshape(2 * NX, N_GY, FAN, BLK, BLK)

    def remap_row(pair):
        row_blocks, row_weights = pair
        return jnp.einsum("gvk,gfkj->gfvj", row_blocks.astype(jnp.float32), row_weights.astype(jnp.float32))

    partial_value = lax.map(remap_row, (blocks, weights))
    partial_value = partial_value.reshape(2 * NX * N_GY * FAN, NV * BLK)
    usable = jnp.arange(FAN)[None, None, None, :] < entry_count[:, :, :, None]
    section = jnp.arange(2, dtype=jnp.int32)[:, None, None, None]
    other = 1 - section
    device_of = dest_block // TX
    row_global = (device_of // N_GY) * TX + dest_block % TX
    column_block = device_of % N_GY
    flat_target = other * (NX * N_GY) + row_global * N_GY + column_block
    flat_target = jnp.where(usable, flat_target, 2 * NX * N_GY).astype(jnp.int32)
    summed = jax.ops.segment_sum(partial_value, flat_target.reshape(-1), num_segments=2 * NX * N_GY + 1)
    imported = summed[:2 * NX * N_GY].reshape(2, NX, N_GY, NV, BLK).transpose(0, 3, 1, 2, 4).reshape(2, NV, NX, NY)
    horiz_rate = horiz_coef[:, :, None, None, None]
    vert_rate = vert_coef[:, None, None, :, :]
    relax_rate = couple_rate[:, :, None, None] * sea_mask.astype(jnp.float32)[:, None, :, :]
    values = state
    for substep in range(STEPS):
        padded = jnp.pad(values, ((0, 0), (0, 0), (0, 0), (1, 1), (1, 1)))
        laplace = padded[:, :, :, 2:, 1:-1] + padded[:, :, :, :-2, 1:-1]
        laplace = laplace + padded[:, :, :, 1:-1, 2:] + padded[:, :, :, 1:-1, :-2] - 4.0 * values
        values = values + horiz_rate * laplace
        values = mix_levels(values, vert_rate, 2)
        bottom = values[:, :, 0]
        bottom = bottom + relax_rate * (imported - bottom)
        values = jnp.concatenate([bottom[:, :, None], values[:, :, 1:]], axis=2)
    return values
```

```python
import jax
import jax.numpy as jnp
from jax import lax
from jax.experimental import pallas as pl
from jax.experimental.pallas import tpu as pltpu
from jax.sharding import PartitionSpec as P

NV = 4
LEV = 16
T = 128
FAN = 4
CAP = 8
PEERS = 64
SLOTS = CAP + 1
HALF = 64
VMEM = 40 * 1024 * 1024
WIDE = 58 * 1024 * 1024

f32 = jnp.float32
i32 = jnp.int32


def params(limit=VMEM):
    return pltpu.CompilerParams(vmem_limit_bytes=limit)


def lanes(rows):
    return lax.broadcasted_iota(i32, (rows, T), 1)


def subl(rows):
    return lax.broadcasted_iota(i32, (rows, T), 0)


def unshift(v):
    return lax.rem((NV - v) * 32, T)


def cut(flags, column=None):
    if column is None:
        return flags[0], flags[1]
    return jnp.where((column & 1) == 0, flags[2], flags[3])


def edge_kernel(flags, mask, state, first, last, cols, surf, tile, sea_int, sems):
    loads = [pltpu.make_async_copy(state.at[0, v], tile.at[v], sems.at[v]) for v in range(NV)]
    loads.append(pltpu.make_async_copy(mask.at[0], sea_int, sems.at[NV]))
    for load in loads:
        load.start()
    up, down = cut(flags)
    lane = lanes(HALF)
    keep = cut(flags, lane)
    for v in range(NV):
        loads[v].wait()
        surf[pl.ds(v, T, stride=NV), :] = tile[v, 0]
        for l in range(LEV):
            first[v, l : l + 1, :] = tile[v, l, 0:1, :] * up
            last[v, l : l + 1, :] = tile[v, l, T - 1 : T, :] * down
        for lo in range(0, T, HALF):
            acc = jnp.zeros((HALF, T), f32) if v == 0 else cols[0, lo : lo + HALF, :]
            for l in range(LEV):
                p = v * LEV + l
                turned = pltpu.roll(tile[v, l, lo : lo + HALF, :], (2 * p + 1) % T, 1)
                acc = jnp.where((lane >> 1) == p, turned, acc)
            cols[0, lo : lo + HALF, :] = acc * keep if v == NV - 1 else acc
    loads[NV].wait()
    sea = sea_int[...].astype(f32)
    first[NV] = jnp.broadcast_to(sea[0:1, :] * up, (LEV, T))
    last[NV] = jnp.broadcast_to(sea[T - 1 : T, :] * down, (LEV, T))
    cols[1] = pltpu.roll(sea, 1, 1) * cut(flags, lanes(T))


def edges(flags, mask, state):
    vmem = pl.BlockSpec(memory_space=pltpu.VMEM)
    hbm = pl.BlockSpec(memory_space=pltpu.HBM)
    return pl.pallas_call(
        edge_kernel,
        in_specs=[pl.BlockSpec(memory_space=pltpu.SMEM), hbm, hbm],
        out_specs=[vmem] * 4,
        out_shape=[
            jax.ShapeDtypeStruct((NV + 1, LEV, T), f32),
            jax.ShapeDtypeStruct((NV + 1, LEV, T), f32),
            jax.ShapeDtypeStruct((2, T, T), f32),
            jax.ShapeDtypeStruct((T * NV, T), f32),
        ],
        scratch_shapes=[
            pltpu.VMEM((NV, LEV, T, T), f32),
            pltpu.VMEM((T, T), i32),
            pltpu.SemaphoreType.DMA((NV + 1,)),
        ],
        compiler_params=params(WIDE),
        cost_estimate=pl.CostEstimate(flops=4 << 20, bytes_accessed=5 << 20, transcendentals=0),
        name="edges",
    )(flags, mask, state)


CHUNKS = 16


def remap_kernel(dest, count, me, surf, weight, out, blocks, used, label, sems):
    rows = T // CHUNKS

    def fetch(c):
        piece = pl.ds(c * rows, rows)
        return pltpu.make_async_copy(weight.at[0, piece, 0], blocks.at[piece], sems.at[c])

    for c in range(CHUNKS):
        fetch(c).start()
    out[...] = jnp.zeros_like(out)

    def clear(i, _):
        used[i] = 0
        for k in range(CAP):
            label[i * CAP + k] = 0
        return 0

    lax.fori_loop(0, PEERS, clear, 0)

    def chunk(c, _):
        fetch(c).wait()
        for r in range(rows):
            row = c * rows + r
            at_pair = pl.multiple_of(c * rows * NV + (r // 2) * 8, 8)
            pair = surf[pl.ds(at_pair, 8), :].astype(jnp.bfloat16)
            live_count = count[row]
            for f in range(FAN):
                target = dest[row * FAN + f]
                peer = lax.shift_right_logical(target, 7) & (PEERS - 1)
                live = f < live_count
                at = used[peer]
                used[peer] = at + jnp.where(live, 1, 0)
                label[jnp.where(live, peer * CAP + at, PEERS * CAP)] = (target & (T - 1)) + 1
                slot = jnp.where(live, peer * SLOTS + at, CAP)
                product = jnp.dot(pair, blocks[row, f], preferred_element_type=f32)
                half = (r % 2) * NV
                out[slot] = product[half : half + NV, :]
        return 0

    lax.fori_loop(0, CHUNKS, chunk, 0)
    place = lax.broadcasted_iota(i32, (NV, T), 0) * T + lax.broadcasted_iota(i32, (NV, T), 1)
    place = place - me[0] * CAP

    def write(i, _):
        block = jnp.zeros((NV, T), i32)
        for k in range(CAP):
            block = jnp.where(place == k, label[i * CAP + k], block)
        out[i * SLOTS + CAP] = block.astype(f32)
        return 0

    lax.fori_loop(0, PEERS, write, 0)


def remap(dest, count, me, surf, weight):
    smem = pl.BlockSpec(memory_space=pltpu.SMEM)
    vmem = pl.BlockSpec(memory_space=pltpu.VMEM)
    hbm = pl.BlockSpec(memory_space=pltpu.HBM)
    return pl.pallas_call(
        remap_kernel,
        in_specs=[smem, smem, smem, vmem, hbm],
        out_specs=vmem,
        out_shape=jax.ShapeDtypeStruct((PEERS * SLOTS, NV, T), f32),
        scratch_shapes=[
            pltpu.VMEM((T, FAN, T, T), jnp.bfloat16),
            pltpu.SMEM((PEERS,), i32),
            pltpu.SMEM((PEERS * CAP + 8,), i32),
            pltpu.SemaphoreType.DMA((CHUNKS,)),
        ],
        compiler_params=params(),
        cost_estimate=pl.CostEstimate(flops=67 << 20, bytes_accessed=22 << 20, transcendentals=0),
        name="remap",
    )(dest, count, me, surf, weight)


def sealed(block, *after):
    anywhere = pl.BlockSpec(memory_space=pl.ANY)

    def kernel(*refs):
        del refs

    return pl.pallas_call(
        kernel,
        in_specs=[anywhere] * (1 + len(after)),
        out_specs=anywhere,
        out_shape=jax.ShapeDtypeStruct(block.shape, block.dtype),
        input_output_aliases={0: 0},
        name="sealed",
    )(block, *after)


def merged(left, right):
    return jnp.where((lanes(T) & 1) == 0, left, pltpu.roll(right, T - 2, 1))


def diffuse(u, up, down, side, rate):
    rows = u.shape[0]
    lane, sub = lanes(rows), subl(rows)
    north = jnp.where(sub == 0, up, pltpu.roll(u, 1, 0))
    south = jnp.where(sub == rows - 1, down, pltpu.roll(u, rows - 1, 0))
    west = jnp.where(lane == 0, side, pltpu.roll(u, 1, 1))
    east = jnp.where(lane == T - 1, side, pltpu.roll(u, T - 1, 1))
    return u + rate * ((north + south) + (west + east) - 4.0 * u)


def level_diffuse(u, top, bottom, side, rate, l, part):
    lo = part * HALF
    up = top[0, l : l + 1, :] if part == 0 else u[0, 0, l, lo - 1 : lo, :]
    down = bottom[0, l : l + 1, :] if lo + HALF == T else u[0, 0, l, lo + HALF : lo + HALF + 1, :]
    spin = side[lo : lo + HALF, :]
    if l:
        spin = pltpu.roll(spin, T - 2 * l, 1)
    return diffuse(u[0, 0, l, lo : lo + HALF, :], up, down, spin, rate)


def first_kernel(rate_ref, flags, u, vert, top, bottom, left, right, out, first, last, cols, side):
    v = pl.program_id(0)
    rate = rate_ref[v]
    side[...] = pltpu.roll(merged(left[0], right[0]), unshift(v), 1)
    for part in range(T // HALF):
        lo = part * HALF
        coef = vert[0, lo : lo + HALF, :]
        before = None
        here = level_diffuse(u, top, bottom, side, rate, 0, part)
        for l in range(LEV):
            after = level_diffuse(u, top, bottom, side, rate, l + 1, part) if l + 1 < LEV else None
            if before is None:
                term = after - here
            elif after is None:
                term = before - here
            else:
                term = (after - here) + (before - here)
            out[0, 0, l, lo : lo + HALF, :] = here + coef * term
            before, here = here, after
    lane = lanes(HALF)
    for lo in range(0, T, HALF):
        acc = jnp.zeros((HALF, T), f32)
        for l in range(LEV):
            turned = pltpu.roll(out[0, 0, l, lo : lo + HALF, :], 2 * l + 1, 1)
            acc = jnp.where((lane >> 1) == l, turned, acc)
        spot = pltpu.roll(acc, v * 32, 1)
        spot = spot * cut(flags, lane)
        cols[lo : lo + HALF, :] = jnp.where((lane >> 5) == v, spot, cols[lo : lo + HALF, :])
    up, down = cut(flags)
    for l in range(LEV):
        first[0, l : l + 1, :] = out[0, 0, l, 0:1, :] * up
        last[0, l : l + 1, :] = out[0, 0, l, T - 1 : T, :] * down


def second_kernel(rate_ref, flags, u, vert, top, bottom, left, right, out, side):
    v = pl.program_id(0)
    rate = rate_ref[v]
    side[...] = pltpu.roll(merged(left[...], right[...]), unshift(v), 1)
    for part in range(T // HALF):
        lo = part * HALF
        coef = vert[0, lo : lo + HALF, :]
        before = level_diffuse(u, top, bottom, side, rate, 1, part)
        here = level_diffuse(u, top, bottom, side, rate, 2, part)
        out[0, 0, 0, lo : lo + HALF, :] = before
        out[0, 0, 1, lo : lo + HALF, :] = before + coef * ((here - before) - before)
        for l in range(2, LEV):
            after = level_diffuse(u, top, bottom, side, rate, l + 1, part) if l + 1 < LEV else None
            term = before - here
            if after is not None:
                term = (after - here) + term
            out[0, 0, l, lo : lo + HALF, :] = here + coef * term
            before, here = here, after


def step_call(kernel, rate, flags, u, vert, top, bottom, left, right, emit, name):
    whole = lambda *n: pl.BlockSpec(n, lambda v: (0,) * len(n))
    rows = pl.BlockSpec((1, LEV, T), lambda v: (v, 0, 0))
    tile = pl.BlockSpec((1, 1, LEV, T, T), lambda v: (0, v, 0, 0, 0))
    side = whole(*left.shape)
    out_specs, out_shape = [tile], [jax.ShapeDtypeStruct(u.shape, f32)]
    if emit:
        out_specs += [rows, rows, whole(T, T)]
        out_shape += [jax.ShapeDtypeStruct((NV, LEV, T), f32)] * 2
        out_shape += [jax.ShapeDtypeStruct((T, T), f32)]
    return pl.pallas_call(
        kernel,
        grid=(NV,),
        in_specs=[
            pl.BlockSpec(memory_space=pltpu.SMEM),
            pl.BlockSpec(memory_space=pltpu.SMEM),
            tile,
            whole(1, T, T),
            rows,
            rows,
            side,
            side,
        ],
        out_specs=out_specs,
        out_shape=out_shape,
        scratch_shapes=[pltpu.VMEM((T, T), f32)],
        compiler_params=params(),
        cost_estimate=pl.CostEstimate(flops=24 << 20, bytes_accessed=9 << 20, transcendentals=0),
        name=name,
    )(rate, flags, u, vert, top, bottom, left, right)


def unpack_kernel(flags, data, after, imp, first, last, cols):
    del after
    size = SLOTS * NV
    sub = subl(T).astype(f32) + 1.0
    picks = []
    for j in range(NV):
        table = jnp.sum(data[pl.ds(CAP * NV + j, PEERS, stride=size), :], axis=0, keepdims=True)
        picks.append((sub == table).astype(jnp.bfloat16))
    pick = jnp.concatenate(picks, axis=1)
    lane = lanes(T)
    acc = jnp.zeros((T, T), f32)
    for v in range(NV):
        block = jnp.concatenate(
            [data[pl.ds(s * size + v, CAP, stride=NV), :] for s in range(PEERS)], axis=0
        )
        high = block.astype(jnp.bfloat16)
        low = (block - high.astype(f32)).astype(jnp.bfloat16)
        total = jnp.dot(pick, high, preferred_element_type=f32)
        total = total + jnp.dot(pick, low, preferred_element_type=f32)
        imp[v] = total
        first[v] = jnp.broadcast_to(total[0:1, :] * flags[0], (8, T))
        last[v] = jnp.broadcast_to(total[T - 1 : T, :] * flags[1], (8, T))
        acc = jnp.where((lane >> 1) == v * LEV, pltpu.roll(total, (32 * v + 1) % T, 1), acc)
    cols[...] = acc * cut(flags, lane)


def unpack(flags, data, after):
    return pl.pallas_call(
        unpack_kernel,
        in_specs=[
            pl.BlockSpec(memory_space=pltpu.SMEM),
            pl.BlockSpec(memory_space=pltpu.VMEM),
            pl.BlockSpec(memory_space=pl.ANY),
        ],
        out_shape=[
            jax.ShapeDtypeStruct((NV, T, T), f32),
            jax.ShapeDtypeStruct((NV, 8, T), f32),
            jax.ShapeDtypeStruct((NV, 8, T), f32),
            jax.ShapeDtypeStruct((T, T), f32),
        ],
        compiler_params=params(),
        cost_estimate=pl.CostEstimate(flops=200 << 20, bytes_accessed=2 << 20, transcendentals=0),
        name="unpack",
    )(flags, data, after)


def final_kernel(
    horiz, relax, prior, mid, vert, mask, top, bottom, left, right, sea_top, sea_bottom, sea_left, sea_right,
    imp, imp_top, imp_bottom, imp_left, imp_right, out,
):
    v = pl.program_id(0)
    pull = relax[v]
    spin = unshift(v)

    def relaxed(base, sea, new):
        return base + pull * sea * (new - base)

    sea = mask[0].astype(f32)
    new = imp[0]
    u = relaxed(prior[0, 0, 0], sea, new)
    up = relaxed(top[0, 0:1, :], sea_top[0, 0:1, :], imp_top[0, 0:1, :])
    down = relaxed(bottom[0, 0:1, :], sea_bottom[0, 0:1, :], imp_bottom[0, 0:1, :])
    side = relaxed(
        pltpu.roll(merged(left[...], right[...]), spin, 1),
        merged(sea_left[0], sea_right[0]),
        pltpu.roll(merged(imp_left[...], imp_right[...]), spin, 1),
    )
    h = diffuse(u, up, down, side, horiz[v])
    coef = vert[0]
    value = h + coef * (mid[0, 0, 0] - h)
    out[0, 0, 0] = relaxed(value, sea, new)
    out[0, 0, 1] = mid[0, 0, 1] + coef * h


def final(horiz, relax, prior, mid, vert, mask, rows2, cols2, rows1, cols1, imp, imp_rows, imp_cols):
    whole = lambda *n: pl.BlockSpec(n, lambda v: (0,) * len(n))
    smem = pl.BlockSpec(memory_space=pltpu.SMEM)
    row2 = pl.BlockSpec((1, LEV, T), lambda v: (v, 0, 0))
    row1 = pl.BlockSpec((1, LEV, T), lambda v: (NV, 0, 0))
    rowi = pl.BlockSpec((1, 8, T), lambda v: (v, 0, 0))
    sea_col = pl.BlockSpec((1, T, T), lambda v: (1, 0, 0))
    pairs = pl.BlockSpec((1, 1, 2, T, T), lambda v: (0, v, 0, 0, 0))
    return pl.pallas_call(
        final_kernel,
        grid=(NV,),
        in_specs=[
            smem,
            smem,
            pl.BlockSpec((1, 1, 1, T, T), lambda v: (0, v, 0, 0, 0)),
            pairs,
            whole(1, T, T),
            whole(1, T, T),
            row2,
            row2,
            whole(T, T),
            whole(T, T),
            row1,
            row1,
            sea_col,
            sea_col,
            pl.BlockSpec((1, T, T), lambda v: (v, 0, 0)),
            rowi,
            rowi,
            whole(T, T),
            whole(T, T),
        ],
        out_specs=pairs,
        out_shape=jax.ShapeDtypeStruct(mid.shape, f32),
        input_output_aliases={3: 0},
        compiler_params=params(),
        cost_estimate=pl.CostEstimate(flops=2 << 20, bytes_accessed=3 << 20, transcendentals=0),
        name="final",
    )(
        horiz, relax, prior, mid, vert, mask, *rows2, *cols2, *rows1, *cols1, imp, *imp_rows, *imp_cols
    )


def shifted(block, axis, by, across):
    count = lax.axis_size(axis)
    if not across:
        return lax.ppermute(
            block, axis, [(i, (i + by) % count) for i in range(count)]
        )
    return lax.ppermute(
        block,
        ("comp", axis),
        [
            (c * count + i, (1 - c) * count + (i + by) % count)
            for c in range(2)
            for i in range(count)
        ],
    )


def neighbours(first, last, cols, across=False):
    rows = shifted(last, "gx", 1, across), shifted(first, "gx", -1, across)
    sides = shifted(cols, "gy", 1, across), shifted(cols, "gy", -1, across)
    return rows, sides


def local(
    state, horiz_coef, vert_coef, couple_rate, sea_mask, dest_block, entry_count, remap_weight
):
    horiz, relax = horiz_coef[0], couple_rate[0]
    gx, gy = lax.axis_index("gx"), lax.axis_index("gy")
    ends = lax.axis_size("gx") - 1, lax.axis_size("gy") - 1
    me = (gx * (ends[1] + 1) + gy).astype(i32)
    flags = jnp.stack([gx > 0, gx < ends[0], gy < ends[1], gy > 0]).astype(f32)
    first, last, cols, surf = edges(flags, sea_mask, state)
    rows1, cols1 = neighbours(first, last, cols)
    packed = remap(
        dest_block.reshape(T * FAN), entry_count.reshape(T), me.reshape(1), surf, remap_weight
    )
    packed = sealed(packed, *rows1, *cols1).reshape(PEERS, SLOTS, NV, T)
    packed = lax.all_to_all(packed, ("gx", "gy"), split_axis=0, concat_axis=0, tiled=True)
    prior, first, last, cols = step_call(
        first_kernel, horiz, flags, state, vert_coef, *rows1, *cols1, True, "first_step"
    )
    rows2, cols2 = neighbours(first, last, cols)
    imp, first, last, cols = unpack(flags, packed.reshape(PEERS * SLOTS * NV, T), cols)
    imp = lax.ppermute(imp, "comp", [(0, 1), (1, 0)])
    imp_rows, imp_cols = neighbours(first, last, cols, across=True)
    (mid,) = step_call(
        second_kernel, horiz, flags, prior, vert_coef, *rows2, *cols2, False, "second_step"
    )
    return final(
        horiz, relax, prior, mid, vert_coef, sea_mask, rows2, cols2, rows1, cols1, imp, imp_rows, imp_cols
    )


def solution(mesh):
    in_specs = (
        P("comp", None, None, "gx", "gy"),
        P("comp", None),
        P("comp", "gx", "gy"),
        P("comp", None),
        P("comp", "gx", "gy"),
        P("comp", "gx", "gy", None),
        P("comp", "gx", "gy"),
        P("comp", "gx", "gy", None, None, None),
    )
    out_specs = P("comp", None, None, "gx", "gy")
    return jax.shard_map(local, mesh=mesh, in_specs=in_specs, out_specs=out_specs, check_vma=False)
```

```python
import jax
import jax.numpy as jnp
from jax import lax
from jax.experimental import pallas as pl
from jax.experimental.pallas import tpu as pltpu
from jax.sharding import PartitionSpec as P

NV = 4
LEV = 16
PLANES = NV * LEV
T = 128
FAN = 4
CAP = 8
PEERS = 64
SLOTS = CAP + 1
HALF = 64
CHUNKS = 16
MIB = 1024 * 1024
LIMIT = 58 * MIB
ROW_VERT = 2 * PLANES
ROW_SEA = ROW_VERT + 8
ROW_SIZE = ROW_SEA + 8
COL_NEXT = T
COL_COEF = 2 * T
COL_TOP = 3 * T
COL_BOTTOM = COL_TOP + 8
COL_SIZE = COL_BOTTOM + 8
KEEP_BASE = 0
KEEP_ONE = NV * T
KEEP_PART = 2 * NV * T
KEEP_VERT = 3 * NV * T
KEEP_SEA = KEEP_VERT + T
KEEP_SIDE = KEEP_SEA + T
KEEP_SEA_SIDE = KEEP_SIDE + T
KEEP_ENDS = KEEP_SEA_SIDE + T
KEEP_SIZE = KEEP_ENDS + 16

f32 = jnp.float32
i32 = jnp.int32
bf16 = jnp.bfloat16

SMEM = pl.BlockSpec(memory_space=pltpu.SMEM)
VMEM = pl.BlockSpec(memory_space=pltpu.VMEM)
HBM = pl.BlockSpec(memory_space=pl.ANY)


def params(limit=LIMIT):
    return pltpu.CompilerParams(vmem_limit_bytes=limit)


def cost(flops, size):
    return pl.CostEstimate(flops=flops, bytes_accessed=size, transcendentals=0)


def lanes(rows):
    return lax.broadcasted_iota(i32, (rows, T), 1)


def subl(rows):
    return lax.broadcasted_iota(i32, (rows, T), 0)


def inside():
    gx, gy = lax.axis_index("gx"), lax.axis_index("gy")
    one = lambda test: jnp.where(test, 1.0, 0.0).astype(f32)
    return (
        one(gx > 0),
        one(gx < lax.axis_size("gx") - 1),
        one(gy > 0),
        one(gy < lax.axis_size("gy") - 1),
    )


def column_keep(rows):
    _, _, before, after = inside()
    return jnp.where((lanes(rows) & 1) == 0, after, before)


def run(copies):
    for copy in copies:
        copy.start()
    for copy in copies:
        copy.wait()


def row_kernel(state, vert, mask, head, tail, high, low, coef, sea, sems):
    ends = pl.ds(0, 8), pl.ds(T - 8, 8)
    copies = []
    for k, buffer in enumerate((high, low)):
        copies.append(pltpu.make_async_copy(state.at[0, :, :, ends[k]], buffer, sems.at[3 * k]))
        copies.append(pltpu.make_async_copy(vert.at[0, ends[k]], coef.at[k], sems.at[3 * k + 1]))
        copies.append(pltpu.make_async_copy(mask.at[0, ends[k]], sea.at[k], sems.at[3 * k + 2]))
    run(copies)
    up, down, _, _ = inside()
    for k, (out, buffer, keep) in enumerate(((head, high, up), (tail, low, down))):
        outer, following = (0, 1) if k == 0 else (7, 6)
        for p in range(PLANES):
            v, l = divmod(p, LEV)
            out[p : p + 1, :] = buffer[v, l, outer : outer + 1, :] * keep
            out[PLANES + p : PLANES + p + 1, :] = buffer[v, l, following : following + 1, :] * keep
        line = coef[k, outer : outer + 1, :] * keep
        out[ROW_VERT : ROW_VERT + 8, :] = jnp.broadcast_to(line, (8, T))
        line = sea[k, outer : outer + 1, :].astype(f32) * keep
        out[ROW_SEA : ROW_SEA + 8, :] = jnp.broadcast_to(line, (8, T))


def outer_rows(state, vert, mask):
    return pl.pallas_call(
        row_kernel,
        in_specs=[HBM, HBM, HBM],
        out_specs=[VMEM, VMEM],
        out_shape=[jax.ShapeDtypeStruct((ROW_SIZE, T), f32)] * 2,
        scratch_shapes=[
            pltpu.VMEM((NV, LEV, 8, T), f32),
            pltpu.VMEM((NV, LEV, 8, T), f32),
            pltpu.VMEM((2, 8, T), f32),
            pltpu.VMEM((2, 8, T), i32),
            pltpu.SemaphoreType.DMA((6,)),
        ],
        compiler_params=params(),
        cost_estimate=cost(1 << 16, 1 << 19),
        name="outer_rows",
    )(state, vert, mask)


def column_kernel(state, vert, mask, cols, surf, tile, coef, wet, sea, sems):
    loads = [pltpu.make_async_copy(state.at[0, v], tile.at[v], sems.at[v]) for v in range(NV)]
    loads.append(pltpu.make_async_copy(vert.at[0], coef, sems.at[NV]))
    loads.append(pltpu.make_async_copy(mask.at[0], sea, sems.at[NV + 1]))
    for load in loads:
        load.start()
    lane = lanes(HALF)
    keep = column_keep(HALF)
    for v in range(NV):
        loads[v].wait()
        surf[pl.ds(v, T, stride=NV), :] = tile[v, 0]
        for lo in range(0, T, HALF):
            outer, following = pl.ds(lo, HALF), pl.ds(COL_NEXT + lo, HALF)
            acc = jnp.zeros((HALF, T), f32) if v == 0 else cols[outer, :]
            acc2 = jnp.zeros((HALF, T), f32) if v == 0 else cols[following, :]
            for l in range(LEV):
                p = v * LEV + l
                plane = tile[v, l, lo : lo + HALF, :]
                acc = jnp.where((lane >> 1) == p, pltpu.roll(plane, (2 * p + 1) % T, 1), acc)
                hit = (lane == 2 * p) | (lane == (2 * p + 3) % T)
                acc2 = jnp.where(hit, pltpu.roll(plane, (2 * p + 2) % T, 1), acc2)
            last = v == NV - 1
            cols[outer, :] = acc * keep if last else acc
            cols[following, :] = acc2 * keep if last else acc2
    loads[NV].wait()
    loads[NV + 1].wait()
    lane = lanes(T)
    wet[...] = sea[...].astype(f32)
    pair = jnp.where(lane < 2, pltpu.roll(coef[...], 1, 1), pltpu.roll(wet[...], 3, 1))
    cols[COL_COEF : COL_COEF + T, :] = pair * column_keep(T)


def outer_columns(state, vert, mask):
    square = jax.ShapeDtypeStruct((T, T), f32)
    return pl.pallas_call(
        column_kernel,
        in_specs=[HBM, HBM, HBM],
        out_specs=[VMEM] * 5,
        out_shape=[
            jax.ShapeDtypeStruct((COL_TOP, T), f32),
            jax.ShapeDtypeStruct((T * NV, T), f32),
            jax.ShapeDtypeStruct((NV, LEV, T, T), f32),
            square,
            square,
        ],
        scratch_shapes=[pltpu.VMEM((T, T), i32), pltpu.SemaphoreType.DMA((NV + 2,))],
        compiler_params=params(47 * MIB),
        cost_estimate=cost(6 << 20, 9 << 20),
        name="outer_columns",
    )(state, vert, mask)


def corner_kernel(cols, top, bottom, out):
    out[0:COL_COEF, :] = cols[0:COL_COEF, :]
    lane, sub = lanes(PLANES), subl(PLANES)
    keep = column_keep(PLANES)
    for k, rows in enumerate((top, bottom)):
        line = rows[0:PLANES, :]
        at = COL_COEF + k * PLANES
        out[at : at + PLANES, :] = jnp.where(
            (lane == 4) | (lane == 5), pltpu.roll(line, 5, 1) * keep, cols[at : at + PLANES, :]
        )
        first = jnp.broadcast_to(line[:, 0:1], (PLANES, T))
        last = jnp.broadcast_to(line[:, T - 1 : T], (PLANES, T))
        spread = jnp.where(lane == 2 * sub, last, jnp.where(lane == 2 * sub + 1, first, 0.0))
        total = jnp.sum(spread * keep, axis=0, keepdims=True)
        at = COL_TOP + 8 * k
        out[at : at + 8, :] = jnp.broadcast_to(total, (8, T))


def with_corners(cols, top, bottom):
    return pl.pallas_call(
        corner_kernel,
        in_specs=[VMEM] * 3,
        out_specs=VMEM,
        out_shape=jax.ShapeDtypeStruct((COL_SIZE, T), f32),
        compiler_params=params(4 * MIB),
        cost_estimate=cost(1 << 16, 1 << 18),
        name="with_corners",
    )(cols, top, bottom)


def remap_kernel(dest_in, count_in, surf, weight, after, out, blocks, dest, count, used, label, sems):
    del after
    rows = T // CHUNKS
    lists = [
        pltpu.make_async_copy(dest_in, dest, sems.at[CHUNKS]),
        pltpu.make_async_copy(count_in, count, sems.at[CHUNKS + 1]),
    ]
    for copy in lists:
        copy.start()

    def fetch(c):
        piece = pl.ds(c * rows, rows)
        return pltpu.make_async_copy(weight.at[0, piece, 0], blocks.at[piece], sems.at[c])

    for c in range(CHUNKS):
        fetch(c).start()
    out[...] = jnp.zeros_like(out)

    def clear(i, _):
        used[i] = 0
        for k in range(CAP):
            label[i * CAP + k] = 0
        return 0

    lax.fori_loop(0, PEERS, clear, 0)
    for copy in lists:
        copy.wait()
    sub = subl(8)

    def slot_of(row, f):
        target = dest[f, row]
        peer = lax.shift_right_logical(target, 7) & (PEERS - 1)
        live = f < count[0, row]
        at = used[peer]
        used[peer] = at + jnp.where(live, 1, 0)
        label[jnp.where(live, peer * CAP + at, PEERS * CAP)] = (target & (T - 1)) + 1
        return jnp.where(live, peer * SLOTS + at, CAP)

    def chunk(c, _):
        fetch(c).wait()
        for r in range(0, rows, 2):
            row = c * rows + r
            slots = [[slot_of(row + q, f) for f in range(FAN)] for q in range(2)]
            pair = surf[pl.ds(pl.multiple_of(row * NV, 8), 8), :]
            pair = jnp.concatenate(
                [jnp.where(sub < NV, pair, 0.0), jnp.where(sub >= NV, pair, 0.0)], axis=1
            ).astype(bf16)
            for f in range(0, FAN, 2):
                block = jnp.concatenate(
                    [
                        jnp.concatenate([blocks[row + q, f], blocks[row + q, f + 1]], axis=1)
                        for q in range(2)
                    ],
                    axis=0,
                )
                product = jnp.dot(pair, block, preferred_element_type=f32)
                for q in range(2):
                    for g in range(2):
                        part = product[q * NV : (q + 1) * NV, g * T : (g + 1) * T]
                        out[slots[q][f + g]] = part
        return 0

    lax.fori_loop(0, CHUNKS, chunk, 0)
    me = lax.axis_index("gx") * lax.axis_size("gy") + lax.axis_index("gy")
    place = lax.broadcasted_iota(i32, (NV, T), 0) * T + lax.broadcasted_iota(i32, (NV, T), 1)
    place = place - me * CAP

    def write(i, _):
        block = jnp.zeros((NV, T), i32)
        for k in range(CAP):
            block = jnp.where(place == k, label[i * CAP + k], block)
        out[i * SLOTS + CAP] = block.astype(f32)
        return 0

    lax.fori_loop(0, PEERS, write, 0)


def remap(dest, count, surf, weight, after):
    return pl.pallas_call(
        remap_kernel,
        in_specs=[HBM, HBM, VMEM, HBM, HBM],
        out_specs=VMEM,
        out_shape=jax.ShapeDtypeStruct((PEERS * SLOTS, NV, T), f32),
        scratch_shapes=[
            pltpu.VMEM((T, FAN, T, T), bf16),
            pltpu.SMEM((FAN, T), i32),
            pltpu.SMEM((1, T), i32),
            pltpu.SMEM((PEERS,), i32),
            pltpu.SMEM((PEERS * CAP + 8,), i32),
            pltpu.SemaphoreType.DMA((CHUNKS + 2,)),
        ],
        compiler_params=params(44 * MIB),
        cost_estimate=cost(67 << 20, 20 << 20),
        name="remap",
    )(dest, count, surf, weight, after)


def sealed(block, *after):
    def kernel(*refs):
        del refs

    return pl.pallas_call(
        kernel,
        in_specs=[HBM] * (1 + len(after)),
        out_specs=HBM,
        out_shape=jax.ShapeDtypeStruct(block.shape, block.dtype),
        input_output_aliases={0: 0},
        name="sealed",
    )(block, *after)


def merged(left, right, back=2):
    return jnp.where((lanes(left.shape[0]) & 1) == 0, left, pltpu.roll(right, T - back, 1))


def diffuse(u, up, down, side, rate):
    rows = u.shape[0]
    lane, sub = lanes(rows), subl(rows)
    north = jnp.where(sub == 0, up, pltpu.roll(u, 1, 0))
    south = jnp.where(sub == rows - 1, down, pltpu.roll(u, rows - 1, 0))
    west = jnp.where(lane == 0, side, pltpu.roll(u, 1, 1))
    east = jnp.where(lane == T - 1, side, pltpu.roll(u, T - 1, 1))
    return u + rate * ((north + south) + (west + east) - 4.0 * u)


def level_diffuse(u, top, bottom, side, rate, l, lo):
    up = top[l : l + 1, :] if lo == 0 else u[l, lo - 1 : lo, :]
    down = bottom[l : l + 1, :] if lo + HALF == T else u[l, lo + HALF : lo + HALF + 1, :]
    spin = side[lo : lo + HALF, :]
    if l:
        spin = pltpu.roll(spin, T - 2 * l, 1)
    return diffuse(u[l, lo : lo + HALF, :], up, down, spin, rate)


def halo_columns(rate, left, right, own):
    lane, sub = lanes(T), subl(T)
    here = merged(left[0:T, :], right[0:T, :])
    outer = merged(left[COL_NEXT : COL_NEXT + T, :], right[COL_NEXT : COL_NEXT + T, :], 4)
    inner = pltpu.roll(own[0:T, :], T - 1, 1)
    ends = [merged(left[at : at + 8, :], right[at : at + 8, :])[0:1, :] for at in (COL_TOP, COL_BOTTOM)]
    north = jnp.where(sub == 0, ends[0], pltpu.roll(here, 1, 0))
    south = jnp.where(sub == T - 1, ends[1], pltpu.roll(here, T - 1, 0))
    plane = ((lane + 1) >> 1) & (PLANES - 1)
    number = jnp.full((T, T), rate[0, 0], f32)
    for v in range(1, NV):
        number = jnp.where(plane // LEV == v, rate[0, v], number)
    h = here + number * ((north + south) + (outer + inner) - 4.0 * here)
    coef = jnp.where(
        (lane & 1) == 0,
        jnp.broadcast_to(left[COL_COEF : COL_COEF + T, 0:1], (T, T)),
        jnp.broadcast_to(right[COL_COEF : COL_COEF + T, 1:2], (T, T)),
    )
    level = plane % LEV
    above = jnp.where(level < LEV - 1, pltpu.roll(h, T - 2, 1) - h, 0.0)
    below = jnp.where(level > 0, pltpu.roll(h, 2, 1) - h, 0.0)
    return here, h + coef * (above + below)


def halo_rows(rate, rows, own, left, right, k, v):
    at = v * LEV
    lane, level = lanes(LEV), subl(LEV)
    here = rows[at : at + LEV, :]
    corner = COL_COEF + k * PLANES + at
    west = jnp.where(
        lane == 0, pltpu.roll(left[corner : corner + LEV, :], T - 4, 1), pltpu.roll(here, 1, 1)
    )
    east = jnp.where(
        lane == T - 1,
        pltpu.roll(right[corner : corner + LEV, :], T - 6, 1),
        pltpu.roll(here, T - 1, 1),
    )
    outer = rows[PLANES + at : PLANES + at + LEV, :]
    inner = own[at : at + LEV, :]
    h = here + rate[0, v] * ((outer + inner) + (west + east) - 4.0 * here)
    above = jnp.where(level < LEV - 1, pltpu.roll(h, LEV - 1, 0) - h, 0.0)
    below = jnp.where(level > 0, pltpu.roll(h, 1, 0) - h, 0.0)
    return h + rows[ROW_VERT : ROW_VERT + 1, :] * (above + below)


def step_kernel(
    rate, u, coef, sea, own, top, bottom, near, far,
    out, keep, w, stage, inner, top1, bottom1, top2, bottom2, side1, side2, turned, sems,
):
    def emit(v):
        levels = pl.ds(2, LEV - 2)
        return pltpu.make_async_copy(stage.at[v], out.at[0, v, levels], sems.at[v])

    up, down, _, _ = inside()
    side1[...], side2[...] = halo_columns(rate, near, far, own)
    for v in range(NV):
        at = v * LEV
        for l in range(LEV):
            inner[0, at + l : at + l + 1, :] = u[v, l, 0:1, :] * up
            inner[1, at + l : at + l + 1, :] = u[v, l, T - 1 : T, :] * down
    for v in range(NV):
        at = v * LEV
        top1[v] = top[at : at + LEV, :]
        bottom1[v] = bottom[at : at + LEV, :]
        top2[v] = halo_rows(rate, top, inner.at[0], near, far, 0, v)
        bottom2[v] = halo_rows(rate, bottom, inner.at[1], near, far, 1, v)

    def first(v, _):
        number = rate[0, v]
        turned[...] = pltpu.roll(side1[...], lax.rem((NV - v) * 32, T), 1)
        source, result = u.at[v], w.at[v]
        for lo in range(0, T, HALF):
            mix = coef[lo : lo + HALF, :]
            at = lambda l: level_diffuse(source, top1.at[v], bottom1.at[v], turned, number, l, lo)
            before, here = None, at(0)
            for l in range(LEV):
                after = at(l + 1) if l + 1 < LEV else None
                if before is None:
                    term = after - here
                elif after is None:
                    term = before - here
                else:
                    term = (after - here) + (before - here)
                result[l, lo : lo + HALF, :] = here + mix * term
                before, here = here, after
        return 0

    lax.fori_loop(0, NV, first, 0)

    def second(v, _):
        number = rate[0, v]
        turned[...] = pltpu.roll(side2[...], lax.rem((NV - v) * 32, T), 1)
        source, result = w.at[v], stage.at[v]
        for lo in range(0, T, HALF):
            mix = coef[lo : lo + HALF, :]
            at = lambda l: level_diffuse(source, top2.at[v], bottom2.at[v], turned, number, l, lo)
            before, here = at(1), at(2)
            row = pl.multiple_of(v * T + lo, 8)
            keep[pl.ds(KEEP_BASE + row, HALF), :] = source[0, lo : lo + HALF, :]
            keep[pl.ds(KEEP_ONE + row, HALF), :] = before
            keep[pl.ds(KEEP_PART + row, HALF), :] = before + mix * ((here - before) - before)
            for l in range(2, LEV):
                after = at(l + 1) if l + 1 < LEV else None
                term = before - here
                if after is not None:
                    term = (after - here) + term
                result[l - 2, lo : lo + HALF, :] = here + mix * term
                before, here = here, after
        emit(v).start()
        return 0

    lax.fori_loop(0, NV, second, 0)
    keep[KEEP_VERT : KEEP_VERT + T, :] = coef[...]
    keep[KEEP_SEA : KEEP_SEA + T, :] = sea[...]
    keep[KEEP_SIDE : KEEP_SIDE + T, :] = side2[...]
    coefs = pl.ds(COL_COEF, T)
    keep[KEEP_SEA_SIDE : KEEP_SEA_SIDE + T, :] = jnp.where(
        lanes(T) == 0, pltpu.roll(near[coefs, :], T - 2, 1), pltpu.roll(far[coefs, :], T - 4, 1)
    )
    for k, (rows, line) in enumerate(((top2, top), (bottom2, bottom))):
        for v in range(NV):
            keep[KEEP_ENDS + 8 * k + v : KEEP_ENDS + 8 * k + v + 1, :] = rows[v, 0:1, :]
        keep[KEEP_ENDS + 8 * k + NV : KEEP_ENDS + 8 * k + 8, :] = line[ROW_SEA : ROW_SEA + NV, :]
    for v in range(NV):
        emit(v).wait()


def two_steps(rate, u, coef, sea, own, top, bottom, left, right):
    rows = pltpu.VMEM((NV, LEV, T), f32)
    square = pltpu.VMEM((T, T), f32)
    return pl.pallas_call(
        step_kernel,
        in_specs=[SMEM] + [VMEM] * 8,
        out_specs=[HBM, VMEM],
        out_shape=[
            jax.ShapeDtypeStruct((1,) + u.shape, f32),
            jax.ShapeDtypeStruct((KEEP_SIZE, T), f32),
        ],
        scratch_shapes=[
            pltpu.VMEM((NV, LEV, T, T), f32),
            pltpu.VMEM((NV, LEV - 2, T, T), f32),
            pltpu.VMEM((2, PLANES, T), f32),
            rows,
            rows,
            rows,
            rows,
            square,
            square,
            square,
            pltpu.SemaphoreType.DMA((NV,)),
        ],
        compiler_params=params(16 * MIB),
        cost_estimate=cost(48 << 20, 10 << 20),
        name="two_steps",
    )(rate, u, coef, sea, own, top, bottom, left, right)


def unpack_kernel(data, after, imp, first, last, cols):
    del after
    size = SLOTS * NV
    sub = subl(T).astype(f32) + 1.0
    picks = []
    for j in range(NV):
        table = jnp.sum(data[pl.ds(CAP * NV + j, PEERS, stride=size), :], axis=0, keepdims=True)
        picks.append((sub == table).astype(bf16))
    pick = jnp.concatenate(picks, axis=1)
    lane = lanes(T)
    up, down, _, _ = inside()
    acc = jnp.zeros((T, T), f32)
    for v in range(NV):
        block = jnp.concatenate(
            [data[pl.ds(s * size + v, CAP, stride=NV), :] for s in range(PEERS)], axis=0
        )
        high = block.astype(bf16)
        low = (block - high.astype(f32)).astype(bf16)
        total = jnp.dot(pick, high, preferred_element_type=f32)
        total = total + jnp.dot(pick, low, preferred_element_type=f32)
        imp[v] = total
        for out, row, keep in ((first, 0, up), (last, T - 1, down)):
            out[v : v + 1, :] = total[row : row + 1, :] * keep
            out[NV + v : NV + v + 1, :] = total[row : row + 1, :] * keep
        acc = jnp.where((lane >> 1) == v, pltpu.roll(total, 2 * v + 1, 1), acc)
    cols[...] = jnp.transpose(acc * column_keep(T))[0 : 2 * NV, :]


def unpack(data, after):
    return pl.pallas_call(
        unpack_kernel,
        in_specs=[VMEM, HBM],
        out_specs=[VMEM] * 4,
        out_shape=[
            jax.ShapeDtypeStruct((NV, T, T), f32),
            jax.ShapeDtypeStruct((2 * NV, T), f32),
            jax.ShapeDtypeStruct((2 * NV, T), f32),
            jax.ShapeDtypeStruct((2 * NV, T), f32),
        ],
        compiler_params=params(12 * MIB),
        cost_estimate=cost(200 << 20, 2 << 20),
        name="unpack",
    )(data, after)


def final_kernel(
    horiz, relax, mid, near, imp, imp_top, imp_bottom, imp_left, imp_right, out, stage, sems
):
    del mid
    odd = (subl(2 * NV) & 1) == 1
    ends = jnp.where(odd, imp_right[...], imp_left[...])
    ends = jnp.concatenate([ends, jnp.zeros((T - 2 * NV, T), f32)], axis=0)
    side_new = jnp.transpose(ends)
    sea, sea_side = near[KEEP_SEA : KEEP_SEA + T, :], near[KEEP_SEA_SIDE : KEEP_SEA_SIDE + T, :]
    coef = near[KEEP_VERT : KEEP_VERT + T, :]
    side_base = near[KEEP_SIDE : KEEP_SIDE + T, :]
    lane = lanes(T)
    copies = []
    for v in range(NV):
        pull = relax[0, v]

        def relaxed(base, wet, new, pull=pull):
            return base + pull * wet * (new - base)

        ends = []
        for k, new in enumerate((imp_top, imp_bottom)):
            at = KEEP_ENDS + 8 * k
            ends.append(
                relaxed(near[at + v : at + v + 1, :], near[at + NV : at + NV + 1, :], new[v : v + 1, :])
            )
        turn = (T - 32 * v) % T
        base = pltpu.roll(side_base, turn, 1) if turn else side_base
        new = pltpu.roll(side_new, T - 2 * v, 1) if v else side_new
        new = jnp.where(lane == 0, new, pltpu.roll(side_new, T - 2 - 2 * v, 1))
        u = relaxed(near[KEEP_BASE + v * T : KEEP_BASE + (v + 1) * T, :], sea, imp[v])
        h = diffuse(u, ends[0], ends[1], relaxed(base, sea_side, new), horiz[0, v])
        one = near[KEEP_ONE + v * T : KEEP_ONE + (v + 1) * T, :]
        stage[v, 0] = relaxed(h + coef * (one - h), sea, imp[v])
        stage[v, 1] = near[KEEP_PART + v * T : KEEP_PART + (v + 1) * T, :] + coef * h
        copies.append(
            pltpu.make_async_copy(stage.at[v], out.at[0, v, pl.ds(0, 2)], sems.at[v])
        )
        copies[-1].start()
    for copy in copies:
        copy.wait()


def final(horiz, relax, mid, keep, imp, imp_rows, imp_cols):
    return pl.pallas_call(
        final_kernel,
        in_specs=[SMEM, SMEM, HBM] + [VMEM] * 6,
        out_specs=HBM,
        out_shape=jax.ShapeDtypeStruct(mid.shape, f32),
        input_output_aliases={2: 0},
        scratch_shapes=[
            pltpu.VMEM((NV, 2, T, T), f32),
            pltpu.SemaphoreType.DMA((NV,)),
        ],
        compiler_params=params(6 * MIB),
        cost_estimate=cost(2 << 20, 3 << 20),
        name="final",
    )(horiz, relax, mid, keep, imp, *imp_rows, *imp_cols)


def shifted(block, axis, by, across=False):
    count = lax.axis_size(axis)
    if not across:
        return lax.ppermute(block, axis, [(i, (i + by) % count) for i in range(count)])
    return lax.ppermute(
        block,
        ("comp", axis),
        [
            (c * count + i, (1 - c) * count + (i + by) % count)
            for c in range(2)
            for i in range(count)
        ],
    )


def local(
    state, horiz_coef, vert_coef, couple_rate, sea_mask, dest_block, entry_count, remap_weight
):
    head, tail = outer_rows(state, vert_coef, sea_mask)
    top, bottom = shifted(tail, "gx", 1), shifted(head, "gx", -1)
    cols, surf, tile, coef, sea = outer_columns(state, vert_coef, sea_mask)
    cols = with_corners(cols, top, bottom)
    left, right = shifted(cols, "gy", 1), shifted(cols, "gy", -1)
    dest = dest_block.reshape(T, FAN).T
    packed = remap(dest, entry_count.reshape(1, T), surf, remap_weight, cols)
    packed = sealed(packed, left, right).reshape(PEERS, SLOTS, NV, T)
    packed = lax.all_to_all(packed, ("gx", "gy"), split_axis=0, concat_axis=0, tiled=True)
    mid, keep = two_steps(horiz_coef, tile, coef, sea, cols, top, bottom, left, right)
    imp, first, last, cols = unpack(packed.reshape(PEERS * SLOTS * NV, T), keep)
    imp = lax.ppermute(imp, "comp", [(0, 1), (1, 0)])
    imp_rows = shifted(last, "gx", 1, True), shifted(first, "gx", -1, True)
    imp_cols = shifted(cols, "gy", 1, True), shifted(cols, "gy", -1, True)
    return final(horiz_coef, couple_rate, mid, keep, imp, imp_rows, imp_cols)


def solution(mesh):
    in_specs = (
        P("comp", None, None, "gx", "gy"),
        P("comp", None),
        P("comp", "gx", "gy"),
        P("comp", None),
        P("comp", "gx", "gy"),
        P("comp", "gx", "gy", None),
        P("comp", "gx", "gy"),
        P("comp", "gx", "gy", None, None, None),
    )
    out_specs = P("comp", None, None, "gx", "gy")
    return jax.shard_map(local, mesh=mesh, in_specs=in_specs, out_specs=out_specs, check_vma=False)
```

```python
import jax
import jax.numpy as jnp
from jax import lax
from jax.experimental import pallas as pl
from jax.experimental.pallas import tpu as pltpu
from jax.sharding import PartitionSpec as P

NV = 4
LEV = 16
PLANES = NV * LEV
T = 128
FAN = 4
CAP = 8
PEERS = 64
SLOTS = CAP + 1
HALF = 64
CHUNKS = 16
MIB = 1024 * 1024
ROW_VERT = 2 * PLANES
ROW_SEA = ROW_VERT + 8
ROW_SIZE = ROW_SEA + 8
COL_NEXT = T
COL_COEF = 2 * T
COL_TOP = 3 * T
COL_BOTTOM = COL_TOP + 8
COL_SIZE = COL_BOTTOM + 8
KEEP_BASE = 0
KEEP_ONE = NV * T
KEEP_PART = 2 * NV * T
KEEP_VERT = 3 * NV * T
KEEP_SEA = KEEP_VERT + T
KEEP_SIDE = KEEP_SEA + T
KEEP_SEA_SIDE = KEEP_SIDE + T
KEEP_ENDS = KEEP_SEA_SIDE + T
KEEP_SIZE = KEEP_ENDS + 16

f32 = jnp.float32
i32 = jnp.int32
bf16 = jnp.bfloat16

SMEM = pl.BlockSpec(memory_space=pltpu.SMEM)
VMEM = pl.BlockSpec(memory_space=pltpu.VMEM)
HBM = pl.BlockSpec(memory_space=pl.ANY)


def params(limit):
    return pltpu.CompilerParams(vmem_limit_bytes=limit)


def cost(flops, size):
    return pl.CostEstimate(flops=flops, bytes_accessed=size, transcendentals=0)


def lanes(rows):
    return lax.broadcasted_iota(i32, (rows, T), 1)


def subl(rows):
    return lax.broadcasted_iota(i32, (rows, T), 0)


def inside():
    gx, gy = lax.axis_index("gx"), lax.axis_index("gy")
    one = lambda test: jnp.where(test, 1.0, 0.0).astype(f32)
    return (
        one(gx > 0),
        one(gx < lax.axis_size("gx") - 1),
        one(gy > 0),
        one(gy < lax.axis_size("gy") - 1),
    )


def column_keep(rows):
    _, _, before, after = inside()
    return jnp.where((lanes(rows) & 1) == 0, after, before)


def run(copies):
    for copy in copies:
        copy.start()
    for copy in copies:
        copy.wait()


def row_kernel(state, vert, mask, after, head, tail, high, low, coef, sea, sems):
    del after
    ends = pl.ds(0, 8), pl.ds(T - 8, 8)
    copies = []
    for k, buffer in enumerate((high, low)):
        copies.append(pltpu.make_async_copy(state.at[0, :, :, ends[k]], buffer, sems.at[3 * k]))
        copies.append(pltpu.make_async_copy(vert.at[0, ends[k]], coef.at[k], sems.at[3 * k + 1]))
        copies.append(pltpu.make_async_copy(mask.at[0, ends[k]], sea.at[k], sems.at[3 * k + 2]))
    run(copies)
    up, down, _, _ = inside()
    for k, (out, buffer, keep) in enumerate(((head, high, up), (tail, low, down))):
        outer, following = (0, 1) if k == 0 else (7, 6)
        for p in range(PLANES):
            v, l = divmod(p, LEV)
            out[p : p + 1, :] = buffer[v, l, outer : outer + 1, :] * keep
            out[PLANES + p : PLANES + p + 1, :] = buffer[v, l, following : following + 1, :] * keep
        line = coef[k, outer : outer + 1, :] * keep
        out[ROW_VERT : ROW_VERT + 8, :] = jnp.broadcast_to(line, (8, T))
        line = sea[k, outer : outer + 1, :].astype(f32) * keep
        out[ROW_SEA : ROW_SEA + 8, :] = jnp.broadcast_to(line, (8, T))


def outer_rows(state, vert, mask, after):
    return pl.pallas_call(
        row_kernel,
        in_specs=[HBM] * 4,
        out_specs=[VMEM, VMEM],
        out_shape=[jax.ShapeDtypeStruct((ROW_SIZE, T), f32)] * 2,
        scratch_shapes=[
            pltpu.VMEM((NV, LEV, 8, T), f32),
            pltpu.VMEM((NV, LEV, 8, T), f32),
            pltpu.VMEM((2, 8, T), f32),
            pltpu.VMEM((2, 8, T), i32),
            pltpu.SemaphoreType.DMA((6,)),
        ],
        compiler_params=params(51 * MIB),
        cost_estimate=cost(1 << 16, 1 << 19),
        name="outer_rows",
    )(state, vert, mask, after)


def column_kernel(state, vert, mask, after, cols, tile, coef, wet, sea, sems):
    del after
    loads = [pltpu.make_async_copy(state.at[0, v], tile.at[v], sems.at[v]) for v in range(NV)]
    loads.append(pltpu.make_async_copy(vert.at[0], coef, sems.at[NV]))
    loads.append(pltpu.make_async_copy(mask.at[0], sea, sems.at[NV + 1]))
    for load in loads:
        load.start()
    lane = lanes(HALF)
    keep = column_keep(HALF)
    for v in range(NV):
        loads[v].wait()
        for lo in range(0, T, HALF):
            outer, following = pl.ds(lo, HALF), pl.ds(COL_NEXT + lo, HALF)
            acc = jnp.zeros((HALF, T), f32) if v == 0 else cols[outer, :]
            acc2 = jnp.zeros((HALF, T), f32) if v == 0 else cols[following, :]
            for l in range(LEV):
                p = v * LEV + l
                plane = tile[v, l, lo : lo + HALF, :]
                acc = jnp.where((lane >> 1) == p, pltpu.roll(plane, (2 * p + 1) % T, 1), acc)
                hit = (lane == 2 * p) | (lane == (2 * p + 3) % T)
                acc2 = jnp.where(hit, pltpu.roll(plane, (2 * p + 2) % T, 1), acc2)
            last = v == NV - 1
            cols[outer, :] = acc * keep if last else acc
            cols[following, :] = acc2 * keep if last else acc2
    loads[NV].wait()
    loads[NV + 1].wait()
    lane = lanes(T)
    wet[...] = sea[...].astype(f32)
    pair = jnp.where(lane < 2, pltpu.roll(coef[...], 1, 1), pltpu.roll(wet[...], 3, 1))
    cols[COL_COEF : COL_COEF + T, :] = pair * column_keep(T)


def outer_columns(state, vert, mask, after):
    square = jax.ShapeDtypeStruct((T, T), f32)
    return pl.pallas_call(
        column_kernel,
        in_specs=[HBM] * 4,
        out_specs=[VMEM] * 4,
        out_shape=[
            jax.ShapeDtypeStruct((COL_TOP, T), f32),
            jax.ShapeDtypeStruct((NV, LEV, T, T), f32),
            square,
            square,
        ],
        scratch_shapes=[pltpu.VMEM((T, T), i32), pltpu.SemaphoreType.DMA((NV + 2,))],
        compiler_params=params(46 * MIB),
        cost_estimate=cost(6 << 20, 9 << 20),
        name="outer_columns",
    )(state, vert, mask, after)


def corner_kernel(cols, top, bottom, out):
    out[0:COL_COEF, :] = cols[0:COL_COEF, :]
    lane, sub = lanes(PLANES), subl(PLANES)
    keep = column_keep(PLANES)
    for k, rows in enumerate((top, bottom)):
        line = rows[0:PLANES, :]
        at = COL_COEF + k * PLANES
        out[at : at + PLANES, :] = jnp.where(
            (lane == 4) | (lane == 5), pltpu.roll(line, 5, 1) * keep, cols[at : at + PLANES, :]
        )
        first = jnp.broadcast_to(line[:, 0:1], (PLANES, T))
        last = jnp.broadcast_to(line[:, T - 1 : T], (PLANES, T))
        spread = jnp.where(lane == 2 * sub, last, jnp.where(lane == 2 * sub + 1, first, 0.0))
        total = jnp.sum(spread * keep, axis=0, keepdims=True)
        at = COL_TOP + 8 * k
        out[at : at + 8, :] = jnp.broadcast_to(total, (8, T))


def with_corners(cols, top, bottom):
    return pl.pallas_call(
        corner_kernel,
        in_specs=[VMEM] * 3,
        out_specs=VMEM,
        out_shape=jax.ShapeDtypeStruct((COL_SIZE, T), f32),
        compiler_params=params(4 * MIB),
        cost_estimate=cost(1 << 16, 1 << 18),
        name="with_corners",
    )(cols, top, bottom)


def remap_kernel(
    dest_in, count_in, state, weight, out, blocks, planes, surf, dest, count, used, label, sems
):
    rows = T // CHUNKS
    lists = [
        pltpu.make_async_copy(dest_in, dest, sems.at[CHUNKS]),
        pltpu.make_async_copy(count_in, count, sems.at[CHUNKS + 1]),
    ]
    for v in range(NV):
        lists.append(pltpu.make_async_copy(state.at[0, v, 0], planes.at[v], sems.at[CHUNKS + 2 + v]))
    for copy in lists:
        copy.start()

    def fetch(c):
        piece = pl.ds(c * rows, rows)
        return pltpu.make_async_copy(weight.at[0, piece, 0], blocks.at[piece], sems.at[c])

    for c in range(CHUNKS):
        fetch(c).start()
    out[...] = jnp.zeros_like(out)

    def clear(i, _):
        used[i] = 0
        for k in range(CAP):
            label[i * CAP + k] = 0
        return 0

    lax.fori_loop(0, PEERS, clear, 0)
    for copy in lists:
        copy.wait()
    for v in range(NV):
        surf[pl.ds(v, T, stride=NV), :] = planes[v]
    sub = subl(8)

    def slot_of(row, f):
        target = dest[f, row]
        peer = lax.shift_right_logical(target, 7) & (PEERS - 1)
        live = f < count[0, row]
        at = used[peer]
        used[peer] = at + jnp.where(live, 1, 0)
        label[jnp.where(live, peer * CAP + at, PEERS * CAP)] = (target & (T - 1)) + 1
        return jnp.where(live, peer * SLOTS + at, CAP)

    def chunk(c, _):
        fetch(c).wait()
        for r in range(0, rows, 2):
            row = c * rows + r
            slots = [[slot_of(row + q, f) for f in range(FAN)] for q in range(2)]
            pair = surf[pl.ds(pl.multiple_of(row * NV, 8), 8), :]
            pair = jnp.concatenate(
                [jnp.where(sub < NV, pair, 0.0), jnp.where(sub >= NV, pair, 0.0)], axis=1
            ).astype(bf16)
            for f in range(0, FAN, 2):
                block = jnp.concatenate(
                    [
                        jnp.concatenate([blocks[row + q, f], blocks[row + q, f + 1]], axis=1)
                        for q in range(2)
                    ],
                    axis=0,
                )
                product = jnp.dot(pair, block, preferred_element_type=f32)
                for q in range(2):
                    for g in range(2):
                        part = product[q * NV : (q + 1) * NV, g * T : (g + 1) * T]
                        out[slots[q][f + g]] = part
        return 0

    lax.fori_loop(0, CHUNKS, chunk, 0)
    me = lax.axis_index("gx") * lax.axis_size("gy") + lax.axis_index("gy")
    place = lax.broadcasted_iota(i32, (NV, T), 0) * T + lax.broadcasted_iota(i32, (NV, T), 1)
    place = place - me * CAP

    def write(i, _):
        block = jnp.zeros((NV, T), i32)
        for k in range(CAP):
            block = jnp.where(place == k, label[i * CAP + k], block)
        out[i * SLOTS + CAP] = block.astype(f32)
        return 0

    lax.fori_loop(0, PEERS, write, 0)


def remap(dest, count, state, weight):
    return pl.pallas_call(
        remap_kernel,
        in_specs=[HBM] * 4,
        out_specs=VMEM,
        out_shape=jax.ShapeDtypeStruct((PEERS * SLOTS, NV, T), f32),
        scratch_shapes=[
            pltpu.VMEM((T, FAN, T, T), bf16),
            pltpu.VMEM((NV, T, T), f32),
            pltpu.VMEM((T * NV, T), f32),
            pltpu.SMEM((FAN, T), i32),
            pltpu.SMEM((1, T), i32),
            pltpu.SMEM((PEERS,), i32),
            pltpu.SMEM((PEERS * CAP + 8,), i32),
            pltpu.SemaphoreType.DMA((CHUNKS + 2 + NV,)),
        ],
        compiler_params=params(51 * MIB),
        cost_estimate=cost(67 << 20, 20 << 20),
        name="remap",
    )(dest, count, state, weight)


def merged(left, right, back=2):
    return jnp.where((lanes(left.shape[0]) & 1) == 0, left, pltpu.roll(right, T - back, 1))


def diffuse(u, up, down, side, rate):
    rows = u.shape[0]
    lane, sub = lanes(rows), subl(rows)
    north = jnp.where(sub == 0, up, pltpu.roll(u, 1, 0))
    south = jnp.where(sub == rows - 1, down, pltpu.roll(u, rows - 1, 0))
    west = jnp.where(lane == 0, side, pltpu.roll(u, 1, 1))
    east = jnp.where(lane == T - 1, side, pltpu.roll(u, T - 1, 1))
    return u + rate * ((north + south) + (west + east) - 4.0 * u)


def level_diffuse(u, top, bottom, side, rate, l, lo):
    up = top[l : l + 1, :] if lo == 0 else u[l, lo - 1 : lo, :]
    down = bottom[l : l + 1, :] if lo + HALF == T else u[l, lo + HALF : lo + HALF + 1, :]
    spin = side[lo : lo + HALF, :]
    if l:
        spin = pltpu.roll(spin, T - 2 * l, 1)
    return diffuse(u[l, lo : lo + HALF, :], up, down, spin, rate)


def halo_columns(rate, left, right, own):
    lane, sub = lanes(T), subl(T)
    here = merged(left[0:T, :], right[0:T, :])
    outer = merged(left[COL_NEXT : COL_NEXT + T, :], right[COL_NEXT : COL_NEXT + T, :], 4)
    inner = pltpu.roll(own[0:T, :], T - 1, 1)
    ends = [merged(left[at : at + 8, :], right[at : at + 8, :])[0:1, :] for at in (COL_TOP, COL_BOTTOM)]
    north = jnp.where(sub == 0, ends[0], pltpu.roll(here, 1, 0))
    south = jnp.where(sub == T - 1, ends[1], pltpu.roll(here, T - 1, 0))
    plane = ((lane + 1) >> 1) & (PLANES - 1)
    number = jnp.full((T, T), rate[0, 0], f32)
    for v in range(1, NV):
        number = jnp.where(plane // LEV == v, rate[0, v], number)
    h = here + number * ((north + south) + (outer + inner) - 4.0 * here)
    coef = jnp.where(
        (lane & 1) == 0,
        jnp.broadcast_to(left[COL_COEF : COL_COEF + T, 0:1], (T, T)),
        jnp.broadcast_to(right[COL_COEF : COL_COEF + T, 1:2], (T, T)),
    )
    level = plane % LEV
    above = jnp.where(level < LEV - 1, pltpu.roll(h, T - 2, 1) - h, 0.0)
    below = jnp.where(level > 0, pltpu.roll(h, 2, 1) - h, 0.0)
    return here, h + coef * (above + below)


def halo_rows(rate, rows, own, left, right, k, v):
    at = v * LEV
    lane, level = lanes(LEV), subl(LEV)
    here = rows[at : at + LEV, :]
    corner = COL_COEF + k * PLANES + at
    west = jnp.where(
        lane == 0, pltpu.roll(left[corner : corner + LEV, :], T - 4, 1), pltpu.roll(here, 1, 1)
    )
    east = jnp.where(
        lane == T - 1,
        pltpu.roll(right[corner : corner + LEV, :], T - 6, 1),
        pltpu.roll(here, T - 1, 1),
    )
    outer = rows[PLANES + at : PLANES + at + LEV, :]
    inner = own[at : at + LEV, :]
    h = here + rate[0, v] * ((outer + inner) + (west + east) - 4.0 * here)
    above = jnp.where(level < LEV - 1, pltpu.roll(h, LEV - 1, 0) - h, 0.0)
    below = jnp.where(level > 0, pltpu.roll(h, 1, 0) - h, 0.0)
    return h + rows[ROW_VERT : ROW_VERT + 1, :] * (above + below)


def step_kernel(
    rate, u, coef, sea, own, top, bottom, near, far, after,
    out, keep, w, stage, inner, top1, bottom1, top2, bottom2, side1, side2, turned, sems,
):
    del after

    def emit(v):
        levels = pl.ds(2, LEV - 2)
        return pltpu.make_async_copy(stage.at[v], out.at[0, v, levels], sems.at[v])

    up, down, _, _ = inside()
    side1[...], side2[...] = halo_columns(rate, near, far, own)
    for v in range(NV):
        at = v * LEV
        for l in range(LEV):
            inner[0, at + l : at + l + 1, :] = u[v, l, 0:1, :] * up
            inner[1, at + l : at + l + 1, :] = u[v, l, T - 1 : T, :] * down
    for v in range(NV):
        at = v * LEV
        top1[v] = top[at : at + LEV, :]
        bottom1[v] = bottom[at : at + LEV, :]
        top2[v] = halo_rows(rate, top, inner.at[0], near, far, 0, v)
        bottom2[v] = halo_rows(rate, bottom, inner.at[1], near, far, 1, v)

    def first(v, _):
        number = rate[0, v]
        turned[...] = pltpu.roll(side1[...], lax.rem((NV - v) * 32, T), 1)
        source, result = u.at[v], w.at[v]
        for lo in range(0, T, HALF):
            mix = coef[lo : lo + HALF, :]
            at = lambda l: level_diffuse(source, top1.at[v], bottom1.at[v], turned, number, l, lo)
            before, here = None, at(0)
            for l in range(LEV):
                after = at(l + 1) if l + 1 < LEV else None
                if before is None:
                    term = after - here
                elif after is None:
                    term = before - here
                else:
                    term = (after - here) + (before - here)
                result[l, lo : lo + HALF, :] = here + mix * term
                before, here = here, after
        return 0

    lax.fori_loop(0, NV, first, 0)

    def second(v, _):
        number = rate[0, v]
        turned[...] = pltpu.roll(side2[...], lax.rem((NV - v) * 32, T), 1)
        source, result = w.at[v], stage.at[v]
        for lo in range(0, T, HALF):
            mix = coef[lo : lo + HALF, :]
            at = lambda l: level_diffuse(source, top2.at[v], bottom2.at[v], turned, number, l, lo)
            before, here = at(1), at(2)
            row = pl.multiple_of(v * T + lo, 8)
            keep[pl.ds(KEEP_BASE + row, HALF), :] = source[0, lo : lo + HALF, :]
            keep[pl.ds(KEEP_ONE + row, HALF), :] = before
            keep[pl.ds(KEEP_PART + row, HALF), :] = before + mix * ((here - before) - before)
            for l in range(2, LEV):
                after = at(l + 1) if l + 1 < LEV else None
                term = before - here
                if after is not None:
                    term = (after - here) + term
                result[l - 2, lo : lo + HALF, :] = here + mix * term
                before, here = here, after
        emit(v).start()
        return 0

    lax.fori_loop(0, NV, second, 0)
    keep[KEEP_VERT : KEEP_VERT + T, :] = coef[...]
    keep[KEEP_SEA : KEEP_SEA + T, :] = sea[...]
    keep[KEEP_SIDE : KEEP_SIDE + T, :] = side2[...]
    coefs = pl.ds(COL_COEF, T)
    keep[KEEP_SEA_SIDE : KEEP_SEA_SIDE + T, :] = jnp.where(
        lanes(T) == 0, pltpu.roll(near[coefs, :], T - 2, 1), pltpu.roll(far[coefs, :], T - 4, 1)
    )
    for k, (rows, line) in enumerate(((top2, top), (bottom2, bottom))):
        for v in range(NV):
            keep[KEEP_ENDS + 8 * k + v : KEEP_ENDS + 8 * k + v + 1, :] = rows[v, 0:1, :]
        keep[KEEP_ENDS + 8 * k + NV : KEEP_ENDS + 8 * k + 8, :] = line[ROW_SEA : ROW_SEA + NV, :]
    for v in range(NV):
        emit(v).wait()


def two_steps(rate, u, coef, sea, own, top, bottom, left, right, after):
    rows = pltpu.VMEM((NV, LEV, T), f32)
    square = pltpu.VMEM((T, T), f32)
    return pl.pallas_call(
        step_kernel,
        in_specs=[SMEM] + [VMEM] * 8 + [HBM],
        out_specs=[HBM, VMEM],
        out_shape=[
            jax.ShapeDtypeStruct((1,) + u.shape, f32),
            jax.ShapeDtypeStruct((KEEP_SIZE, T), f32),
        ],
        scratch_shapes=[
            pltpu.VMEM((NV, LEV, T, T), f32),
            pltpu.VMEM((NV, LEV - 2, T, T), f32),
            pltpu.VMEM((2, PLANES, T), f32),
            rows,
            rows,
            rows,
            rows,
            square,
            square,
            square,
            pltpu.SemaphoreType.DMA((NV,)),
        ],
        compiler_params=params(16 * MIB),
        cost_estimate=cost(48 << 20, 10 << 20),
        name="two_steps",
    )(rate, u, coef, sea, own, top, bottom, left, right, after)


def unpack_kernel(data, after, imp, first, last, cols):
    del after
    size = SLOTS * NV
    sub = subl(T).astype(f32) + 1.0
    picks = []
    for j in range(NV):
        table = jnp.sum(data[pl.ds(CAP * NV + j, PEERS, stride=size), :], axis=0, keepdims=True)
        picks.append((sub == table).astype(bf16))
    pick = jnp.concatenate(picks, axis=1)
    lane = lanes(T)
    up, down, _, _ = inside()
    acc = jnp.zeros((T, T), f32)
    for v in range(NV):
        block = jnp.concatenate(
            [data[pl.ds(s * size + v, CAP, stride=NV), :] for s in range(PEERS)], axis=0
        )
        high = block.astype(bf16)
        low = (block - high.astype(f32)).astype(bf16)
        total = jnp.dot(pick, high, preferred_element_type=f32)
        total = total + jnp.dot(pick, low, preferred_element_type=f32)
        imp[v] = total
        for out, row, keep in ((first, 0, up), (last, T - 1, down)):
            out[v : v + 1, :] = total[row : row + 1, :] * keep
            out[NV + v : NV + v + 1, :] = total[row : row + 1, :] * keep
        acc = jnp.where((lane >> 1) == v, pltpu.roll(total, 2 * v + 1, 1), acc)
    cols[...] = jnp.transpose(acc * column_keep(T))[0 : 2 * NV, :]


def unpack(data, after):
    return pl.pallas_call(
        unpack_kernel,
        in_specs=[VMEM, HBM],
        out_specs=[VMEM] * 4,
        out_shape=[
            jax.ShapeDtypeStruct((NV, T, T), f32),
            jax.ShapeDtypeStruct((2 * NV, T), f32),
            jax.ShapeDtypeStruct((2 * NV, T), f32),
            jax.ShapeDtypeStruct((2 * NV, T), f32),
        ],
        compiler_params=params(12 * MIB),
        cost_estimate=cost(200 << 20, 2 << 20),
        name="unpack",
    )(data, after)


def final_kernel(
    horiz, relax, mid, near, imp, imp_top, imp_bottom, imp_left, imp_right, out, stage, sems
):
    del mid
    odd = (subl(2 * NV) & 1) == 1
    ends = jnp.where(odd, imp_right[...], imp_left[...])
    ends = jnp.concatenate([ends, jnp.zeros((T - 2 * NV, T), f32)], axis=0)
    side_new = jnp.transpose(ends)
    sea, sea_side = near[KEEP_SEA : KEEP_SEA + T, :], near[KEEP_SEA_SIDE : KEEP_SEA_SIDE + T, :]
    coef = near[KEEP_VERT : KEEP_VERT + T, :]
    side_base = near[KEEP_SIDE : KEEP_SIDE + T, :]
    lane = lanes(T)
    copies = []
    for v in range(NV):
        pull = relax[0, v]

        def relaxed(base, wet, new, pull=pull):
            return base + pull * wet * (new - base)

        ends = []
        for k, new in enumerate((imp_top, imp_bottom)):
            at = KEEP_ENDS + 8 * k
            ends.append(
                relaxed(near[at + v : at + v + 1, :], near[at + NV : at + NV + 1, :], new[v : v + 1, :])
            )
        turn = (T - 32 * v) % T
        base = pltpu.roll(side_base, turn, 1) if turn else side_base
        new = pltpu.roll(side_new, T - 2 * v, 1) if v else side_new
        new = jnp.where(lane == 0, new, pltpu.roll(side_new, T - 2 - 2 * v, 1))
        u = relaxed(near[KEEP_BASE + v * T : KEEP_BASE + (v + 1) * T, :], sea, imp[v])
        h = diffuse(u, ends[0], ends[1], relaxed(base, sea_side, new), horiz[0, v])
        one = near[KEEP_ONE + v * T : KEEP_ONE + (v + 1) * T, :]
        stage[v, 0] = relaxed(h + coef * (one - h), sea, imp[v])
        stage[v, 1] = near[KEEP_PART + v * T : KEEP_PART + (v + 1) * T, :] + coef * h
        copies.append(
            pltpu.make_async_copy(stage.at[v], out.at[0, v, pl.ds(0, 2)], sems.at[v])
        )
        copies[-1].start()
    for copy in copies:
        copy.wait()


def final(horiz, relax, mid, keep, imp, imp_rows, imp_cols):
    return pl.pallas_call(
        final_kernel,
        in_specs=[SMEM, SMEM, HBM] + [VMEM] * 6,
        out_specs=HBM,
        out_shape=jax.ShapeDtypeStruct(mid.shape, f32),
        input_output_aliases={2: 0},
        scratch_shapes=[
            pltpu.VMEM((NV, 2, T, T), f32),
            pltpu.SemaphoreType.DMA((NV,)),
        ],
        compiler_params=params(6 * MIB),
        cost_estimate=cost(2 << 20, 3 << 20),
        name="final",
    )(horiz, relax, mid, keep, imp, *imp_rows, *imp_cols)


def shifted(block, axis, by, across=False):
    count = lax.axis_size(axis)
    if not across:
        return lax.ppermute(block, axis, [(i, (i + by) % count) for i in range(count)])
    return lax.ppermute(
        block,
        ("comp", axis),
        [
            (c * count + i, (1 - c) * count + (i + by) % count)
            for c in range(2)
            for i in range(count)
        ],
    )


def local(
    state, horiz_coef, vert_coef, couple_rate, sea_mask, dest_block, entry_count, remap_weight
):
    dest = dest_block.reshape(T, FAN).T
    sent = remap(dest, entry_count.reshape(1, T), state, remap_weight)
    packed = lax.all_to_all(
        sent.reshape(PEERS, SLOTS, NV, T), ("gx", "gy"), split_axis=0, concat_axis=0, tiled=True
    )
    head, tail = outer_rows(state, vert_coef, sea_mask, sent)
    top, bottom = shifted(tail, "gx", 1), shifted(head, "gx", -1)
    cols, tile, coef, sea = outer_columns(state, vert_coef, sea_mask, head)
    cols = with_corners(cols, top, bottom)
    left, right = shifted(cols, "gy", 1), shifted(cols, "gy", -1)
    new, first, last, sides = unpack(packed.reshape(PEERS * SLOTS * NV, T), cols)
    imp = lax.ppermute(new, "comp", [(0, 1), (1, 0)])
    imp_rows = shifted(last, "gx", 1, True), shifted(first, "gx", -1, True)
    imp_cols = shifted(sides, "gy", 1, True), shifted(sides, "gy", -1, True)
    mid, keep = two_steps(horiz_coef, tile, coef, sea, cols, top, bottom, left, right, new)
    return final(horiz_coef, couple_rate, mid, keep, imp, imp_rows, imp_cols)


def solution(mesh):
    in_specs = (
        P("comp", None, None, "gx", "gy"),
        P("comp", None),
        P("comp", "gx", "gy"),
        P("comp", None),
        P("comp", "gx", "gy"),
        P("comp", "gx", "gy", None),
        P("comp", "gx", "gy"),
        P("comp", "gx", "gy", None, None, None),
    )
    out_specs = P("comp", None, None, "gx", "gy")
    return jax.shard_map(local, mesh=mesh, in_specs=in_specs, out_specs=out_specs, check_vma=False)
```

```python
import jax
import jax.numpy as jnp
from jax import lax
from jax.experimental import pallas as pl
from jax.experimental.pallas import tpu as pltpu
from jax.sharding import PartitionSpec as P

NV = 4
LEV = 16
PLANES = NV * LEV
T = 128
FAN = 4
CAP = 8
PEERS = 64
SLOTS = CAP + 1
HALF = 64
CHUNKS = 16
MIRROR = 4
MIB = 1024 * 1024
ROW_VERT = 2 * PLANES
ROW_SEA = ROW_VERT + 8
ROW_SIZE = ROW_SEA + 8
COL_NEXT = T
COL_COEF = 2 * T
COL_TOP = 3 * T
COL_BOTTOM = COL_TOP + 8
COL_SIZE = COL_BOTTOM + 8
KEEP_BASE = 0
KEEP_ONE = NV * T
KEEP_PART = 2 * NV * T
KEEP_VERT = 3 * NV * T
KEEP_SEA = KEEP_VERT + T
KEEP_SIDE = KEEP_SEA + T
KEEP_SEA_SIDE = KEEP_SIDE + T
KEEP_ENDS = KEEP_SEA_SIDE + T
KEEP_SIZE = KEEP_ENDS + 16

f32 = jnp.float32
i32 = jnp.int32
bf16 = jnp.bfloat16

SMEM = pl.BlockSpec(memory_space=pltpu.SMEM)
VMEM = pl.BlockSpec(memory_space=pltpu.VMEM)
HBM = pl.BlockSpec(memory_space=pl.ANY)


def params(limit):
    return pltpu.CompilerParams(vmem_limit_bytes=limit)


def cost(flops, size):
    return pl.CostEstimate(flops=flops, bytes_accessed=size, transcendentals=0)


def lanes(rows):
    return lax.broadcasted_iota(i32, (rows, T), 1)


def subl(rows):
    return lax.broadcasted_iota(i32, (rows, T), 0)


def inside(flip=0):
    gx, gy = lax.axis_index("gx"), lax.axis_index("gy") ^ flip
    one = lambda test: jnp.where(test, 1.0, 0.0).astype(f32)
    return (
        one(gx > 0),
        one(gx < lax.axis_size("gx") - 1),
        one(gy > 0),
        one(gy < lax.axis_size("gy") - 1),
    )


def column_keep(rows, flip=0):
    _, _, before, after = inside(flip)
    return jnp.where((lanes(rows) & 1) == 0, after, before)


def run(copies):
    for copy in copies:
        copy.start()
    for copy in copies:
        copy.wait()


def row_kernel(state, vert, mask, head, tail, high, low, coef, sea, sems):
    ends = pl.ds(0, 8), pl.ds(T - 8, 8)
    copies = []
    for k, buffer in enumerate((high, low)):
        copies.append(pltpu.make_async_copy(state.at[0, :, :, ends[k]], buffer, sems.at[3 * k]))
        copies.append(pltpu.make_async_copy(vert.at[0, ends[k]], coef.at[k], sems.at[3 * k + 1]))
        copies.append(pltpu.make_async_copy(mask.at[0, ends[k]], sea.at[k], sems.at[3 * k + 2]))
    run(copies)
    up, down, _, _ = inside()
    for k, (out, buffer, keep) in enumerate(((head, high, up), (tail, low, down))):
        outer, following = (0, 1) if k == 0 else (7, 6)
        for p in range(PLANES):
            v, l = divmod(p, LEV)
            out[p : p + 1, :] = buffer[v, l, outer : outer + 1, :] * keep
            out[PLANES + p : PLANES + p + 1, :] = buffer[v, l, following : following + 1, :] * keep
        line = coef[k, outer : outer + 1, :] * keep
        out[ROW_VERT : ROW_VERT + 8, :] = jnp.broadcast_to(line, (8, T))
        line = sea[k, outer : outer + 1, :].astype(f32) * keep
        out[ROW_SEA : ROW_SEA + 8, :] = jnp.broadcast_to(line, (8, T))


def outer_rows(state, vert, mask):
    return pl.pallas_call(
        row_kernel,
        in_specs=[HBM] * 3,
        out_specs=[VMEM, VMEM],
        out_shape=[jax.ShapeDtypeStruct((ROW_SIZE, T), f32)] * 2,
        scratch_shapes=[
            pltpu.VMEM((NV, LEV, 8, T), f32),
            pltpu.VMEM((NV, LEV, 8, T), f32),
            pltpu.VMEM((2, 8, T), f32),
            pltpu.VMEM((2, 8, T), i32),
            pltpu.SemaphoreType.DMA((6,)),
        ],
        compiler_params=params(58 * MIB),
        cost_estimate=cost(1 << 16, 1 << 19),
        name="outer_rows",
    )(state, vert, mask)


def column_kernel(state, vert, mask, after, cols, tile, coef, wet, sea, sems):
    del after
    loads = [pltpu.make_async_copy(state.at[0, v], tile.at[v], sems.at[v]) for v in range(NV)]
    loads.append(pltpu.make_async_copy(vert.at[0], coef, sems.at[NV]))
    loads.append(pltpu.make_async_copy(mask.at[0], sea, sems.at[NV + 1]))
    for load in loads:
        load.start()
    lane = lanes(HALF)
    keep = column_keep(HALF)
    for v in range(NV):
        loads[v].wait()
        for lo in range(0, T, HALF):
            outer, following = pl.ds(lo, HALF), pl.ds(COL_NEXT + lo, HALF)
            acc = jnp.zeros((HALF, T), f32) if v == 0 else cols[outer, :]
            acc2 = jnp.zeros((HALF, T), f32) if v == 0 else cols[following, :]
            for l in range(LEV):
                p = v * LEV + l
                plane = tile[v, l, lo : lo + HALF, :]
                acc = jnp.where((lane >> 1) == p, pltpu.roll(plane, (2 * p + 1) % T, 1), acc)
                hit = (lane == 2 * p) | (lane == (2 * p + 3) % T)
                acc2 = jnp.where(hit, pltpu.roll(plane, (2 * p + 2) % T, 1), acc2)
            last = v == NV - 1
            cols[outer, :] = acc * keep if last else acc
            cols[following, :] = acc2 * keep if last else acc2
    loads[NV].wait()
    loads[NV + 1].wait()
    lane = lanes(T)
    wet[...] = sea[...].astype(f32)
    pair = jnp.where(lane < 2, pltpu.roll(coef[...], 1, 1), pltpu.roll(wet[...], 3, 1))
    cols[COL_COEF : COL_COEF + T, :] = pair * column_keep(T)


def outer_columns(state, vert, mask, after):
    square = jax.ShapeDtypeStruct((T, T), f32)
    return pl.pallas_call(
        column_kernel,
        in_specs=[HBM] * 4,
        out_specs=[VMEM] * 4,
        out_shape=[
            jax.ShapeDtypeStruct((COL_TOP, T), f32),
            jax.ShapeDtypeStruct((NV, LEV, T, T), f32),
            square,
            square,
        ],
        scratch_shapes=[pltpu.VMEM((T, T), i32), pltpu.SemaphoreType.DMA((NV + 2,))],
        compiler_params=params(46 * MIB),
        cost_estimate=cost(6 << 20, 9 << 20),
        name="outer_columns",
    )(state, vert, mask, after)


def corner_kernel(cols, top, bottom, out):
    out[0:COL_COEF, :] = cols[0:COL_COEF, :]
    lane, sub = lanes(PLANES), subl(PLANES)
    keep = column_keep(PLANES)
    for k, rows in enumerate((top, bottom)):
        line = rows[0:PLANES, :]
        at = COL_COEF + k * PLANES
        out[at : at + PLANES, :] = jnp.where(
            (lane == 4) | (lane == 5), pltpu.roll(line, 5, 1) * keep, cols[at : at + PLANES, :]
        )
        first = jnp.broadcast_to(line[:, 0:1], (PLANES, T))
        last = jnp.broadcast_to(line[:, T - 1 : T], (PLANES, T))
        spread = jnp.where(lane == 2 * sub, last, jnp.where(lane == 2 * sub + 1, first, 0.0))
        total = jnp.sum(spread * keep, axis=0, keepdims=True)
        at = COL_TOP + 8 * k
        out[at : at + 8, :] = jnp.broadcast_to(total, (8, T))


def with_corners(cols, top, bottom):
    return pl.pallas_call(
        corner_kernel,
        in_specs=[VMEM] * 3,
        out_specs=VMEM,
        out_shape=jax.ShapeDtypeStruct((COL_SIZE, T), f32),
        compiler_params=params(4 * MIB),
        cost_estimate=cost(1 << 16, 1 << 18),
        name="with_corners",
    )(cols, top, bottom)


def remap_kernel(
    dest_in, count_in, state, weight, after, out, blocks, planes, surf, dest, count, used, label, sems
):
    del after
    rows = T // CHUNKS
    lists = [
        pltpu.make_async_copy(dest_in, dest, sems.at[CHUNKS]),
        pltpu.make_async_copy(count_in, count, sems.at[CHUNKS + 1]),
    ]
    for v in range(NV):
        lists.append(pltpu.make_async_copy(state.at[0, v, 0], planes.at[v], sems.at[CHUNKS + 2 + v]))
    for copy in lists:
        copy.start()

    def fetch(c):
        piece = pl.ds(c * rows, rows)
        return pltpu.make_async_copy(weight.at[0, piece, 0], blocks.at[piece], sems.at[c])

    for c in range(CHUNKS):
        fetch(c).start()
    out[...] = jnp.zeros_like(out)

    def clear(i, _):
        used[i] = 0
        for k in range(CAP):
            label[i * CAP + k] = 0
        return 0

    lax.fori_loop(0, PEERS, clear, 0)
    for copy in lists:
        copy.wait()
    for v in range(NV):
        surf[pl.ds(v, T, stride=NV), :] = planes[v]
    sub = subl(8)

    def slot_of(row, f):
        target = dest[f, row]
        peer = (lax.shift_right_logical(target, 7) & (PEERS - 1)) ^ MIRROR
        live = f < count[0, row]
        at = used[peer]
        used[peer] = at + jnp.where(live, 1, 0)
        label[jnp.where(live, peer * CAP + at, PEERS * CAP)] = (target & (T - 1)) + 1
        return jnp.where(live, peer * SLOTS + at, CAP)

    def chunk(c, _):
        fetch(c).wait()
        for r in range(0, rows, 2):
            row = c * rows + r
            slots = [[slot_of(row + q, f) for f in range(FAN)] for q in range(2)]
            pair = surf[pl.ds(pl.multiple_of(row * NV, 8), 8), :]
            pair = jnp.concatenate(
                [jnp.where(sub < NV, pair, 0.0), jnp.where(sub >= NV, pair, 0.0)], axis=1
            ).astype(bf16)
            for f in range(0, FAN, 2):
                block = jnp.concatenate(
                    [
                        jnp.concatenate([blocks[row + q, f], blocks[row + q, f + 1]], axis=1)
                        for q in range(2)
                    ],
                    axis=0,
                )
                product = jnp.dot(pair, block, preferred_element_type=f32)
                for q in range(2):
                    for g in range(2):
                        part = product[q * NV : (q + 1) * NV, g * T : (g + 1) * T]
                        out[slots[q][f + g]] = part
        return 0

    lax.fori_loop(0, CHUNKS, chunk, 0)
    me = lax.axis_index("gx") * lax.axis_size("gy") + lax.axis_index("gy")
    place = lax.broadcasted_iota(i32, (NV, T), 0) * T + lax.broadcasted_iota(i32, (NV, T), 1)
    place = place - me * CAP

    def write(i, _):
        block = jnp.zeros((NV, T), i32)
        for k in range(CAP):
            block = jnp.where(place == k, label[i * CAP + k], block)
        out[i * SLOTS + CAP] = block.astype(f32)
        return 0

    lax.fori_loop(0, PEERS, write, 0)


def remap(dest, count, state, weight, after):
    return pl.pallas_call(
        remap_kernel,
        in_specs=[HBM] * 5,
        out_specs=VMEM,
        out_shape=jax.ShapeDtypeStruct((PEERS * SLOTS, NV, T), f32),
        scratch_shapes=[
            pltpu.VMEM((T, FAN, T, T), bf16),
            pltpu.VMEM((NV, T, T), f32),
            pltpu.VMEM((T * NV, T), f32),
            pltpu.SMEM((FAN, T), i32),
            pltpu.SMEM((1, T), i32),
            pltpu.SMEM((PEERS,), i32),
            pltpu.SMEM((PEERS * CAP + 8,), i32),
            pltpu.SemaphoreType.DMA((CHUNKS + 2 + NV,)),
        ],
        compiler_params=params(51 * MIB),
        cost_estimate=cost(67 << 20, 20 << 20),
        name="remap",
    )(dest, count, state, weight, after)


def merged(left, right, back=2):
    return jnp.where((lanes(left.shape[0]) & 1) == 0, left, pltpu.roll(right, T - back, 1))


def diffuse(u, up, down, side, rate):
    rows = u.shape[0]
    lane, sub = lanes(rows), subl(rows)
    north = jnp.where(sub == 0, up, pltpu.roll(u, 1, 0))
    south = jnp.where(sub == rows - 1, down, pltpu.roll(u, rows - 1, 0))
    west = jnp.where(lane == 0, side, pltpu.roll(u, 1, 1))
    east = jnp.where(lane == T - 1, side, pltpu.roll(u, T - 1, 1))
    return u + rate * ((north + south) + (west + east) - 4.0 * u)


def level_inner(u, rate, l, lo):
    nothing = jnp.zeros((1, T), f32)
    up = nothing if lo == 0 else u[l, lo - 1 : lo, :]
    down = nothing if lo + HALF == T else u[l, lo + HALF : lo + HALF + 1, :]
    return diffuse(u[l, lo : lo + HALF, :], up, down, 0.0, rate)


def inner_kernel(rate, u, coef, after, out):
    del after

    def body(v, _):
        number = rate[0, v]
        source, result = u.at[v], out.at[v]
        for lo in range(0, T, HALF):
            mix = coef[lo : lo + HALF, :]
            before, here = None, level_inner(source, number, 0, lo)
            for l in range(LEV):
                after = level_inner(source, number, l + 1, lo) if l + 1 < LEV else None
                if before is None:
                    term = after - here
                elif after is None:
                    term = before - here
                else:
                    term = (after - here) + (before - here)
                result[l, lo : lo + HALF, :] = here + mix * term
                before, here = here, after
        return 0

    lax.fori_loop(0, NV, body, 0)


def inner_step(rate, u, coef, after):
    return pl.pallas_call(
        inner_kernel,
        in_specs=[SMEM, VMEM, VMEM, HBM],
        out_specs=VMEM,
        out_shape=jax.ShapeDtypeStruct(u.shape, f32),
        compiler_params=params(10 * MIB),
        cost_estimate=cost(24 << 20, 9 << 20),
        name="inner_step",
    )(rate, u, coef, after)


def level_diffuse(u, top, bottom, side, rate, l, lo):
    up = top[l : l + 1, :] if lo == 0 else u[l, lo - 1 : lo, :]
    down = bottom[l : l + 1, :] if lo + HALF == T else u[l, lo + HALF : lo + HALF + 1, :]
    spin = side[lo : lo + HALF, :]
    if l:
        spin = pltpu.roll(spin, T - 2 * l, 1)
    return diffuse(u[l, lo : lo + HALF, :], up, down, spin, rate)


def halo_columns(rate, vert, left, right, own):
    lane, sub = lanes(T), subl(T)
    here = merged(left[0:T, :], right[0:T, :])
    outer = merged(left[COL_NEXT : COL_NEXT + T, :], right[COL_NEXT : COL_NEXT + T, :], 4)
    inner = pltpu.roll(own[0:T, :], T - 1, 1)
    ends = [merged(left[at : at + 8, :], right[at : at + 8, :])[0:1, :] for at in (COL_TOP, COL_BOTTOM)]
    north = jnp.where(sub == 0, ends[0], pltpu.roll(here, 1, 0))
    south = jnp.where(sub == T - 1, ends[1], pltpu.roll(here, T - 1, 0))
    plane = ((lane + 1) >> 1) & (PLANES - 1)
    number = jnp.full((T, T), rate[0, 0], f32)
    for v in range(1, NV):
        number = jnp.where(plane // LEV == v, rate[0, v], number)
    h = here + number * ((north + south) + (outer + inner) - 4.0 * here)
    coef = jnp.where(
        (lane & 1) == 0,
        jnp.broadcast_to(left[COL_COEF : COL_COEF + T, 0:1], (T, T)),
        jnp.broadcast_to(right[COL_COEF : COL_COEF + T, 1:2], (T, T)),
    )
    level = plane % LEV

    def mixed(h, coef):
        above = jnp.where(level < LEV - 1, pltpu.roll(h, T - 2, 1) - h, 0.0)
        below = jnp.where(level > 0, pltpu.roll(h, 2, 1) - h, 0.0)
        return h + coef * (above + below)

    mine = jnp.where(
        (lane & 1) == 0,
        jnp.broadcast_to(vert[:, 0:1], (T, T)),
        jnp.broadcast_to(vert[:, T - 1 : T], (T, T)),
    )
    return mixed(number * here, mine), mixed(h, coef)


def halo_rows(rate, vert, rows, own, left, right, k, v):
    at = v * LEV
    lane, level = lanes(LEV), subl(LEV)
    here = rows[at : at + LEV, :]
    corner = COL_COEF + k * PLANES + at
    west = jnp.where(
        lane == 0, pltpu.roll(left[corner : corner + LEV, :], T - 4, 1), pltpu.roll(here, 1, 1)
    )
    east = jnp.where(
        lane == T - 1,
        pltpu.roll(right[corner : corner + LEV, :], T - 6, 1),
        pltpu.roll(here, T - 1, 1),
    )
    outer = rows[PLANES + at : PLANES + at + LEV, :]
    inner = own[at : at + LEV, :]
    h = here + rate[0, v] * ((outer + inner) + (west + east) - 4.0 * here)

    def mixed(h, coef):
        above = jnp.where(level < LEV - 1, pltpu.roll(h, LEV - 1, 0) - h, 0.0)
        below = jnp.where(level > 0, pltpu.roll(h, 1, 0) - h, 0.0)
        return h + coef * (above + below)

    edge = k * (T - 1)
    return (
        mixed(rate[0, v] * here, vert[edge : edge + 1, :]),
        mixed(h, rows[ROW_VERT : ROW_VERT + 1, :]),
    )


def step_kernel(
    rate, inner, coef, sea, head, tail, own, top, bottom, near, far, after,
    out, keep, w, stage, ends, top1, bottom1, top2, bottom2, side1, side2, turned, sems,
):
    del after
    loads = [
        pltpu.make_async_copy(rows.at[pl.ds(0, PLANES)], ends.at[k], sems.at[k])
        for k, rows in enumerate((head, tail))
    ]
    for load in loads:
        load.start()

    def emit(v):
        levels = pl.ds(2, LEV - 2)
        return pltpu.make_async_copy(stage.at[v], out.at[0, v, levels], sems.at[v])

    side1[...], side2[...] = halo_columns(rate, coef, near, far, own)
    for load in loads:
        load.wait()
    for v in range(NV):
        top1[v], top2[v] = halo_rows(rate, coef, top, ends.at[0], near, far, 0, v)
        bottom1[v], bottom2[v] = halo_rows(rate, coef, bottom, ends.at[1], near, far, 1, v)
    lane = lanes(HALF)
    rim = (lane == 0) | (lane == T - 1)

    def complete(v, _):
        turned[...] = pltpu.roll(side1[...], lax.rem((NV - v) * 32, T), 1)
        for l in range(LEV):
            for lo in range(0, T, HALF):
                add = turned[lo : lo + HALF, :]
                if l:
                    add = pltpu.roll(add, T - 2 * l, 1)
                w[v, l, lo : lo + HALF, :] = inner[v, l, lo : lo + HALF, :] + jnp.where(rim, add, 0.0)
            w[v, l, 0:1, :] = w[v, l, 0:1, :] + top1[v, l : l + 1, :]
            w[v, l, T - 1 : T, :] = w[v, l, T - 1 : T, :] + bottom1[v, l : l + 1, :]
        return 0

    lax.fori_loop(0, NV, complete, 0)

    def second(v, _):
        number = rate[0, v]
        turned[...] = pltpu.roll(side2[...], lax.rem((NV - v) * 32, T), 1)
        source, result = w.at[v], stage.at[v]
        for lo in range(0, T, HALF):
            mix = coef[lo : lo + HALF, :]
            at = lambda l: level_diffuse(source, top2.at[v], bottom2.at[v], turned, number, l, lo)
            before, here = at(1), at(2)
            row = pl.multiple_of(v * T + lo, 8)
            keep[pl.ds(KEEP_BASE + row, HALF), :] = source[0, lo : lo + HALF, :]
            keep[pl.ds(KEEP_ONE + row, HALF), :] = before
            keep[pl.ds(KEEP_PART + row, HALF), :] = before + mix * ((here - before) - before)
            for l in range(2, LEV):
                after = at(l + 1) if l + 1 < LEV else None
                term = before - here
                if after is not None:
                    term = (after - here) + term
                result[l - 2, lo : lo + HALF, :] = here + mix * term
                before, here = here, after
        emit(v).start()
        return 0

    lax.fori_loop(0, NV, second, 0)
    keep[KEEP_VERT : KEEP_VERT + T, :] = coef[...]
    keep[KEEP_SEA : KEEP_SEA + T, :] = sea[...]
    keep[KEEP_SIDE : KEEP_SIDE + T, :] = side2[...]
    coefs = pl.ds(COL_COEF, T)
    keep[KEEP_SEA_SIDE : KEEP_SEA_SIDE + T, :] = jnp.where(
        lanes(T) == 0, pltpu.roll(near[coefs, :], T - 2, 1), pltpu.roll(far[coefs, :], T - 4, 1)
    )
    for k, (rows, line) in enumerate(((top2, top), (bottom2, bottom))):
        for v in range(NV):
            keep[KEEP_ENDS + 8 * k + v : KEEP_ENDS + 8 * k + v + 1, :] = rows[v, 0:1, :]
        keep[KEEP_ENDS + 8 * k + NV : KEEP_ENDS + 8 * k + 8, :] = line[ROW_SEA : ROW_SEA + NV, :]
    for v in range(NV):
        emit(v).wait()


def second_step(rate, inner, coef, sea, head, tail, own, top, bottom, left, right, after):
    rows = pltpu.VMEM((NV, LEV, T), f32)
    square = pltpu.VMEM((T, T), f32)
    return pl.pallas_call(
        step_kernel,
        in_specs=[SMEM] + [VMEM] * 3 + [HBM] * 2 + [VMEM] * 5 + [HBM],
        out_specs=[HBM, VMEM],
        out_shape=[
            jax.ShapeDtypeStruct((1,) + inner.shape, f32),
            jax.ShapeDtypeStruct((KEEP_SIZE, T), f32),
        ],
        scratch_shapes=[
            pltpu.VMEM((NV, LEV, T, T), f32),
            pltpu.VMEM((NV, LEV - 2, T, T), f32),
            pltpu.VMEM((2, PLANES, T), f32),
            rows,
            rows,
            rows,
            rows,
            square,
            square,
            square,
            pltpu.SemaphoreType.DMA((NV,)),
        ],
        compiler_params=params(16 * MIB),
        cost_estimate=cost(48 << 20, 10 << 20),
        name="second_step",
    )(rate, inner, coef, sea, head, tail, own, top, bottom, left, right, after)


def unpack_kernel(data, left, right, step, imp, first, last, cols):
    del left, right, step
    size = SLOTS * NV
    sub = subl(T).astype(f32) + 1.0
    picks = []
    for j in range(NV):
        table = jnp.sum(data[pl.ds(CAP * NV + j, PEERS, stride=size), :], axis=0, keepdims=True)
        picks.append((sub == table).astype(bf16))
    pick = jnp.concatenate(picks, axis=1)
    lane = lanes(T)
    up, down, _, _ = inside()
    acc = jnp.zeros((T, T), f32)
    for v in range(NV):
        block = jnp.concatenate(
            [data[pl.ds(s * size + v, CAP, stride=NV), :] for s in range(PEERS)], axis=0
        )
        high = block.astype(bf16)
        low = (block - high.astype(f32)).astype(bf16)
        total = jnp.dot(pick, high, preferred_element_type=f32)
        total = total + jnp.dot(pick, low, preferred_element_type=f32)
        imp[v] = total
        for out, row, keep in ((first, 0, up), (last, T - 1, down)):
            out[v : v + 1, :] = total[row : row + 1, :] * keep
            out[NV + v : NV + v + 1, :] = total[row : row + 1, :] * keep
        acc = jnp.where((lane >> 1) == v, pltpu.roll(total, 2 * v + 1, 1), acc)
    cols[...] = jnp.transpose(acc * column_keep(T, MIRROR))[0 : 2 * NV, :]


def unpack(data, *after):
    return pl.pallas_call(
        unpack_kernel,
        in_specs=[VMEM] + [HBM] * len(after),
        out_specs=[VMEM] * 4,
        out_shape=[
            jax.ShapeDtypeStruct((NV, T, T), f32),
            jax.ShapeDtypeStruct((2 * NV, T), f32),
            jax.ShapeDtypeStruct((2 * NV, T), f32),
            jax.ShapeDtypeStruct((2 * NV, T), f32),
        ],
        compiler_params=params(12 * MIB),
        cost_estimate=cost(200 << 20, 2 << 20),
        name="unpack",
    )(data, *after)


def final_kernel(
    horiz, relax, mid, near, imp, imp_top, imp_bottom, imp_left, imp_right, out, stage, sems
):
    del mid
    odd = (subl(2 * NV) & 1) == 1
    ends = jnp.where(odd, imp_right[...], imp_left[...])
    ends = jnp.concatenate([ends, jnp.zeros((T - 2 * NV, T), f32)], axis=0)
    side_new = jnp.transpose(ends)
    sea, sea_side = near[KEEP_SEA : KEEP_SEA + T, :], near[KEEP_SEA_SIDE : KEEP_SEA_SIDE + T, :]
    coef = near[KEEP_VERT : KEEP_VERT + T, :]
    side_base = near[KEEP_SIDE : KEEP_SIDE + T, :]
    lane = lanes(T)
    copies = []
    for v in range(NV):
        pull = relax[0, v]

        def relaxed(base, wet, new, pull=pull):
            return base + pull * wet * (new - base)

        ends = []
        for k, new in enumerate((imp_top, imp_bottom)):
            at = KEEP_ENDS + 8 * k
            ends.append(
                relaxed(near[at + v : at + v + 1, :], near[at + NV : at + NV + 1, :], new[v : v + 1, :])
            )
        turn = (T - 32 * v) % T
        base = pltpu.roll(side_base, turn, 1) if turn else side_base
        new = pltpu.roll(side_new, T - 2 * v, 1) if v else side_new
        new = jnp.where(lane == 0, new, pltpu.roll(side_new, T - 2 - 2 * v, 1))
        u = relaxed(near[KEEP_BASE + v * T : KEEP_BASE + (v + 1) * T, :], sea, imp[v])
        h = diffuse(u, ends[0], ends[1], relaxed(base, sea_side, new), horiz[0, v])
        one = near[KEEP_ONE + v * T : KEEP_ONE + (v + 1) * T, :]
        stage[v, 0] = relaxed(h + coef * (one - h), sea, imp[v])
        stage[v, 1] = near[KEEP_PART + v * T : KEEP_PART + (v + 1) * T, :] + coef * h
        copies.append(
            pltpu.make_async_copy(stage.at[v], out.at[0, v, pl.ds(0, 2)], sems.at[v])
        )
        copies[-1].start()
    for copy in copies:
        copy.wait()


def final(horiz, relax, mid, keep, imp, imp_rows, imp_cols):
    return pl.pallas_call(
        final_kernel,
        in_specs=[SMEM, SMEM, HBM] + [VMEM] * 6,
        out_specs=HBM,
        out_shape=jax.ShapeDtypeStruct(mid.shape, f32),
        input_output_aliases={2: 0},
        scratch_shapes=[
            pltpu.VMEM((NV, 2, T, T), f32),
            pltpu.SemaphoreType.DMA((NV,)),
        ],
        compiler_params=params(6 * MIB),
        cost_estimate=cost(2 << 20, 3 << 20),
        name="final",
    )(horiz, relax, mid, keep, imp, *imp_rows, *imp_cols)


def shifted(block, axis, by):
    count = lax.axis_size(axis)
    return lax.ppermute(block, axis, [(i, (i + by) % count) for i in range(count)])


def crossed(block, gx_by=0, gy_by=0):
    size = lax.axis_size("gx"), lax.axis_size("gy")
    route = []
    for c in range(2):
        for i in range(size[0]):
            for j in range(size[1]):
                to = (i + gx_by) % size[0], ((j ^ MIRROR) + gy_by) % size[1]
                route.append(((c * size[0] + i) * size[1] + j, ((1 - c) * size[0] + to[0]) * size[1] + to[1]))
    return lax.ppermute(block, ("comp", "gx", "gy"), route)


def local(
    state, horiz_coef, vert_coef, couple_rate, sea_mask, dest_block, entry_count, remap_weight
):
    head, tail = outer_rows(state, vert_coef, sea_mask)
    top, bottom = shifted(tail, "gx", 1), shifted(head, "gx", -1)
    dest = dest_block.reshape(T, FAN).T
    sent = remap(dest, entry_count.reshape(1, T), state, remap_weight, head)
    packed = lax.all_to_all(
        sent.reshape(PEERS, SLOTS, NV, T), ("gx", "gy"), split_axis=0, concat_axis=0, tiled=True
    )
    cols, tile, coef, sea = outer_columns(state, vert_coef, sea_mask, sent)
    cols = with_corners(cols, top, bottom)
    left, right = shifted(cols, "gy", 1), shifted(cols, "gy", -1)
    inner = inner_step(horiz_coef, tile, coef, cols)
    new, first, last, sides = unpack(
        packed.reshape(PEERS * SLOTS * NV, T), left, right, inner
    )
    imp = crossed(new)
    imp_rows = crossed(last, gx_by=1), crossed(first, gx_by=-1)
    imp_cols = crossed(sides, gy_by=1), crossed(sides, gy_by=-1)
    mid, keep = second_step(
        horiz_coef, inner, coef, sea, head, tail, cols, top, bottom, left, right, new
    )
    return final(horiz_coef, couple_rate, mid, keep, imp, imp_rows, imp_cols)


def solution(mesh):
    in_specs = (
        P("comp", None, None, "gx", "gy"),
        P("comp", None),
        P("comp", "gx", "gy"),
        P("comp", None),
        P("comp", "gx", "gy"),
        P("comp", "gx", "gy", None),
        P("comp", "gx", "gy"),
        P("comp", "gx", "gy", None, None, None),
    )
    out_specs = P("comp", None, None, "gx", "gy")
    return jax.shard_map(local, mesh=mesh, in_specs=in_specs, out_specs=out_specs, check_vma=False)
```

```python
import jax
import jax.numpy as jnp
from jax import lax
from jax.experimental import pallas as pl
from jax.experimental.pallas import tpu as pltpu
from jax.sharding import PartitionSpec as P

NV = 4
LEV = 16
PLANES = NV * LEV
T = 128
FAN = 4
CAP = 8
PEERS = 64
SLOTS = CAP + 1
HALF = 64
CHUNKS = 16
MIRROR = 4
MIB = 1024 * 1024
LIMIT = 58 * MIB
ROW_VERT = 2 * PLANES
ROW_SEA = ROW_VERT + 8
ROW_SIZE = ROW_SEA + 8
COL_NEXT = T
COL_COEF = 2 * T
COL_TOP = 3 * T
COL_BOTTOM = COL_TOP + 8
COL_SIZE = COL_BOTTOM + 8
KEEP_BASE = 0
KEEP_ONE = NV * T
KEEP_PART = 2 * NV * T
KEEP_VERT = 3 * NV * T
KEEP_SEA = KEEP_VERT + T
KEEP_SIDE = KEEP_SEA + T
KEEP_SEA_SIDE = KEEP_SIDE + T
KEEP_ENDS = KEEP_SEA_SIDE + T
KEEP_SIZE = KEEP_ENDS + 16

f32 = jnp.float32
i32 = jnp.int32
bf16 = jnp.bfloat16

SMEM = pl.BlockSpec(memory_space=pltpu.SMEM)
VMEM = pl.BlockSpec(memory_space=pltpu.VMEM)
HBM = pl.BlockSpec(memory_space=pl.ANY)


def params(limit=LIMIT):
    return pltpu.CompilerParams(vmem_limit_bytes=limit)


def cost(flops, size):
    return pl.CostEstimate(flops=flops, bytes_accessed=size, transcendentals=0)


def lanes(rows):
    return lax.broadcasted_iota(i32, (rows, T), 1)


def subl(rows):
    return lax.broadcasted_iota(i32, (rows, T), 0)


def inside(flip=0):
    gx, gy = lax.axis_index("gx"), lax.axis_index("gy") ^ flip
    one = lambda test: jnp.where(test, 1.0, 0.0).astype(f32)
    return (
        one(gx > 0),
        one(gx < lax.axis_size("gx") - 1),
        one(gy > 0),
        one(gy < lax.axis_size("gy") - 1),
    )


def column_keep(rows, flip=0):
    _, _, before, after = inside(flip)
    return jnp.where((lanes(rows) & 1) == 0, after, before)


def run(copies):
    for copy in copies:
        copy.start()
    for copy in copies:
        copy.wait()


def row_kernel(state, vert, mask, head, tail, high, low, coef, sea, sems):
    ends = pl.ds(0, 8), pl.ds(T - 8, 8)
    copies = []
    for k, buffer in enumerate((high, low)):
        copies.append(pltpu.make_async_copy(state.at[0, :, :, ends[k]], buffer, sems.at[3 * k]))
        copies.append(pltpu.make_async_copy(vert.at[0, ends[k]], coef.at[k], sems.at[3 * k + 1]))
        copies.append(pltpu.make_async_copy(mask.at[0, ends[k]], sea.at[k], sems.at[3 * k + 2]))
    run(copies)
    up, down, _, _ = inside()
    for k, (out, buffer, keep) in enumerate(((head, high, up), (tail, low, down))):
        outer, following = (0, 1) if k == 0 else (7, 6)
        for p in range(PLANES):
            v, l = divmod(p, LEV)
            out[p : p + 1, :] = buffer[v, l, outer : outer + 1, :] * keep
            out[PLANES + p : PLANES + p + 1, :] = buffer[v, l, following : following + 1, :] * keep
        line = coef[k, outer : outer + 1, :] * keep
        out[ROW_VERT : ROW_VERT + 8, :] = jnp.broadcast_to(line, (8, T))
        line = sea[k, outer : outer + 1, :].astype(f32) * keep
        out[ROW_SEA : ROW_SEA + 8, :] = jnp.broadcast_to(line, (8, T))


def outer_rows(state, vert, mask):
    return pl.pallas_call(
        row_kernel,
        in_specs=[HBM, HBM, HBM],
        out_specs=[VMEM, VMEM],
        out_shape=[jax.ShapeDtypeStruct((ROW_SIZE, T), f32)] * 2,
        scratch_shapes=[
            pltpu.VMEM((NV, LEV, 8, T), f32),
            pltpu.VMEM((NV, LEV, 8, T), f32),
            pltpu.VMEM((2, 8, T), f32),
            pltpu.VMEM((2, 8, T), i32),
            pltpu.SemaphoreType.DMA((6,)),
        ],
        compiler_params=params(),
        cost_estimate=cost(1 << 16, 1 << 19),
        name="outer_rows",
    )(state, vert, mask)


def column_kernel(state, vert, mask, cols, surf, tile, coef, wet, sea, sems):
    loads = [pltpu.make_async_copy(state.at[0, v], tile.at[v], sems.at[v]) for v in range(NV)]
    loads.append(pltpu.make_async_copy(vert.at[0], coef, sems.at[NV]))
    loads.append(pltpu.make_async_copy(mask.at[0], sea, sems.at[NV + 1]))
    for load in loads:
        load.start()
    lane = lanes(HALF)
    keep = column_keep(HALF)
    for v in range(NV):
        loads[v].wait()
        surf[pl.ds(v, T, stride=NV), :] = tile[v, 0]
        for lo in range(0, T, HALF):
            outer, following = pl.ds(lo, HALF), pl.ds(COL_NEXT + lo, HALF)
            acc = jnp.zeros((HALF, T), f32) if v == 0 else cols[outer, :]
            acc2 = jnp.zeros((HALF, T), f32) if v == 0 else cols[following, :]
            for l in range(LEV):
                p = v * LEV + l
                plane = tile[v, l, lo : lo + HALF, :]
                acc = jnp.where((lane >> 1) == p, pltpu.roll(plane, (2 * p + 1) % T, 1), acc)
                hit = (lane == 2 * p) | (lane == (2 * p + 3) % T)
                acc2 = jnp.where(hit, pltpu.roll(plane, (2 * p + 2) % T, 1), acc2)
            last = v == NV - 1
            cols[outer, :] = acc * keep if last else acc
            cols[following, :] = acc2 * keep if last else acc2
    loads[NV].wait()
    loads[NV + 1].wait()
    lane = lanes(T)
    wet[...] = sea[...].astype(f32)
    pair = jnp.where(lane < 2, pltpu.roll(coef[...], 1, 1), pltpu.roll(wet[...], 3, 1))
    cols[COL_COEF : COL_COEF + T, :] = pair * column_keep(T)


def outer_columns(state, vert, mask):
    square = jax.ShapeDtypeStruct((T, T), f32)
    return pl.pallas_call(
        column_kernel,
        in_specs=[HBM, HBM, HBM],
        out_specs=[VMEM] * 5,
        out_shape=[
            jax.ShapeDtypeStruct((COL_TOP, T), f32),
            jax.ShapeDtypeStruct((T * NV, T), f32),
            jax.ShapeDtypeStruct((NV, LEV, T, T), f32),
            square,
            square,
        ],
        scratch_shapes=[pltpu.VMEM((T, T), i32), pltpu.SemaphoreType.DMA((NV + 2,))],
        compiler_params=params(47 * MIB),
        cost_estimate=cost(6 << 20, 9 << 20),
        name="outer_columns",
    )(state, vert, mask)


def corner_kernel(cols, top, bottom, out):
    out[0:COL_COEF, :] = cols[0:COL_COEF, :]
    lane, sub = lanes(PLANES), subl(PLANES)
    keep = column_keep(PLANES)
    for k, rows in enumerate((top, bottom)):
        line = rows[0:PLANES, :]
        at = COL_COEF + k * PLANES
        out[at : at + PLANES, :] = jnp.where(
            (lane == 4) | (lane == 5), pltpu.roll(line, 5, 1) * keep, cols[at : at + PLANES, :]
        )
        first = jnp.broadcast_to(line[:, 0:1], (PLANES, T))
        last = jnp.broadcast_to(line[:, T - 1 : T], (PLANES, T))
        spread = jnp.where(lane == 2 * sub, last, jnp.where(lane == 2 * sub + 1, first, 0.0))
        total = jnp.sum(spread * keep, axis=0, keepdims=True)
        at = COL_TOP + 8 * k
        out[at : at + 8, :] = jnp.broadcast_to(total, (8, T))


def with_corners(cols, top, bottom):
    return pl.pallas_call(
        corner_kernel,
        in_specs=[VMEM] * 3,
        out_specs=VMEM,
        out_shape=jax.ShapeDtypeStruct((COL_SIZE, T), f32),
        compiler_params=params(4 * MIB),
        cost_estimate=cost(1 << 16, 1 << 18),
        name="with_corners",
    )(cols, top, bottom)


def remap_kernel(dest_in, count_in, surf, weight, after, out, blocks, dest, count, used, label, sems):
    del after
    rows = T // CHUNKS
    lists = [
        pltpu.make_async_copy(dest_in, dest, sems.at[CHUNKS]),
        pltpu.make_async_copy(count_in, count, sems.at[CHUNKS + 1]),
    ]
    for copy in lists:
        copy.start()

    def fetch(c):
        piece = pl.ds(c * rows, rows)
        return pltpu.make_async_copy(weight.at[0, piece, 0], blocks.at[piece], sems.at[c])

    for c in range(CHUNKS):
        fetch(c).start()
    out[...] = jnp.zeros_like(out)

    def clear(i, _):
        used[i] = 0
        for k in range(CAP):
            label[i * CAP + k] = 0
        return 0

    lax.fori_loop(0, PEERS, clear, 0)
    for copy in lists:
        copy.wait()
    sub = subl(8)

    def slot_of(row, f):
        target = dest[f, row]
        peer = (lax.shift_right_logical(target, 7) & (PEERS - 1)) ^ MIRROR
        live = f < count[0, row]
        at = used[peer]
        used[peer] = at + jnp.where(live, 1, 0)
        label[jnp.where(live, peer * CAP + at, PEERS * CAP)] = (target & (T - 1)) + 1
        return jnp.where(live, peer * SLOTS + at, CAP)

    def chunk(c, _):
        fetch(c).wait()
        for r in range(0, rows, 2):
            row = c * rows + r
            slots = [[slot_of(row + q, f) for f in range(FAN)] for q in range(2)]
            pair = surf[pl.ds(pl.multiple_of(row * NV, 8), 8), :]
            pair = jnp.concatenate(
                [jnp.where(sub < NV, pair, 0.0), jnp.where(sub >= NV, pair, 0.0)], axis=1
            ).astype(bf16)
            for f in range(0, FAN, 2):
                block = jnp.concatenate(
                    [
                        jnp.concatenate([blocks[row + q, f], blocks[row + q, f + 1]], axis=1)
                        for q in range(2)
                    ],
                    axis=0,
                )
                product = jnp.dot(pair, block, preferred_element_type=f32)
                for q in range(2):
                    for g in range(2):
                        part = product[q * NV : (q + 1) * NV, g * T : (g + 1) * T]
                        out[slots[q][f + g]] = part
        return 0

    lax.fori_loop(0, CHUNKS, chunk, 0)
    me = lax.axis_index("gx") * lax.axis_size("gy") + lax.axis_index("gy")
    place = lax.broadcasted_iota(i32, (NV, T), 0) * T + lax.broadcasted_iota(i32, (NV, T), 1)
    place = place - me * CAP

    def write(i, _):
        block = jnp.zeros((NV, T), i32)
        for k in range(CAP):
            block = jnp.where(place == k, label[i * CAP + k], block)
        out[i * SLOTS + CAP] = block.astype(f32)
        return 0

    lax.fori_loop(0, PEERS, write, 0)


def remap(dest, count, surf, weight, after):
    return pl.pallas_call(
        remap_kernel,
        in_specs=[HBM, HBM, VMEM, HBM, HBM],
        out_specs=VMEM,
        out_shape=jax.ShapeDtypeStruct((PEERS * SLOTS, NV, T), f32),
        scratch_shapes=[
            pltpu.VMEM((T, FAN, T, T), bf16),
            pltpu.SMEM((FAN, T), i32),
            pltpu.SMEM((1, T), i32),
            pltpu.SMEM((PEERS,), i32),
            pltpu.SMEM((PEERS * CAP + 8,), i32),
            pltpu.SemaphoreType.DMA((CHUNKS + 2,)),
        ],
        compiler_params=params(44 * MIB),
        cost_estimate=cost(67 << 20, 20 << 20),
        name="remap",
    )(dest, count, surf, weight, after)


def sealed(block, *after):
    def kernel(*refs):
        del refs

    return pl.pallas_call(
        kernel,
        in_specs=[HBM] * (1 + len(after)),
        out_specs=HBM,
        out_shape=jax.ShapeDtypeStruct(block.shape, block.dtype),
        input_output_aliases={0: 0},
        compiler_params=params(MIB),
        name="sealed",
    )(block, *after)


def merged(left, right, back=2):
    return jnp.where((lanes(left.shape[0]) & 1) == 0, left, pltpu.roll(right, T - back, 1))


def diffuse(u, up, down, side, rate):
    rows = u.shape[0]
    lane, sub = lanes(rows), subl(rows)
    north = jnp.where(sub == 0, up, pltpu.roll(u, 1, 0))
    south = jnp.where(sub == rows - 1, down, pltpu.roll(u, rows - 1, 0))
    west = jnp.where(lane == 0, side, pltpu.roll(u, 1, 1))
    east = jnp.where(lane == T - 1, side, pltpu.roll(u, T - 1, 1))
    return u + rate * ((north + south) + (west + east) - 4.0 * u)


def level_diffuse(u, top, bottom, side, rate, l, lo):
    up = top[l : l + 1, :] if lo == 0 else u[l, lo - 1 : lo, :]
    down = bottom[l : l + 1, :] if lo + HALF == T else u[l, lo + HALF : lo + HALF + 1, :]
    spin = side[lo : lo + HALF, :]
    if l:
        spin = pltpu.roll(spin, T - 2 * l, 1)
    return diffuse(u[l, lo : lo + HALF, :], up, down, spin, rate)


def halo_columns(rate, left, right, own):
    lane, sub = lanes(T), subl(T)
    here = merged(left[0:T, :], right[0:T, :])
    outer = merged(left[COL_NEXT : COL_NEXT + T, :], right[COL_NEXT : COL_NEXT + T, :], 4)
    inner = pltpu.roll(own[0:T, :], T - 1, 1)
    ends = [merged(left[at : at + 8, :], right[at : at + 8, :])[0:1, :] for at in (COL_TOP, COL_BOTTOM)]
    north = jnp.where(sub == 0, ends[0], pltpu.roll(here, 1, 0))
    south = jnp.where(sub == T - 1, ends[1], pltpu.roll(here, T - 1, 0))
    plane = ((lane + 1) >> 1) & (PLANES - 1)
    number = jnp.full((T, T), rate[0, 0], f32)
    for v in range(1, NV):
        number = jnp.where(plane // LEV == v, rate[0, v], number)
    h = here + number * ((north + south) + (outer + inner) - 4.0 * here)
    coef = jnp.where(
        (lane & 1) == 0,
        jnp.broadcast_to(left[COL_COEF : COL_COEF + T, 0:1], (T, T)),
        jnp.broadcast_to(right[COL_COEF : COL_COEF + T, 1:2], (T, T)),
    )
    level = plane % LEV
    above = jnp.where(level < LEV - 1, pltpu.roll(h, T - 2, 1) - h, 0.0)
    below = jnp.where(level > 0, pltpu.roll(h, 2, 1) - h, 0.0)
    return here, h + coef * (above + below)


def halo_rows(rate, rows, own, left, right, k, v):
    at = v * LEV
    lane, level = lanes(LEV), subl(LEV)
    here = rows[at : at + LEV, :]
    corner = COL_COEF + k * PLANES + at
    west = jnp.where(
        lane == 0, pltpu.roll(left[corner : corner + LEV, :], T - 4, 1), pltpu.roll(here, 1, 1)
    )
    east = jnp.where(
        lane == T - 1,
        pltpu.roll(right[corner : corner + LEV, :], T - 6, 1),
        pltpu.roll(here, T - 1, 1),
    )
    outer = rows[PLANES + at : PLANES + at + LEV, :]
    inner = own[at : at + LEV, :]
    h = here + rate[0, v] * ((outer + inner) + (west + east) - 4.0 * here)
    above = jnp.where(level < LEV - 1, pltpu.roll(h, LEV - 1, 0) - h, 0.0)
    below = jnp.where(level > 0, pltpu.roll(h, 1, 0) - h, 0.0)
    return h + rows[ROW_VERT : ROW_VERT + 1, :] * (above + below)


def step_kernel(
    rate, u, coef, sea, own, top, bottom, near, far,
    out, keep, w, stage, inner, top1, bottom1, top2, bottom2, side1, side2, turned, sems,
):
    def emit(v):
        levels = pl.ds(2, LEV - 2)
        return pltpu.make_async_copy(stage.at[v], out.at[0, v, levels], sems.at[v])

    up, down, _, _ = inside()
    side1[...], side2[...] = halo_columns(rate, near, far, own)
    for v in range(NV):
        at = v * LEV
        for l in range(LEV):
            inner[0, at + l : at + l + 1, :] = u[v, l, 0:1, :] * up
            inner[1, at + l : at + l + 1, :] = u[v, l, T - 1 : T, :] * down
    for v in range(NV):
        at = v * LEV
        top1[v] = top[at : at + LEV, :]
        bottom1[v] = bottom[at : at + LEV, :]
        top2[v] = halo_rows(rate, top, inner.at[0], near, far, 0, v)
        bottom2[v] = halo_rows(rate, bottom, inner.at[1], near, far, 1, v)

    def first(v, _):
        number = rate[0, v]
        turned[...] = pltpu.roll(side1[...], lax.rem((NV - v) * 32, T), 1)
        source, result = u.at[v], w.at[v]
        for lo in range(0, T, HALF):
            mix = coef[lo : lo + HALF, :]
            at = lambda l: level_diffuse(source, top1.at[v], bottom1.at[v], turned, number, l, lo)
            before, here = None, at(0)
            for l in range(LEV):
                after = at(l + 1) if l + 1 < LEV else None
                if before is None:
                    term = after - here
                elif after is None:
                    term = before - here
                else:
                    term = (after - here) + (before - here)
                result[l, lo : lo + HALF, :] = here + mix * term
                before, here = here, after
        return 0

    lax.fori_loop(0, NV, first, 0)

    def second(v, _):
        number = rate[0, v]
        turned[...] = pltpu.roll(side2[...], lax.rem((NV - v) * 32, T), 1)
        source, result = w.at[v], stage.at[v]
        for lo in range(0, T, HALF):
            mix = coef[lo : lo + HALF, :]
            at = lambda l: level_diffuse(source, top2.at[v], bottom2.at[v], turned, number, l, lo)
            before, here = at(1), at(2)
            row = pl.multiple_of(v * T + lo, 8)
            keep[pl.ds(KEEP_BASE + row, HALF), :] = source[0, lo : lo + HALF, :]
            keep[pl.ds(KEEP_ONE + row, HALF), :] = before
            keep[pl.ds(KEEP_PART + row, HALF), :] = before + mix * ((here - before) - before)
            for l in range(2, LEV):
                after = at(l + 1) if l + 1 < LEV else None
                term = before - here
                if after is not None:
                    term = (after - here) + term
                result[l - 2, lo : lo + HALF, :] = here + mix * term
                before, here = here, after
        emit(v).start()
        return 0

    lax.fori_loop(0, NV, second, 0)
    keep[KEEP_VERT : KEEP_VERT + T, :] = coef[...]
    keep[KEEP_SEA : KEEP_SEA + T, :] = sea[...]
    keep[KEEP_SIDE : KEEP_SIDE + T, :] = side2[...]
    coefs = pl.ds(COL_COEF, T)
    keep[KEEP_SEA_SIDE : KEEP_SEA_SIDE + T, :] = jnp.where(
        lanes(T) == 0, pltpu.roll(near[coefs, :], T - 2, 1), pltpu.roll(far[coefs, :], T - 4, 1)
    )
    for k, (rows, line) in enumerate(((top2, top), (bottom2, bottom))):
        for v in range(NV):
            keep[KEEP_ENDS + 8 * k + v : KEEP_ENDS + 8 * k + v + 1, :] = rows[v, 0:1, :]
        keep[KEEP_ENDS + 8 * k + NV : KEEP_ENDS + 8 * k + 8, :] = line[ROW_SEA : ROW_SEA + NV, :]
    for v in range(NV):
        emit(v).wait()


def two_steps(rate, u, coef, sea, own, top, bottom, left, right):
    rows = pltpu.VMEM((NV, LEV, T), f32)
    square = pltpu.VMEM((T, T), f32)
    return pl.pallas_call(
        step_kernel,
        in_specs=[SMEM] + [VMEM] * 8,
        out_specs=[HBM, VMEM],
        out_shape=[
            jax.ShapeDtypeStruct((1,) + u.shape, f32),
            jax.ShapeDtypeStruct((KEEP_SIZE, T), f32),
        ],
        scratch_shapes=[
            pltpu.VMEM((NV, LEV, T, T), f32),
            pltpu.VMEM((NV, LEV - 2, T, T), f32),
            pltpu.VMEM((2, PLANES, T), f32),
            rows,
            rows,
            rows,
            rows,
            square,
            square,
            square,
            pltpu.SemaphoreType.DMA((NV,)),
        ],
        compiler_params=params(16 * MIB),
        cost_estimate=cost(48 << 20, 10 << 20),
        name="two_steps",
    )(rate, u, coef, sea, own, top, bottom, left, right)


def unpack_kernel(data, after, imp, first, last, cols):
    del after
    size = SLOTS * NV
    sub = subl(T).astype(f32) + 1.0
    picks = []
    for j in range(NV):
        table = jnp.sum(data[pl.ds(CAP * NV + j, PEERS, stride=size), :], axis=0, keepdims=True)
        picks.append((sub == table).astype(bf16))
    pick = jnp.concatenate(picks, axis=1)
    lane = lanes(T)
    up, down, _, _ = inside()
    acc = jnp.zeros((T, T), f32)
    for v in range(NV):
        block = jnp.concatenate(
            [data[pl.ds(s * size + v, CAP, stride=NV), :] for s in range(PEERS)], axis=0
        )
        high = block.astype(bf16)
        low = (block - high.astype(f32)).astype(bf16)
        total = jnp.dot(pick, high, preferred_element_type=f32)
        total = total + jnp.dot(pick, low, preferred_element_type=f32)
        imp[v] = total
        for out, row, keep in ((first, 0, up), (last, T - 1, down)):
            out[v : v + 1, :] = total[row : row + 1, :] * keep
            out[NV + v : NV + v + 1, :] = total[row : row + 1, :] * keep
        acc = jnp.where((lane >> 1) == v, pltpu.roll(total, 2 * v + 1, 1), acc)
    cols[...] = jnp.transpose(acc * column_keep(T, MIRROR))[0 : 2 * NV, :]


def unpack(data, after):
    return pl.pallas_call(
        unpack_kernel,
        in_specs=[VMEM, HBM],
        out_specs=[VMEM] * 4,
        out_shape=[
            jax.ShapeDtypeStruct((NV, T, T), f32),
            jax.ShapeDtypeStruct((2 * NV, T), f32),
            jax.ShapeDtypeStruct((2 * NV, T), f32),
            jax.ShapeDtypeStruct((2 * NV, T), f32),
        ],
        compiler_params=params(12 * MIB),
        cost_estimate=cost(200 << 20, 2 << 20),
        name="unpack",
    )(data, after)


def final_kernel(
    horiz, relax, mid, near, imp, imp_top, imp_bottom, imp_left, imp_right, out, stage, sems
):
    del mid
    odd = (subl(2 * NV) & 1) == 1
    ends = jnp.where(odd, imp_right[...], imp_left[...])
    ends = jnp.concatenate([ends, jnp.zeros((T - 2 * NV, T), f32)], axis=0)
    side_new = jnp.transpose(ends)
    sea, sea_side = near[KEEP_SEA : KEEP_SEA + T, :], near[KEEP_SEA_SIDE : KEEP_SEA_SIDE + T, :]
    coef = near[KEEP_VERT : KEEP_VERT + T, :]
    side_base = near[KEEP_SIDE : KEEP_SIDE + T, :]
    lane = lanes(T)
    copies = []
    for v in range(NV):
        pull = relax[0, v]

        def relaxed(base, wet, new, pull=pull):
            return base + pull * wet * (new - base)

        ends = []
        for k, new in enumerate((imp_top, imp_bottom)):
            at = KEEP_ENDS + 8 * k
            ends.append(
                relaxed(near[at + v : at + v + 1, :], near[at + NV : at + NV + 1, :], new[v : v + 1, :])
            )
        turn = (T - 32 * v) % T
        base = pltpu.roll(side_base, turn, 1) if turn else side_base
        new = pltpu.roll(side_new, T - 2 * v, 1) if v else side_new
        new = jnp.where(lane == 0, new, pltpu.roll(side_new, T - 2 - 2 * v, 1))
        u = relaxed(near[KEEP_BASE + v * T : KEEP_BASE + (v + 1) * T, :], sea, imp[v])
        h = diffuse(u, ends[0], ends[1], relaxed(base, sea_side, new), horiz[0, v])
        one = near[KEEP_ONE + v * T : KEEP_ONE + (v + 1) * T, :]
        stage[v, 0] = relaxed(h + coef * (one - h), sea, imp[v])
        stage[v, 1] = near[KEEP_PART + v * T : KEEP_PART + (v + 1) * T, :] + coef * h
        copies.append(
            pltpu.make_async_copy(stage.at[v], out.at[0, v, pl.ds(0, 2)], sems.at[v])
        )
        copies[-1].start()
    for copy in copies:
        copy.wait()


def final(horiz, relax, mid, keep, imp, imp_rows, imp_cols):
    return pl.pallas_call(
        final_kernel,
        in_specs=[SMEM, SMEM, HBM] + [VMEM] * 6,
        out_specs=HBM,
        out_shape=jax.ShapeDtypeStruct(mid.shape, f32),
        input_output_aliases={2: 0},
        scratch_shapes=[
            pltpu.VMEM((NV, 2, T, T), f32),
            pltpu.SemaphoreType.DMA((NV,)),
        ],
        compiler_params=params(6 * MIB),
        cost_estimate=cost(2 << 20, 3 << 20),
        name="final",
    )(horiz, relax, mid, keep, imp, *imp_rows, *imp_cols)


def shifted(block, axis, by):
    count = lax.axis_size(axis)
    return lax.ppermute(block, axis, [(i, (i + by) % count) for i in range(count)])


def crossed(block, gx_by=0, gy_by=0):
    size = lax.axis_size("gx"), lax.axis_size("gy")
    route = []
    for c in range(2):
        for i in range(size[0]):
            for j in range(size[1]):
                to = (i + gx_by) % size[0], ((j ^ MIRROR) + gy_by) % size[1]
                route.append(((c * size[0] + i) * size[1] + j, ((1 - c) * size[0] + to[0]) * size[1] + to[1]))
    return lax.ppermute(block, ("comp", "gx", "gy"), route)


def local(
    state, horiz_coef, vert_coef, couple_rate, sea_mask, dest_block, entry_count, remap_weight
):
    head, tail = outer_rows(state, vert_coef, sea_mask)
    top, bottom = shifted(tail, "gx", 1), shifted(head, "gx", -1)
    cols, surf, tile, coef, sea = outer_columns(state, vert_coef, sea_mask)
    cols = with_corners(cols, top, bottom)
    left, right = shifted(cols, "gy", 1), shifted(cols, "gy", -1)
    dest = dest_block.reshape(T, FAN).T
    packed = remap(dest, entry_count.reshape(1, T), surf, remap_weight, cols)
    packed = sealed(packed, left, right).reshape(PEERS, SLOTS, NV, T)
    packed = lax.all_to_all(packed, ("gx", "gy"), split_axis=0, concat_axis=0, tiled=True)
    mid, keep = two_steps(horiz_coef, tile, coef, sea, cols, top, bottom, left, right)
    new, first, last, sides = unpack(packed.reshape(PEERS * SLOTS * NV, T), keep)
    imp = crossed(new)
    imp_rows = crossed(last, gx_by=1), crossed(first, gx_by=-1)
    imp_cols = crossed(sides, gy_by=1), crossed(sides, gy_by=-1)
    return final(horiz_coef, couple_rate, mid, keep, imp, imp_rows, imp_cols)


def solution(mesh):
    in_specs = (
        P("comp", None, None, "gx", "gy"),
        P("comp", None),
        P("comp", "gx", "gy"),
        P("comp", None),
        P("comp", "gx", "gy"),
        P("comp", "gx", "gy", None),
        P("comp", "gx", "gy"),
        P("comp", "gx", "gy", None, None, None),
    )
    out_specs = P("comp", None, None, "gx", "gy")
    return jax.shard_map(local, mesh=mesh, in_specs=in_specs, out_specs=out_specs, check_vma=False)
```

```python
import jax
import jax.numpy as jnp
from jax import lax
from jax.experimental import pallas as pl
from jax.experimental.pallas import tpu as pltpu
from jax.sharding import PartitionSpec as P

NV = 4
LEV = 16
PLANES = NV * LEV
T = 128
FAN = 4
CAP = 8
PEERS = 64
SLOTS = CAP + 1
HALF = 64
CHUNKS = 16
MIRROR = 4
MIB = 1024 * 1024
LIMIT = 58 * MIB
ROW_VERT = 2 * PLANES
ROW_SEA = ROW_VERT + 8
ROW_SIZE = ROW_SEA + 8
COL_NEXT = T
COL_COEF = 2 * T
COL_TOP = 3 * T
COL_BOTTOM = COL_TOP + 8
COL_SIZE = COL_BOTTOM + 8
KEEP_BASE = 0
KEEP_ONE = NV * T
KEEP_PART = 2 * NV * T
KEEP_VERT = 3 * NV * T
KEEP_SEA = KEEP_VERT + T
KEEP_SIDE = KEEP_SEA + T
KEEP_SEA_SIDE = KEEP_SIDE + T
KEEP_ENDS = KEEP_SEA_SIDE + T
KEEP_SIZE = KEEP_ENDS + 16

f32 = jnp.float32
i32 = jnp.int32
bf16 = jnp.bfloat16

SMEM = pl.BlockSpec(memory_space=pltpu.SMEM)
VMEM = pl.BlockSpec(memory_space=pltpu.VMEM)
HBM = pl.BlockSpec(memory_space=pl.ANY)


def params(limit=LIMIT):
    return pltpu.CompilerParams(vmem_limit_bytes=limit)


def cost(flops, size):
    return pl.CostEstimate(flops=flops, bytes_accessed=size, transcendentals=0)


def lanes(rows):
    return lax.broadcasted_iota(i32, (rows, T), 1)


def subl(rows):
    return lax.broadcasted_iota(i32, (rows, T), 0)


def inside(flip=0):
    gx, gy = lax.axis_index("gx"), lax.axis_index("gy") ^ flip
    one = lambda test: jnp.where(test, 1.0, 0.0).astype(f32)
    return (
        one(gx > 0),
        one(gx < lax.axis_size("gx") - 1),
        one(gy > 0),
        one(gy < lax.axis_size("gy") - 1),
    )


def column_keep(rows, flip=0):
    _, _, before, after = inside(flip)
    return jnp.where((lanes(rows) & 1) == 0, after, before)


def run(copies):
    for copy in copies:
        copy.start()
    for copy in copies:
        copy.wait()


def row_kernel(state, vert, mask, head, tail, high, low, coef, sea, sems):
    ends = pl.ds(0, 8), pl.ds(T - 8, 8)
    copies = []
    for k, buffer in enumerate((high, low)):
        copies.append(pltpu.make_async_copy(state.at[0, :, :, ends[k]], buffer, sems.at[3 * k]))
        copies.append(pltpu.make_async_copy(vert.at[0, ends[k]], coef.at[k], sems.at[3 * k + 1]))
        copies.append(pltpu.make_async_copy(mask.at[0, ends[k]], sea.at[k], sems.at[3 * k + 2]))
    run(copies)
    up, down, _, _ = inside()
    for k, (out, buffer, keep) in enumerate(((head, high, up), (tail, low, down))):
        outer, following = (0, 1) if k == 0 else (7, 6)
        for p in range(PLANES):
            v, l = divmod(p, LEV)
            out[p : p + 1, :] = buffer[v, l, outer : outer + 1, :] * keep
            out[PLANES + p : PLANES + p + 1, :] = buffer[v, l, following : following + 1, :] * keep
        line = coef[k, outer : outer + 1, :] * keep
        out[ROW_VERT : ROW_VERT + 8, :] = jnp.broadcast_to(line, (8, T))
        line = sea[k, outer : outer + 1, :].astype(f32) * keep
        out[ROW_SEA : ROW_SEA + 8, :] = jnp.broadcast_to(line, (8, T))


def outer_rows(state, vert, mask):
    return pl.pallas_call(
        row_kernel,
        in_specs=[HBM, HBM, HBM],
        out_specs=[VMEM, VMEM],
        out_shape=[jax.ShapeDtypeStruct((ROW_SIZE, T), f32)] * 2,
        scratch_shapes=[
            pltpu.VMEM((NV, LEV, 8, T), f32),
            pltpu.VMEM((NV, LEV, 8, T), f32),
            pltpu.VMEM((2, 8, T), f32),
            pltpu.VMEM((2, 8, T), i32),
            pltpu.SemaphoreType.DMA((6,)),
        ],
        compiler_params=params(),
        cost_estimate=cost(1 << 16, 1 << 19),
        name="outer_rows",
    )(state, vert, mask)


def column_kernel(state, vert, mask, cols, surf, coef, wet, tile, sea, sems):
    loads = [pltpu.make_async_copy(state.at[0, v], tile.at[v], sems.at[v]) for v in range(NV)]
    loads.append(pltpu.make_async_copy(vert.at[0], coef, sems.at[NV]))
    loads.append(pltpu.make_async_copy(mask.at[0], sea, sems.at[NV + 1]))
    for load in loads:
        load.start()
    lane = lanes(HALF)
    keep = column_keep(HALF)
    for v in range(NV):
        loads[v].wait()
        surf[pl.ds(v, T, stride=NV), :] = tile[v, 0]
        for lo in range(0, T, HALF):
            outer, following = pl.ds(lo, HALF), pl.ds(COL_NEXT + lo, HALF)
            acc = jnp.zeros((HALF, T), f32) if v == 0 else cols[outer, :]
            acc2 = jnp.zeros((HALF, T), f32) if v == 0 else cols[following, :]
            for l in range(LEV):
                p = v * LEV + l
                plane = tile[v, l, lo : lo + HALF, :]
                acc = jnp.where((lane >> 1) == p, pltpu.roll(plane, (2 * p + 1) % T, 1), acc)
                hit = (lane == 2 * p) | (lane == (2 * p + 3) % T)
                acc2 = jnp.where(hit, pltpu.roll(plane, (2 * p + 2) % T, 1), acc2)
            last = v == NV - 1
            cols[outer, :] = acc * keep if last else acc
            cols[following, :] = acc2 * keep if last else acc2
    loads[NV].wait()
    loads[NV + 1].wait()
    lane = lanes(T)
    wet[...] = sea[...].astype(f32)
    pair = jnp.where(lane < 2, pltpu.roll(coef[...], 1, 1), pltpu.roll(wet[...], 3, 1))
    cols[COL_COEF : COL_COEF + T, :] = pair * column_keep(T)


def outer_columns(state, vert, mask):
    square = jax.ShapeDtypeStruct((T, T), f32)
    return pl.pallas_call(
        column_kernel,
        in_specs=[HBM, HBM, HBM],
        out_specs=[VMEM] * 4,
        out_shape=[
            jax.ShapeDtypeStruct((COL_TOP, T), f32),
            jax.ShapeDtypeStruct((T * NV, T), f32),
            square,
            square,
        ],
        scratch_shapes=[
            pltpu.VMEM((NV, LEV, T, T), f32),
            pltpu.VMEM((T, T), i32),
            pltpu.SemaphoreType.DMA((NV + 2,)),
        ],
        compiler_params=params(51 * MIB),
        cost_estimate=cost(6 << 20, 9 << 20),
        name="outer_columns",
    )(state, vert, mask)


def corner_kernel(cols, top, bottom, out):
    out[0:COL_COEF, :] = cols[0:COL_COEF, :]
    lane, sub = lanes(PLANES), subl(PLANES)
    keep = column_keep(PLANES)
    for k, rows in enumerate((top, bottom)):
        line = rows[0:PLANES, :]
        at = COL_COEF + k * PLANES
        out[at : at + PLANES, :] = jnp.where(
            (lane == 4) | (lane == 5), pltpu.roll(line, 5, 1) * keep, cols[at : at + PLANES, :]
        )
        first = jnp.broadcast_to(line[:, 0:1], (PLANES, T))
        last = jnp.broadcast_to(line[:, T - 1 : T], (PLANES, T))
        spread = jnp.where(lane == 2 * sub, last, jnp.where(lane == 2 * sub + 1, first, 0.0))
        total = jnp.sum(spread * keep, axis=0, keepdims=True)
        at = COL_TOP + 8 * k
        out[at : at + 8, :] = jnp.broadcast_to(total, (8, T))


def with_corners(cols, top, bottom):
    return pl.pallas_call(
        corner_kernel,
        in_specs=[VMEM] * 3,
        out_specs=VMEM,
        out_shape=jax.ShapeDtypeStruct((COL_SIZE, T), f32),
        compiler_params=params(4 * MIB),
        cost_estimate=cost(1 << 16, 1 << 18),
        name="with_corners",
    )(cols, top, bottom)


def remap_kernel(dest_in, count_in, surf, weight, after, out, blocks, dest, count, used, label, sems):
    del after
    rows = T // CHUNKS
    lists = [
        pltpu.make_async_copy(dest_in, dest, sems.at[CHUNKS]),
        pltpu.make_async_copy(count_in, count, sems.at[CHUNKS + 1]),
    ]
    for copy in lists:
        copy.start()

    def fetch(c):
        piece = pl.ds(c * rows, rows)
        return pltpu.make_async_copy(weight.at[0, piece, 0], blocks.at[piece], sems.at[c])

    for c in range(CHUNKS):
        fetch(c).start()
    out[...] = jnp.zeros_like(out)

    def clear(i, _):
        used[i] = 0
        for k in range(CAP):
            label[i * CAP + k] = 0
        return 0

    lax.fori_loop(0, PEERS, clear, 0)
    for copy in lists:
        copy.wait()
    sub = subl(8)

    def slot_of(row, f):
        target = dest[f, row]
        device = (lax.shift_right_logical(target, 7) & (PEERS - 1)) ^ MIRROR
        peer = (device & 7) * 8 + (device >> 3)
        live = f < count[0, row]
        at = used[peer]
        used[peer] = at + jnp.where(live, 1, 0)
        label[jnp.where(live, peer * CAP + at, PEERS * CAP)] = (target & (T - 1)) + 1
        return jnp.where(live, peer * SLOTS + at, CAP)

    def chunk(c, _):
        fetch(c).wait()
        for r in range(0, rows, 2):
            row = c * rows + r
            slots = [[slot_of(row + q, f) for f in range(FAN)] for q in range(2)]
            pair = surf[pl.ds(pl.multiple_of(row * NV, 8), 8), :]
            pair = jnp.concatenate(
                [jnp.where(sub < NV, pair, 0.0), jnp.where(sub >= NV, pair, 0.0)], axis=1
            ).astype(bf16)
            for f in range(0, FAN, 2):
                block = jnp.concatenate(
                    [
                        jnp.concatenate([blocks[row + q, f], blocks[row + q, f + 1]], axis=1)
                        for q in range(2)
                    ],
                    axis=0,
                )
                product = jnp.dot(pair, block, preferred_element_type=f32)
                for q in range(2):
                    for g in range(2):
                        part = product[q * NV : (q + 1) * NV, g * T : (g + 1) * T]
                        out[slots[q][f + g]] = part
        return 0

    lax.fori_loop(0, CHUNKS, chunk, 0)
    me = lax.axis_index("gy") * lax.axis_size("gx") + lax.axis_index("gx")
    place = lax.broadcasted_iota(i32, (NV, T), 0) * T + lax.broadcasted_iota(i32, (NV, T), 1)
    place = place - me * CAP

    def write(i, _):
        block = jnp.zeros((NV, T), i32)
        for k in range(CAP):
            block = jnp.where(place == k, label[i * CAP + k], block)
        out[i * SLOTS + CAP] = block.astype(f32)
        return 0

    lax.fori_loop(0, PEERS, write, 0)


def remap(dest, count, surf, weight, after):
    return pl.pallas_call(
        remap_kernel,
        in_specs=[HBM, HBM, VMEM, HBM, HBM],
        out_specs=VMEM,
        out_shape=jax.ShapeDtypeStruct((PEERS * SLOTS, NV, T), f32),
        scratch_shapes=[
            pltpu.VMEM((T, FAN, T, T), bf16),
            pltpu.SMEM((FAN, T), i32),
            pltpu.SMEM((1, T), i32),
            pltpu.SMEM((PEERS,), i32),
            pltpu.SMEM((PEERS * CAP + 8,), i32),
            pltpu.SemaphoreType.DMA((CHUNKS + 2,)),
        ],
        compiler_params=params(44 * MIB),
        cost_estimate=cost(67 << 20, 20 << 20),
        name="remap",
    )(dest, count, surf, weight, after)


def sealed(block, *after):
    def kernel(*refs):
        del refs

    return pl.pallas_call(
        kernel,
        in_specs=[HBM] * (1 + len(after)),
        out_specs=HBM,
        out_shape=jax.ShapeDtypeStruct(block.shape, block.dtype),
        input_output_aliases={0: 0},
        compiler_params=params(MIB),
        name="sealed",
    )(block, *after)


def merged(left, right, back=2):
    return jnp.where((lanes(left.shape[0]) & 1) == 0, left, pltpu.roll(right, T - back, 1))


def diffuse(u, up, down, side, rate):
    rows = u.shape[0]
    lane, sub = lanes(rows), subl(rows)
    north = jnp.where(sub == 0, up, pltpu.roll(u, 1, 0))
    south = jnp.where(sub == rows - 1, down, pltpu.roll(u, rows - 1, 0))
    west = jnp.where(lane == 0, side, pltpu.roll(u, 1, 1))
    east = jnp.where(lane == T - 1, side, pltpu.roll(u, T - 1, 1))
    return u + rate * ((north + south) + (west + east) - 4.0 * u)


def level_diffuse(u, top, bottom, side, rate, l, lo):
    up = top[l : l + 1, :] if lo == 0 else u[l, lo - 1 : lo, :]
    down = bottom[l : l + 1, :] if lo + HALF == T else u[l, lo + HALF : lo + HALF + 1, :]
    spin = side[lo : lo + HALF, :]
    if l:
        spin = pltpu.roll(spin, T - 2 * l, 1)
    return diffuse(u[l, lo : lo + HALF, :], up, down, spin, rate)


def halo_columns(rate, left, right, own):
    lane, sub = lanes(T), subl(T)
    here = merged(left[0:T, :], right[0:T, :])
    outer = merged(left[COL_NEXT : COL_NEXT + T, :], right[COL_NEXT : COL_NEXT + T, :], 4)
    inner = pltpu.roll(own[0:T, :], T - 1, 1)
    ends = [merged(left[at : at + 8, :], right[at : at + 8, :])[0:1, :] for at in (COL_TOP, COL_BOTTOM)]
    north = jnp.where(sub == 0, ends[0], pltpu.roll(here, 1, 0))
    south = jnp.where(sub == T - 1, ends[1], pltpu.roll(here, T - 1, 0))
    plane = ((lane + 1) >> 1) & (PLANES - 1)
    number = jnp.full((T, T), rate[0, 0], f32)
    for v in range(1, NV):
        number = jnp.where(plane // LEV == v, rate[0, v], number)
    h = here + number * ((north + south) + (outer + inner) - 4.0 * here)
    coef = jnp.where(
        (lane & 1) == 0,
        jnp.broadcast_to(left[COL_COEF : COL_COEF + T, 0:1], (T, T)),
        jnp.broadcast_to(right[COL_COEF : COL_COEF + T, 1:2], (T, T)),
    )
    level = plane % LEV
    above = jnp.where(level < LEV - 1, pltpu.roll(h, T - 2, 1) - h, 0.0)
    below = jnp.where(level > 0, pltpu.roll(h, 2, 1) - h, 0.0)
    return here, h + coef * (above + below)


def halo_rows(rate, rows, own, left, right, k, v):
    at = v * LEV
    lane, level = lanes(LEV), subl(LEV)
    here = rows[at : at + LEV, :]
    corner = COL_COEF + k * PLANES + at
    west = jnp.where(
        lane == 0, pltpu.roll(left[corner : corner + LEV, :], T - 4, 1), pltpu.roll(here, 1, 1)
    )
    east = jnp.where(
        lane == T - 1,
        pltpu.roll(right[corner : corner + LEV, :], T - 6, 1),
        pltpu.roll(here, T - 1, 1),
    )
    outer = rows[PLANES + at : PLANES + at + LEV, :]
    inner = own[at : at + LEV, :]
    h = here + rate[0, v] * ((outer + inner) + (west + east) - 4.0 * here)
    above = jnp.where(level < LEV - 1, pltpu.roll(h, LEV - 1, 0) - h, 0.0)
    below = jnp.where(level > 0, pltpu.roll(h, 1, 0) - h, 0.0)
    return h + rows[ROW_VERT : ROW_VERT + 1, :] * (above + below)


def step_kernel(
    rate, state, coef, sea, own, top, bottom, near, far,
    out, keep, u, w, stage, inner, top1, bottom1, top2, bottom2, side1, side2, turned, sems,
):
    def emit(v):
        levels = pl.ds(2, LEV - 2)
        return pltpu.make_async_copy(stage.at[v], out.at[0, v, levels], sems.at[v])

    loads = [pltpu.make_async_copy(state.at[0, v], u.at[v], sems.at[v]) for v in range(NV)]
    for load in loads:
        load.start()
    up, down, _, _ = inside()
    side1[...], side2[...] = halo_columns(rate, near, far, own)
    for v in range(NV):
        loads[v].wait()
        at = v * LEV
        for l in range(LEV):
            inner[0, at + l : at + l + 1, :] = u[v, l, 0:1, :] * up
            inner[1, at + l : at + l + 1, :] = u[v, l, T - 1 : T, :] * down
    for v in range(NV):
        at = v * LEV
        top1[v] = top[at : at + LEV, :]
        bottom1[v] = bottom[at : at + LEV, :]
        top2[v] = halo_rows(rate, top, inner.at[0], near, far, 0, v)
        bottom2[v] = halo_rows(rate, bottom, inner.at[1], near, far, 1, v)

    def first(v, _):
        number = rate[0, v]
        turned[...] = pltpu.roll(side1[...], lax.rem((NV - v) * 32, T), 1)
        source, result = u.at[v], w.at[v]
        for lo in range(0, T, HALF):
            mix = coef[lo : lo + HALF, :]
            at = lambda l: level_diffuse(source, top1.at[v], bottom1.at[v], turned, number, l, lo)
            before, here = None, at(0)
            for l in range(LEV):
                after = at(l + 1) if l + 1 < LEV else None
                if before is None:
                    term = after - here
                elif after is None:
                    term = before - here
                else:
                    term = (after - here) + (before - here)
                result[l, lo : lo + HALF, :] = here + mix * term
                before, here = here, after
        return 0

    lax.fori_loop(0, NV, first, 0)

    def second(v, _):
        number = rate[0, v]
        turned[...] = pltpu.roll(side2[...], lax.rem((NV - v) * 32, T), 1)
        source, result = w.at[v], stage.at[v]
        for lo in range(0, T, HALF):
            mix = coef[lo : lo + HALF, :]
            at = lambda l: level_diffuse(source, top2.at[v], bottom2.at[v], turned, number, l, lo)
            before, here = at(1), at(2)
            row = pl.multiple_of(v * T + lo, 8)
            keep[pl.ds(KEEP_BASE + row, HALF), :] = source[0, lo : lo + HALF, :]
            keep[pl.ds(KEEP_ONE + row, HALF), :] = before
            keep[pl.ds(KEEP_PART + row, HALF), :] = before + mix * ((here - before) - before)
            for l in range(2, LEV):
                after = at(l + 1) if l + 1 < LEV else None
                term = before - here
                if after is not None:
                    term = (after - here) + term
                result[l - 2, lo : lo + HALF, :] = here + mix * term
                before, here = here, after
        emit(v).start()
        return 0

    lax.fori_loop(0, NV, second, 0)
    keep[KEEP_VERT : KEEP_VERT + T, :] = coef[...]
    keep[KEEP_SEA : KEEP_SEA + T, :] = sea[...]
    keep[KEEP_SIDE : KEEP_SIDE + T, :] = side2[...]
    coefs = pl.ds(COL_COEF, T)
    keep[KEEP_SEA_SIDE : KEEP_SEA_SIDE + T, :] = jnp.where(
        lanes(T) == 0, pltpu.roll(near[coefs, :], T - 2, 1), pltpu.roll(far[coefs, :], T - 4, 1)
    )
    for k, (rows, line) in enumerate(((top2, top), (bottom2, bottom))):
        for v in range(NV):
            keep[KEEP_ENDS + 8 * k + v : KEEP_ENDS + 8 * k + v + 1, :] = rows[v, 0:1, :]
        keep[KEEP_ENDS + 8 * k + NV : KEEP_ENDS + 8 * k + 8, :] = line[ROW_SEA : ROW_SEA + NV, :]
    for v in range(NV):
        emit(v).wait()


def two_steps(rate, state, coef, sea, own, top, bottom, left, right):
    rows = pltpu.VMEM((NV, LEV, T), f32)
    square = pltpu.VMEM((T, T), f32)
    return pl.pallas_call(
        step_kernel,
        in_specs=[SMEM, HBM] + [VMEM] * 7,
        out_specs=[HBM, VMEM],
        out_shape=[
            jax.ShapeDtypeStruct(state.shape, f32),
            jax.ShapeDtypeStruct((KEEP_SIZE, T), f32),
        ],
        scratch_shapes=[
            pltpu.VMEM((NV, LEV, T, T), f32),
            pltpu.VMEM((NV, LEV, T, T), f32),
            pltpu.VMEM((NV, LEV - 2, T, T), f32),
            pltpu.VMEM((2, PLANES, T), f32),
            rows,
            rows,
            rows,
            rows,
            square,
            square,
            square,
            pltpu.SemaphoreType.DMA((NV,)),
        ],
        compiler_params=params(20 * MIB),
        cost_estimate=cost(48 << 20, 10 << 20),
        name="two_steps",
    )(rate, state, coef, sea, own, top, bottom, left, right)


def unpack_kernel(data, after, imp, first, last, cols):
    del after
    size = SLOTS * NV
    sub = subl(T).astype(f32) + 1.0
    picks = []
    for j in range(NV):
        table = jnp.sum(data[pl.ds(CAP * NV + j, PEERS, stride=size), :], axis=0, keepdims=True)
        picks.append((sub == table).astype(bf16))
    pick = jnp.concatenate(picks, axis=1)
    lane = lanes(T)
    up, down, _, _ = inside()
    acc = jnp.zeros((T, T), f32)
    for v in range(NV):
        block = jnp.concatenate(
            [data[pl.ds(s * size + v, CAP, stride=NV), :] for s in range(PEERS)], axis=0
        )
        high = block.astype(bf16)
        low = (block - high.astype(f32)).astype(bf16)
        total = jnp.dot(pick, high, preferred_element_type=f32)
        total = total + jnp.dot(pick, low, preferred_element_type=f32)
        imp[v] = total
        for out, row, keep in ((first, 0, up), (last, T - 1, down)):
            out[v : v + 1, :] = total[row : row + 1, :] * keep
            out[NV + v : NV + v + 1, :] = total[row : row + 1, :] * keep
        acc = jnp.where((lane >> 1) == v, pltpu.roll(total, 2 * v + 1, 1), acc)
    cols[...] = jnp.transpose(acc * column_keep(T, MIRROR))[0 : 2 * NV, :]


def unpack(data, after):
    return pl.pallas_call(
        unpack_kernel,
        in_specs=[VMEM, HBM],
        out_specs=[VMEM] * 4,
        out_shape=[
            jax.ShapeDtypeStruct((NV, T, T), f32),
            jax.ShapeDtypeStruct((2 * NV, T), f32),
            jax.ShapeDtypeStruct((2 * NV, T), f32),
            jax.ShapeDtypeStruct((2 * NV, T), f32),
        ],
        compiler_params=params(12 * MIB),
        cost_estimate=cost(200 << 20, 2 << 20),
        name="unpack",
    )(data, after)


def final_kernel(
    horiz, relax, mid, near, imp, imp_top, imp_bottom, imp_left, imp_right, out, stage, sems
):
    del mid
    odd = (subl(2 * NV) & 1) == 1
    ends = jnp.where(odd, imp_right[...], imp_left[...])
    ends = jnp.concatenate([ends, jnp.zeros((T - 2 * NV, T), f32)], axis=0)
    side_new = jnp.transpose(ends)
    sea, sea_side = near[KEEP_SEA : KEEP_SEA + T, :], near[KEEP_SEA_SIDE : KEEP_SEA_SIDE + T, :]
    coef = near[KEEP_VERT : KEEP_VERT + T, :]
    side_base = near[KEEP_SIDE : KEEP_SIDE + T, :]
    lane = lanes(T)
    copies = []
    for v in range(NV):
        pull = relax[0, v]

        def relaxed(base, wet, new, pull=pull):
            return base + pull * wet * (new - base)

        ends = []
        for k, new in enumerate((imp_top, imp_bottom)):
            at = KEEP_ENDS + 8 * k
            ends.append(
                relaxed(near[at + v : at + v + 1, :], near[at + NV : at + NV + 1, :], new[v : v + 1, :])
            )
        turn = (T - 32 * v) % T
        base = pltpu.roll(side_base, turn, 1) if turn else side_base
        new = pltpu.roll(side_new, T - 2 * v, 1) if v else side_new
        new = jnp.where(lane == 0, new, pltpu.roll(side_new, T - 2 - 2 * v, 1))
        u = relaxed(near[KEEP_BASE + v * T : KEEP_BASE + (v + 1) * T, :], sea, imp[v])
        h = diffuse(u, ends[0], ends[1], relaxed(base, sea_side, new), horiz[0, v])
        one = near[KEEP_ONE + v * T : KEEP_ONE + (v + 1) * T, :]
        stage[v, 0] = relaxed(h + coef * (one - h), sea, imp[v])
        stage[v, 1] = near[KEEP_PART + v * T : KEEP_PART + (v + 1) * T, :] + coef * h
        copies.append(
            pltpu.make_async_copy(stage.at[v], out.at[0, v, pl.ds(0, 2)], sems.at[v])
        )
        copies[-1].start()
    for copy in copies:
        copy.wait()


def final(horiz, relax, mid, keep, imp, imp_rows, imp_cols):
    return pl.pallas_call(
        final_kernel,
        in_specs=[SMEM, SMEM, HBM] + [VMEM] * 6,
        out_specs=HBM,
        out_shape=jax.ShapeDtypeStruct(mid.shape, f32),
        input_output_aliases={2: 0},
        scratch_shapes=[
            pltpu.VMEM((NV, 2, T, T), f32),
            pltpu.SemaphoreType.DMA((NV,)),
        ],
        compiler_params=params(6 * MIB),
        cost_estimate=cost(2 << 20, 3 << 20),
        name="final",
    )(horiz, relax, mid, keep, imp, *imp_rows, *imp_cols)


def shifted(block, axis, by):
    count = lax.axis_size(axis)
    return lax.ppermute(block, axis, [(i, (i + by) % count) for i in range(count)])


def crossed(block, gx_by=0, gy_by=0):
    size = lax.axis_size("gx"), lax.axis_size("gy")
    route = []
    for c in range(2):
        for i in range(size[0]):
            for j in range(size[1]):
                to = (i + gx_by) % size[0], ((j ^ MIRROR) + gy_by) % size[1]
                route.append(((c * size[0] + i) * size[1] + j, ((1 - c) * size[0] + to[0]) * size[1] + to[1]))
    return lax.ppermute(block, ("comp", "gx", "gy"), route)


def local(
    state, horiz_coef, vert_coef, couple_rate, sea_mask, dest_block, entry_count, remap_weight
):
    head, tail = outer_rows(state, vert_coef, sea_mask)
    top, bottom = shifted(tail, "gx", 1), shifted(head, "gx", -1)
    cols, surf, coef, sea = outer_columns(state, vert_coef, sea_mask)
    cols = with_corners(cols, top, bottom)
    left, right = shifted(cols, "gy", 1), shifted(cols, "gy", -1)
    dest = dest_block.reshape(T, FAN).T
    packed = remap(dest, entry_count.reshape(1, T), surf, remap_weight, cols)
    packed = sealed(packed, left, right).reshape(PEERS, SLOTS, NV, T)
    packed = lax.all_to_all(packed, ("gy", "gx"), split_axis=0, concat_axis=0, tiled=True)
    mid, keep = two_steps(horiz_coef, state, coef, sea, cols, top, bottom, left, right)
    new, first, last, sides = unpack(packed.reshape(PEERS * SLOTS * NV, T), keep)
    imp = crossed(new)
    imp_rows = crossed(last, gx_by=1), crossed(first, gx_by=-1)
    imp_cols = crossed(sides, gy_by=1), crossed(sides, gy_by=-1)
    return final(horiz_coef, couple_rate, mid, keep, imp, imp_rows, imp_cols)


def solution(mesh):
    in_specs = (
        P("comp", None, None, "gx", "gy"),
        P("comp", None),
        P("comp", "gx", "gy"),
        P("comp", None),
        P("comp", "gx", "gy"),
        P("comp", "gx", "gy", None),
        P("comp", "gx", "gy"),
        P("comp", "gx", "gy", None, None, None),
    )
    out_specs = P("comp", None, None, "gx", "gy")
    return jax.shard_map(local, mesh=mesh, in_specs=in_specs, out_specs=out_specs, check_vma=False)
```

```python
import jax
import jax.numpy as jnp
from jax import lax
from jax.experimental import pallas as pl
from jax.experimental.pallas import tpu as pltpu
from jax.sharding import PartitionSpec as P

NV = 4
LEV = 16
PLANES = NV * LEV
T = 128
FAN = 4
CAP = 8
PEERS = 64
SIZE = CAP * NV + 1
EDGE = 32
HALF = 64
CHUNKS = 16
MIRROR = 4
MIB = 1024 * 1024
LIMIT = 58 * MIB
ROW_VERT = 2 * PLANES
ROW_SEA = ROW_VERT + 8
ROW_SIZE = ROW_SEA + 8
COL_NEXT = T
COL_COEF = 2 * T
COL_TOP = 3 * T
COL_BOTTOM = COL_TOP + 8
COL_SIZE = COL_BOTTOM + 8
KEEP_BASE = 0
KEEP_ONE = NV * T
KEEP_PART = 2 * NV * T
KEEP_VERT = 3 * NV * T
KEEP_SEA = KEEP_VERT + T
KEEP_SIDE = KEEP_SEA + T
KEEP_SEA_SIDE = KEEP_SIDE + T
KEEP_ENDS = KEEP_SEA_SIDE + T
KEEP_SIZE = KEEP_ENDS + 16

f32 = jnp.float32
i32 = jnp.int32
bf16 = jnp.bfloat16

SMEM = pl.BlockSpec(memory_space=pltpu.SMEM)
VMEM = pl.BlockSpec(memory_space=pltpu.VMEM)
HBM = pl.BlockSpec(memory_space=pl.ANY)


def params(limit=LIMIT):
    return pltpu.CompilerParams(vmem_limit_bytes=limit)


def cost(flops, size):
    return pl.CostEstimate(flops=flops, bytes_accessed=size, transcendentals=0)


def lanes(rows):
    return lax.broadcasted_iota(i32, (rows, T), 1)


def subl(rows):
    return lax.broadcasted_iota(i32, (rows, T), 0)


def inside():
    gx, gy = lax.axis_index("gx"), lax.axis_index("gy")
    one = lambda test: jnp.where(test, 1.0, 0.0).astype(f32)
    return (
        one(gx > 0),
        one(gx < lax.axis_size("gx") - 1),
        one(gy > 0),
        one(gy < lax.axis_size("gy") - 1),
    )


def column_keep(rows):
    _, _, before, after = inside()
    return jnp.where((lanes(rows) & 1) == 0, after, before)


def run(copies):
    for copy in copies:
        copy.start()
    for copy in copies:
        copy.wait()


def row_kernel(state, vert, mask, head, tail, high, low, coef, sea, sems):
    ends = pl.ds(0, 8), pl.ds(T - 8, 8)
    copies = []
    for k, buffer in enumerate((high, low)):
        copies.append(pltpu.make_async_copy(state.at[0, :, :, ends[k]], buffer, sems.at[3 * k]))
        copies.append(pltpu.make_async_copy(vert.at[0, ends[k]], coef.at[k], sems.at[3 * k + 1]))
        copies.append(pltpu.make_async_copy(mask.at[0, ends[k]], sea.at[k], sems.at[3 * k + 2]))
    run(copies)
    up, down, _, _ = inside()
    for k, (out, buffer, keep) in enumerate(((head, high, up), (tail, low, down))):
        outer, following = (0, 1) if k == 0 else (7, 6)
        for p in range(PLANES):
            v, l = divmod(p, LEV)
            out[p : p + 1, :] = buffer[v, l, outer : outer + 1, :] * keep
            out[PLANES + p : PLANES + p + 1, :] = buffer[v, l, following : following + 1, :] * keep
        line = coef[k, outer : outer + 1, :] * keep
        out[ROW_VERT : ROW_VERT + 8, :] = jnp.broadcast_to(line, (8, T))
        line = sea[k, outer : outer + 1, :].astype(f32) * keep
        out[ROW_SEA : ROW_SEA + 8, :] = jnp.broadcast_to(line, (8, T))


def outer_rows(state, vert, mask):
    return pl.pallas_call(
        row_kernel,
        in_specs=[HBM, HBM, HBM],
        out_specs=[VMEM, VMEM],
        out_shape=[jax.ShapeDtypeStruct((ROW_SIZE, T), f32)] * 2,
        scratch_shapes=[
            pltpu.VMEM((NV, LEV, 8, T), f32),
            pltpu.VMEM((NV, LEV, 8, T), f32),
            pltpu.VMEM((2, 8, T), f32),
            pltpu.VMEM((2, 8, T), i32),
            pltpu.SemaphoreType.DMA((6,)),
        ],
        compiler_params=params(),
        cost_estimate=cost(1 << 16, 1 << 19),
        name="outer_rows",
    )(state, vert, mask)


def column_kernel(state, vert, mask, cols, surf, coef, wet, tile, sea, sems):
    loads = [pltpu.make_async_copy(state.at[0, v], tile.at[v], sems.at[v]) for v in range(NV)]
    loads.append(pltpu.make_async_copy(vert.at[0], coef, sems.at[NV]))
    loads.append(pltpu.make_async_copy(mask.at[0], sea, sems.at[NV + 1]))
    for load in loads:
        load.start()
    lane = lanes(HALF)
    keep = column_keep(HALF)
    for v in range(NV):
        loads[v].wait()
        surf[pl.ds(v, T, stride=NV), :] = tile[v, 0]
        for lo in range(0, T, HALF):
            outer, following = pl.ds(lo, HALF), pl.ds(COL_NEXT + lo, HALF)
            acc = jnp.zeros((HALF, T), f32) if v == 0 else cols[outer, :]
            acc2 = jnp.zeros((HALF, T), f32) if v == 0 else cols[following, :]
            for l in range(LEV):
                p = v * LEV + l
                plane = tile[v, l, lo : lo + HALF, :]
                acc = jnp.where((lane >> 1) == p, pltpu.roll(plane, (2 * p + 1) % T, 1), acc)
                hit = (lane == 2 * p) | (lane == (2 * p + 3) % T)
                acc2 = jnp.where(hit, pltpu.roll(plane, (2 * p + 2) % T, 1), acc2)
            last = v == NV - 1
            cols[outer, :] = acc * keep if last else acc
            cols[following, :] = acc2 * keep if last else acc2
    loads[NV].wait()
    loads[NV + 1].wait()
    lane = lanes(T)
    wet[...] = sea[...].astype(f32)
    pair = jnp.where(lane < 2, pltpu.roll(coef[...], 1, 1), pltpu.roll(wet[...], 3, 1))
    cols[COL_COEF : COL_COEF + T, :] = pair * column_keep(T)


def outer_columns(state, vert, mask):
    square = jax.ShapeDtypeStruct((T, T), f32)
    return pl.pallas_call(
        column_kernel,
        in_specs=[HBM, HBM, HBM],
        out_specs=[VMEM] * 4,
        out_shape=[
            jax.ShapeDtypeStruct((COL_TOP, T), f32),
            jax.ShapeDtypeStruct((T * NV, T), f32),
            square,
            square,
        ],
        scratch_shapes=[
            pltpu.VMEM((NV, LEV, T, T), f32),
            pltpu.VMEM((T, T), i32),
            pltpu.SemaphoreType.DMA((NV + 2,)),
        ],
        compiler_params=params(51 * MIB),
        cost_estimate=cost(6 << 20, 9 << 20),
        name="outer_columns",
    )(state, vert, mask)


def corner_kernel(cols, top, bottom, out):
    out[0:COL_COEF, :] = cols[0:COL_COEF, :]
    lane, sub = lanes(PLANES), subl(PLANES)
    keep = column_keep(PLANES)
    for k, rows in enumerate((top, bottom)):
        line = rows[0:PLANES, :]
        at = COL_COEF + k * PLANES
        out[at : at + PLANES, :] = jnp.where(
            (lane == 4) | (lane == 5), pltpu.roll(line, 5, 1) * keep, cols[at : at + PLANES, :]
        )
        first = jnp.broadcast_to(line[:, 0:1], (PLANES, T))
        last = jnp.broadcast_to(line[:, T - 1 : T], (PLANES, T))
        spread = jnp.where(lane == 2 * sub, last, jnp.where(lane == 2 * sub + 1, first, 0.0))
        total = jnp.sum(spread * keep, axis=0, keepdims=True)
        at = COL_TOP + 8 * k
        out[at : at + 8, :] = jnp.broadcast_to(total, (8, T))


def with_corners(cols, top, bottom):
    return pl.pallas_call(
        corner_kernel,
        in_specs=[VMEM] * 3,
        out_specs=VMEM,
        out_shape=jax.ShapeDtypeStruct((COL_SIZE, T), f32),
        compiler_params=params(4 * MIB),
        cost_estimate=cost(1 << 16, 1 << 18),
        name="with_corners",
    )(cols, top, bottom)


def remap_kernel(
    dest_in, count_in, surf, weight, after, out, blocks, buffer, names, dest, count, used, label, sems
):
    del after
    rows = T // CHUNKS
    lists = [
        pltpu.make_async_copy(dest_in, dest, sems.at[CHUNKS]),
        pltpu.make_async_copy(count_in, count, sems.at[CHUNKS + 1]),
    ]
    for copy in lists:
        copy.start()

    def fetch(c):
        piece = pl.ds(c * rows, rows)
        return pltpu.make_async_copy(weight.at[0, piece, 0], blocks.at[piece], sems.at[c])

    for c in range(CHUNKS):
        fetch(c).start()
    buffer[...] = jnp.zeros_like(buffer)

    def clear(i, _):
        used[i] = 0
        for k in range(CAP):
            label[i * CAP + k] = 0
        return 0

    lax.fori_loop(0, PEERS, clear, 0)
    for copy in lists:
        copy.wait()
    sub = subl(8)

    def place_of(row, f):
        target = dest[f, row]
        peer = (lax.shift_right_logical(target, 7) & (PEERS - 1)) ^ MIRROR
        live = f < count[0, row]
        at = used[peer]
        used[peer] = at + jnp.where(live, 1, 0)
        label[jnp.where(live, peer * CAP + at, PEERS * CAP)] = (target & (T - 1)) + 1
        return jnp.where(live, peer * SIZE + at * NV, PEERS * SIZE)

    def chunk(c, _):
        fetch(c).wait()
        for r in range(0, rows, 2):
            row = c * rows + r
            places = [[place_of(row + q, f) for f in range(FAN)] for q in range(2)]
            pair = surf[pl.ds(pl.multiple_of(row * NV, 8), 8), :]
            pair = jnp.concatenate(
                [jnp.where(sub < NV, pair, 0.0), jnp.where(sub >= NV, pair, 0.0)], axis=1
            ).astype(bf16)
            for f in range(0, FAN, 2):
                block = jnp.concatenate(
                    [
                        jnp.concatenate([blocks[row + q, f], blocks[row + q, f + 1]], axis=1)
                        for q in range(2)
                    ],
                    axis=0,
                )
                product = jnp.dot(pair, block, preferred_element_type=f32)
                for q in range(2):
                    for g in range(2):
                        part = product[q * NV : (q + 1) * NV, g * T : (g + 1) * T]
                        buffer[pl.ds(places[q][f + g], NV), :] = part
        return 0

    lax.fori_loop(0, CHUNKS, chunk, 0)
    lane = lanes(1)

    def name(i, _):
        line = jnp.zeros((1, T), i32)
        for k in range(CAP):
            line = jnp.where(lane == k, label[i * CAP + k], line)
        names[pl.ds(i, 1), :] = line.astype(f32)
        return 0

    lax.fori_loop(0, PEERS, name, 0)
    lane = lanes(PEERS)
    rims = jnp.zeros((PEERS, T), f32)
    for j in range(CAP * NV):
        column = EDGE + 2 * j
        turned = pltpu.roll(buffer[pl.ds(j, PEERS, stride=SIZE), :], (column + 1) % T, 1)
        rims = jnp.where((lane >> 1) == column >> 1, turned, rims)
    lane, sub = lanes(8), subl(8)
    left_end, right_end = sub == MIRROR, sub == MIRROR - 1
    for b in range(PEERS // 8):
        own, rim = names[b * 8 : b * 8 + 8, :], rims[b * 8 : b * 8 + 8, :]
        left_name, left_rim = (jnp.where(left_end, 0.0, pltpu.roll(x, 1, 0)) for x in (own, rim))
        right_name, right_rim = (jnp.where(right_end, 0.0, pltpu.roll(x, 7, 0)) for x in (own, rim))
        line = own + pltpu.roll(left_name, CAP, 1) + pltpu.roll(right_name, 2 * CAP, 1)
        line = line + jnp.where((lane & 1) == 0, left_rim, right_rim)
        buffer[pl.ds(b * 8 * SIZE + SIZE - 1, 8, stride=SIZE), :] = line
    run([pltpu.make_async_copy(buffer.at[pl.ds(0, PEERS * SIZE)], out, sems.at[0])])


def remap(dest, count, surf, weight, after):
    return pl.pallas_call(
        remap_kernel,
        in_specs=[HBM, HBM, VMEM, HBM, HBM],
        out_specs=HBM,
        out_shape=jax.ShapeDtypeStruct((PEERS * SIZE, T), f32),
        scratch_shapes=[
            pltpu.VMEM((T, FAN, T, T), bf16),
            pltpu.VMEM((PEERS * SIZE + 8, T), f32),
            pltpu.VMEM((PEERS, T), f32),
            pltpu.SMEM((FAN, T), i32),
            pltpu.SMEM((1, T), i32),
            pltpu.SMEM((PEERS,), i32),
            pltpu.SMEM((PEERS * CAP + 8,), i32),
            pltpu.SemaphoreType.DMA((CHUNKS + 2,)),
        ],
        compiler_params=params(44 * MIB),
        cost_estimate=cost(67 << 20, 20 << 20),
        name="remap",
    )(dest, count, surf, weight, after)


def sealed(block, *after):
    def kernel(*refs):
        del refs

    return pl.pallas_call(
        kernel,
        in_specs=[HBM] * (1 + len(after)),
        out_specs=HBM,
        out_shape=jax.ShapeDtypeStruct(block.shape, block.dtype),
        input_output_aliases={0: 0},
        compiler_params=params(MIB),
        name="sealed",
    )(block, *after)


def merged(left, right, back=2):
    return jnp.where((lanes(left.shape[0]) & 1) == 0, left, pltpu.roll(right, T - back, 1))


def diffuse(u, up, down, side, rate):
    rows = u.shape[0]
    lane, sub = lanes(rows), subl(rows)
    north = jnp.where(sub == 0, up, pltpu.roll(u, 1, 0))
    south = jnp.where(sub == rows - 1, down, pltpu.roll(u, rows - 1, 0))
    west = jnp.where(lane == 0, side, pltpu.roll(u, 1, 1))
    east = jnp.where(lane == T - 1, side, pltpu.roll(u, T - 1, 1))
    return u + rate * ((north + south) + (west + east) - 4.0 * u)


def level_diffuse(u, top, bottom, side, rate, l, lo):
    up = top[l : l + 1, :] if lo == 0 else u[l, lo - 1 : lo, :]
    down = bottom[l : l + 1, :] if lo + HALF == T else u[l, lo + HALF : lo + HALF + 1, :]
    spin = side[lo : lo + HALF, :]
    if l:
        spin = pltpu.roll(spin, T - 2 * l, 1)
    return diffuse(u[l, lo : lo + HALF, :], up, down, spin, rate)


def halo_columns(rate, left, right, own):
    lane, sub = lanes(T), subl(T)
    here = merged(left[0:T, :], right[0:T, :])
    outer = merged(left[COL_NEXT : COL_NEXT + T, :], right[COL_NEXT : COL_NEXT + T, :], 4)
    inner = pltpu.roll(own[0:T, :], T - 1, 1)
    ends = [merged(left[at : at + 8, :], right[at : at + 8, :])[0:1, :] for at in (COL_TOP, COL_BOTTOM)]
    north = jnp.where(sub == 0, ends[0], pltpu.roll(here, 1, 0))
    south = jnp.where(sub == T - 1, ends[1], pltpu.roll(here, T - 1, 0))
    plane = ((lane + 1) >> 1) & (PLANES - 1)
    number = jnp.full((T, T), rate[0, 0], f32)
    for v in range(1, NV):
        number = jnp.where(plane // LEV == v, rate[0, v], number)
    h = here + number * ((north + south) + (outer + inner) - 4.0 * here)
    coef = jnp.where(
        (lane & 1) == 0,
        jnp.broadcast_to(left[COL_COEF : COL_COEF + T, 0:1], (T, T)),
        jnp.broadcast_to(right[COL_COEF : COL_COEF + T, 1:2], (T, T)),
    )
    level = plane % LEV
    above = jnp.where(level < LEV - 1, pltpu.roll(h, T - 2, 1) - h, 0.0)
    below = jnp.where(level > 0, pltpu.roll(h, 2, 1) - h, 0.0)
    return here, h + coef * (above + below)


def halo_rows(rate, rows, own, left, right, k, v):
    at = v * LEV
    lane, level = lanes(LEV), subl(LEV)
    here = rows[at : at + LEV, :]
    corner = COL_COEF + k * PLANES + at
    west = jnp.where(
        lane == 0, pltpu.roll(left[corner : corner + LEV, :], T - 4, 1), pltpu.roll(here, 1, 1)
    )
    east = jnp.where(
        lane == T - 1,
        pltpu.roll(right[corner : corner + LEV, :], T - 6, 1),
        pltpu.roll(here, T - 1, 1),
    )
    outer = rows[PLANES + at : PLANES + at + LEV, :]
    inner = own[at : at + LEV, :]
    h = here + rate[0, v] * ((outer + inner) + (west + east) - 4.0 * here)
    above = jnp.where(level < LEV - 1, pltpu.roll(h, LEV - 1, 0) - h, 0.0)
    below = jnp.where(level > 0, pltpu.roll(h, 1, 0) - h, 0.0)
    return h + rows[ROW_VERT : ROW_VERT + 1, :] * (above + below)


def step_kernel(
    rate, state, coef, sea, own, top, bottom, near, far,
    out, keep, u, w, stage, inner, top1, bottom1, top2, bottom2, side1, side2, turned, sems,
):
    def emit(v):
        levels = pl.ds(2, LEV - 2)
        return pltpu.make_async_copy(stage.at[v], out.at[0, v, levels], sems.at[v])

    loads = [pltpu.make_async_copy(state.at[0, v], u.at[v], sems.at[v]) for v in range(NV)]
    for load in loads:
        load.start()
    up, down, _, _ = inside()
    side1[...], side2[...] = halo_columns(rate, near, far, own)
    for v in range(NV):
        loads[v].wait()
        at = v * LEV
        for l in range(LEV):
            inner[0, at + l : at + l + 1, :] = u[v, l, 0:1, :] * up
            inner[1, at + l : at + l + 1, :] = u[v, l, T - 1 : T, :] * down
    for v in range(NV):
        at = v * LEV
        top1[v] = top[at : at + LEV, :]
        bottom1[v] = bottom[at : at + LEV, :]
        top2[v] = halo_rows(rate, top, inner.at[0], near, far, 0, v)
        bottom2[v] = halo_rows(rate, bottom, inner.at[1], near, far, 1, v)

    def first(v, _):
        number = rate[0, v]
        turned[...] = pltpu.roll(side1[...], lax.rem((NV - v) * 32, T), 1)
        source, result = u.at[v], w.at[v]
        for lo in range(0, T, HALF):
            mix = coef[lo : lo + HALF, :]
            at = lambda l: level_diffuse(source, top1.at[v], bottom1.at[v], turned, number, l, lo)
            before, here = None, at(0)
            for l in range(LEV):
                after = at(l + 1) if l + 1 < LEV else None
                if before is None:
                    term = after - here
                elif after is None:
                    term = before - here
                else:
                    term = (after - here) + (before - here)
                result[l, lo : lo + HALF, :] = here + mix * term
                before, here = here, after
        return 0

    lax.fori_loop(0, NV, first, 0)

    def second(v, _):
        number = rate[0, v]
        turned[...] = pltpu.roll(side2[...], lax.rem((NV - v) * 32, T), 1)
        source, result = w.at[v], stage.at[v]
        for lo in range(0, T, HALF):
            mix = coef[lo : lo + HALF, :]
            at = lambda l: level_diffuse(source, top2.at[v], bottom2.at[v], turned, number, l, lo)
            before, here = at(1), at(2)
            row = pl.multiple_of(v * T + lo, 8)
            keep[pl.ds(KEEP_BASE + row, HALF), :] = source[0, lo : lo + HALF, :]
            keep[pl.ds(KEEP_ONE + row, HALF), :] = before
            keep[pl.ds(KEEP_PART + row, HALF), :] = before + mix * ((here - before) - before)
            for l in range(2, LEV):
                after = at(l + 1) if l + 1 < LEV else None
                term = before - here
                if after is not None:
                    term = (after - here) + term
                result[l - 2, lo : lo + HALF, :] = here + mix * term
                before, here = here, after
        emit(v).start()
        return 0

    lax.fori_loop(0, NV, second, 0)
    keep[KEEP_VERT : KEEP_VERT + T, :] = coef[...]
    keep[KEEP_SEA : KEEP_SEA + T, :] = sea[...]
    keep[KEEP_SIDE : KEEP_SIDE + T, :] = side2[...]
    coefs = pl.ds(COL_COEF, T)
    keep[KEEP_SEA_SIDE : KEEP_SEA_SIDE + T, :] = jnp.where(
        lanes(T) == 0, pltpu.roll(near[coefs, :], T - 2, 1), pltpu.roll(far[coefs, :], T - 4, 1)
    )
    for k, (rows, line) in enumerate(((top2, top), (bottom2, bottom))):
        for v in range(NV):
            keep[KEEP_ENDS + 8 * k + v : KEEP_ENDS + 8 * k + v + 1, :] = rows[v, 0:1, :]
        keep[KEEP_ENDS + 8 * k + NV : KEEP_ENDS + 8 * k + 8, :] = line[ROW_SEA : ROW_SEA + NV, :]
    for v in range(NV):
        emit(v).wait()


def two_steps(rate, state, coef, sea, own, top, bottom, left, right):
    rows = pltpu.VMEM((NV, LEV, T), f32)
    square = pltpu.VMEM((T, T), f32)
    return pl.pallas_call(
        step_kernel,
        in_specs=[SMEM, HBM] + [VMEM] * 7,
        out_specs=[HBM, VMEM],
        out_shape=[
            jax.ShapeDtypeStruct(state.shape, f32),
            jax.ShapeDtypeStruct((KEEP_SIZE, T), f32),
        ],
        scratch_shapes=[
            pltpu.VMEM((NV, LEV, T, T), f32),
            pltpu.VMEM((NV, LEV, T, T), f32),
            pltpu.VMEM((NV, LEV - 2, T, T), f32),
            pltpu.VMEM((2, PLANES, T), f32),
            rows,
            rows,
            rows,
            rows,
            square,
            square,
            square,
            pltpu.SemaphoreType.DMA((NV,)),
        ],
        compiler_params=params(20 * MIB),
        cost_estimate=cost(48 << 20, 10 << 20),
        name="two_steps",
    )(rate, state, coef, sea, own, top, bottom, left, right)


def unpack_kernel(data, after, imp, first, last):
    del after
    sub = subl(T).astype(f32) + 1.0
    line = data[pl.ds(SIZE - 1, PEERS, stride=SIZE), :]
    fields = jnp.transpose(jnp.concatenate([line, jnp.zeros((T - PEERS, T), f32)], axis=0))

    def two(at, size):
        return fields[at : at + size, :] + pltpu.roll(fields[at + size : at + 2 * size, :], PEERS, 1)

    def split(x):
        high = x.astype(bf16)
        return high, (x - high.astype(f32)).astype(bf16)

    def picks(at):
        return jnp.concatenate(
            [(sub == two(at + k, 1)).astype(bf16) for k in range(0, CAP, 2)], axis=1
        )

    pick = picks(0)
    up, down, _, _ = inside()
    for v in range(NV):
        block = jnp.concatenate(
            [data[pl.ds(k * NV + v, PEERS, stride=SIZE), :] for k in range(CAP)], axis=0
        )
        high, low = split(block)
        total = jnp.dot(pick, high, preferred_element_type=f32)
        total = total + jnp.dot(pick, low, preferred_element_type=f32)
        imp[v * T : (v + 1) * T, :] = total
        for out, row, keep in ((first, 0, up), (last, T - 1, down)):
            out[v : v + 1, :] = total[row : row + 1, :] * keep
            out[NV + v : NV + v + 1, :] = total[row : row + 1, :] * keep
    rims = jnp.concatenate([two(EDGE + 8 * k, 8) for k in range(0, CAP, 2)], axis=1)
    sides = []
    for at in (CAP, 2 * CAP):
        pick = picks(at)
        high, low = (
            lax.dot_general(part, pick, (((1,), (1,)), ((), ())), preferred_element_type=f32)
            for part in split(rims)
        )
        sides.append(high + low)
    imp[NV * T : NV * T + 8, :] = jnp.where((subl(8) & 1) == 0, sides[0], sides[1])


def unpack(data, after):
    return pl.pallas_call(
        unpack_kernel,
        in_specs=[VMEM, HBM],
        out_specs=[VMEM] * 3,
        out_shape=[
            jax.ShapeDtypeStruct((NV * T + 8, T), f32),
            jax.ShapeDtypeStruct((2 * NV, T), f32),
            jax.ShapeDtypeStruct((2 * NV, T), f32),
        ],
        compiler_params=params(12 * MIB),
        cost_estimate=cost(200 << 20, 2 << 20),
        name="unpack",
    )(data, after)


def final_kernel(
    horiz, relax, mid, near, imp, imp_top, imp_bottom, out, stage, sems
):
    del mid
    ends = jnp.concatenate([imp[NV * T : NV * T + 8, :], jnp.zeros((T - 8, T), f32)], axis=0)
    side_new = jnp.transpose(ends)
    sea, sea_side = near[KEEP_SEA : KEEP_SEA + T, :], near[KEEP_SEA_SIDE : KEEP_SEA_SIDE + T, :]
    coef = near[KEEP_VERT : KEEP_VERT + T, :]
    side_base = near[KEEP_SIDE : KEEP_SIDE + T, :]
    lane = lanes(T)
    copies = []
    for v in range(NV):
        pull = relax[0, v]

        def relaxed(base, wet, new, pull=pull):
            return base + pull * wet * (new - base)

        ends = []
        for k, new in enumerate((imp_top, imp_bottom)):
            at = KEEP_ENDS + 8 * k
            ends.append(
                relaxed(near[at + v : at + v + 1, :], near[at + NV : at + NV + 1, :], new[v : v + 1, :])
            )
        turn = (T - 32 * v) % T
        base = pltpu.roll(side_base, turn, 1) if turn else side_base
        new = pltpu.roll(side_new, T - 2 * v, 1) if v else side_new
        new = jnp.where(lane == 0, new, pltpu.roll(side_new, T - 2 - 2 * v, 1))
        mine = imp[v * T : (v + 1) * T, :]
        u = relaxed(near[KEEP_BASE + v * T : KEEP_BASE + (v + 1) * T, :], sea, mine)
        h = diffuse(u, ends[0], ends[1], relaxed(base, sea_side, new), horiz[0, v])
        one = near[KEEP_ONE + v * T : KEEP_ONE + (v + 1) * T, :]
        stage[v, 0] = relaxed(h + coef * (one - h), sea, mine)
        stage[v, 1] = near[KEEP_PART + v * T : KEEP_PART + (v + 1) * T, :] + coef * h
        copies.append(
            pltpu.make_async_copy(stage.at[v], out.at[0, v, pl.ds(0, 2)], sems.at[v])
        )
        copies[-1].start()
    for copy in copies:
        copy.wait()


def final(horiz, relax, mid, keep, imp, imp_rows):
    return pl.pallas_call(
        final_kernel,
        in_specs=[SMEM, SMEM, HBM] + [VMEM] * 4,
        out_specs=HBM,
        out_shape=jax.ShapeDtypeStruct(mid.shape, f32),
        input_output_aliases={2: 0},
        scratch_shapes=[
            pltpu.VMEM((NV, 2, T, T), f32),
            pltpu.SemaphoreType.DMA((NV,)),
        ],
        compiler_params=params(6 * MIB),
        cost_estimate=cost(2 << 20, 3 << 20),
        name="final",
    )(horiz, relax, mid, keep, imp, *imp_rows)


def shifted(block, axis, by):
    count = lax.axis_size(axis)
    return lax.ppermute(block, axis, [(i, (i + by) % count) for i in range(count)])


def crossed(block, gx_by=0):
    size = lax.axis_size("gx"), lax.axis_size("gy")
    route = []
    for c in range(2):
        for i in range(size[0]):
            for j in range(size[1]):
                to = (1 - c) * size[0] + (i + gx_by) % size[0]
                route.append(((c * size[0] + i) * size[1] + j, to * size[1] + (j ^ MIRROR)))
    return lax.ppermute(block, ("comp", "gx", "gy"), route)


def local(
    state, horiz_coef, vert_coef, couple_rate, sea_mask, dest_block, entry_count, remap_weight
):
    head, tail = outer_rows(state, vert_coef, sea_mask)
    top, bottom = shifted(tail, "gx", 1), shifted(head, "gx", -1)
    cols, surf, coef, sea = outer_columns(state, vert_coef, sea_mask)
    cols = with_corners(cols, top, bottom)
    left, right = shifted(cols, "gy", 1), shifted(cols, "gy", -1)
    dest = dest_block.reshape(T, FAN).T
    packed = remap(dest, entry_count.reshape(1, T), surf, remap_weight, cols)
    packed = sealed(packed, left, right).reshape(PEERS, SIZE, 1, T)
    packed = lax.all_to_all(packed, ("gx", "gy"), split_axis=0, concat_axis=0, tiled=True)
    mid, keep = two_steps(horiz_coef, state, coef, sea, cols, top, bottom, left, right)
    new, first, last = unpack(packed.reshape(PEERS * SIZE, T), keep)
    imp = crossed(new)
    imp_rows = crossed(last, 1), crossed(first, -1)
    return final(horiz_coef, couple_rate, mid, keep, imp, imp_rows)


def solution(mesh):
    in_specs = (
        P("comp", None, None, "gx", "gy"),
        P("comp", None),
        P("comp", "gx", "gy"),
        P("comp", None),
        P("comp", "gx", "gy"),
        P("comp", "gx", "gy", None),
        P("comp", "gx", "gy"),
        P("comp", "gx", "gy", None, None, None),
    )
    out_specs = P("comp", None, None, "gx", "gy")
    return jax.shard_map(local, mesh=mesh, in_specs=in_specs, out_specs=out_specs, check_vma=False)
```

```python
import jax
import jax.numpy as jnp
from jax import lax
from jax.experimental import pallas as pl
from jax.experimental.pallas import tpu as pltpu
from jax.sharding import PartitionSpec as P

NV = 4
LEV = 16
PLANES = NV * LEV
T = 128
FAN = 4
CAP = 8
PEERS = 64
SIZE = CAP * NV + 1
EDGE = 32
HALF = 64
CHUNKS = 16
MIRROR = 4
MIB = 1024 * 1024
LIMIT = 58 * MIB
ROW_VERT = 2 * PLANES
ROW_SEA = ROW_VERT + 8
ROW_SIZE = ROW_SEA + 8
COL_NEXT = T
COL_COEF = 2 * T
COL_TOP = 3 * T
COL_BOTTOM = COL_TOP + 8
COL_SIZE = COL_BOTTOM + 8
KEEP_BASE = 0
KEEP_ONE = NV * T
KEEP_PART = 2 * NV * T
KEEP_VERT = 3 * NV * T
KEEP_SEA = KEEP_VERT + T
KEEP_SIDE = KEEP_SEA + T
KEEP_SEA_SIDE = KEEP_SIDE + T
KEEP_ENDS = KEEP_SEA_SIDE + T
KEEP_SIZE = KEEP_ENDS + 16

f32 = jnp.float32
i32 = jnp.int32
bf16 = jnp.bfloat16

SMEM = pl.BlockSpec(memory_space=pltpu.SMEM)
VMEM = pl.BlockSpec(memory_space=pltpu.VMEM)
HBM = pl.BlockSpec(memory_space=pl.ANY)


def params(limit=LIMIT):
    return pltpu.CompilerParams(vmem_limit_bytes=limit)


def cost(flops, size):
    return pl.CostEstimate(flops=flops, bytes_accessed=size, transcendentals=0)


def lanes(rows):
    return lax.broadcasted_iota(i32, (rows, T), 1)


def subl(rows):
    return lax.broadcasted_iota(i32, (rows, T), 0)


def inside():
    gx, gy = lax.axis_index("gx"), lax.axis_index("gy")
    one = lambda test: jnp.where(test, 1.0, 0.0).astype(f32)
    return (
        one(gx > 0),
        one(gx < lax.axis_size("gx") - 1),
        one(gy > 0),
        one(gy < lax.axis_size("gy") - 1),
    )


def column_keep(rows, later=0):
    _, _, before, after = inside()
    return jnp.where((lanes(rows) & 1) == later, after, before)


def run(copies):
    for copy in copies:
        copy.start()
    for copy in copies:
        copy.wait()


def row_kernel(state, vert, mask, head, tail, high, low, coef, sea, sems):
    ends = pl.ds(0, 8), pl.ds(T - 8, 8)
    copies = []
    for k, buffer in enumerate((high, low)):
        copies.append(pltpu.make_async_copy(state.at[0, :, :, ends[k]], buffer, sems.at[3 * k]))
        copies.append(pltpu.make_async_copy(vert.at[0, ends[k]], coef.at[k], sems.at[3 * k + 1]))
        copies.append(pltpu.make_async_copy(mask.at[0, ends[k]], sea.at[k], sems.at[3 * k + 2]))
    run(copies)
    up, down, _, _ = inside()
    for k, (out, buffer, keep) in enumerate(((head, high, up), (tail, low, down))):
        outer, following = (0, 1) if k == 0 else (7, 6)
        flat = buffer.reshape(PLANES * 8, T)
        out[0:PLANES, :] = flat[pl.ds(outer, PLANES, stride=8), :] * keep
        out[PLANES : 2 * PLANES, :] = flat[pl.ds(following, PLANES, stride=8), :] * keep
        line = coef[k, outer : outer + 1, :] * keep
        out[ROW_VERT : ROW_VERT + 8, :] = jnp.broadcast_to(line, (8, T))
        line = sea[k, outer : outer + 1, :].astype(f32) * keep
        out[ROW_SEA : ROW_SEA + 8, :] = jnp.broadcast_to(line, (8, T))


def outer_rows(state, vert, mask):
    return pl.pallas_call(
        row_kernel,
        in_specs=[HBM, HBM, HBM],
        out_specs=[VMEM, VMEM],
        out_shape=[jax.ShapeDtypeStruct((ROW_SIZE, T), f32)] * 2,
        scratch_shapes=[
            pltpu.VMEM((NV, LEV, 8, T), f32),
            pltpu.VMEM((NV, LEV, 8, T), f32),
            pltpu.VMEM((2, 8, T), f32),
            pltpu.VMEM((2, 8, T), i32),
            pltpu.SemaphoreType.DMA((6,)),
        ],
        compiler_params=params(),
        cost_estimate=cost(1 << 16, 1 << 19),
        name="outer_rows",
    )(state, vert, mask)


def column_kernel(state, vert, mask, cols, surf, coef, wet, tile, sea, sems):
    loads = [pltpu.make_async_copy(state.at[0, v], tile.at[v], sems.at[v]) for v in range(NV)]
    loads.append(pltpu.make_async_copy(vert.at[0], coef, sems.at[NV]))
    loads.append(pltpu.make_async_copy(mask.at[0], sea, sems.at[NV + 1]))
    for load in loads:
        load.start()
    lane = lanes(HALF)
    keep = column_keep(HALF)
    keep2 = column_keep(HALF, 1)
    for v in range(NV):
        loads[v].wait()
        surf[pl.ds(v, T, stride=NV), :] = tile[v, 0]
        for lo in range(0, T, HALF):
            outer, following = pl.ds(lo, HALF), pl.ds(COL_NEXT + lo, HALF)
            acc = jnp.zeros((HALF, T), f32) if v == 0 else cols[outer, :]
            acc2 = jnp.zeros((HALF, T), f32) if v == 0 else cols[following, :]
            for l in range(LEV):
                p = v * LEV + l
                plane = tile[v, l, lo : lo + HALF, :]
                turned = pltpu.roll(plane, (2 * p + 1) % T, 1)
                acc = jnp.where((lane >> 1) == p, turned, acc)
                acc2 = jnp.where((lane == (2 * p - 1) % T) | (lane == (2 * p + 2) % T), turned, acc2)
            last = v == NV - 1
            cols[outer, :] = acc * keep if last else acc
            cols[following, :] = acc2 * keep2 if last else acc2
    loads[NV].wait()
    loads[NV + 1].wait()
    lane = lanes(T)
    wet[...] = sea[...].astype(f32)
    pair = jnp.where(lane < 2, pltpu.roll(coef[...], 1, 1), pltpu.roll(wet[...], 3, 1))
    cols[COL_COEF : COL_COEF + T, :] = pair * column_keep(T)


def outer_columns(state, vert, mask):
    square = jax.ShapeDtypeStruct((T, T), f32)
    return pl.pallas_call(
        column_kernel,
        in_specs=[HBM, HBM, HBM],
        out_specs=[VMEM] * 4,
        out_shape=[
            jax.ShapeDtypeStruct((COL_TOP, T), f32),
            jax.ShapeDtypeStruct((T * NV, T), f32),
            square,
            square,
        ],
        scratch_shapes=[
            pltpu.VMEM((NV, LEV, T, T), f32),
            pltpu.VMEM((T, T), i32),
            pltpu.SemaphoreType.DMA((NV + 2,)),
        ],
        compiler_params=params(51 * MIB),
        cost_estimate=cost(6 << 20, 9 << 20),
        name="outer_columns",
    )(state, vert, mask)


def corner_kernel(cols, top, bottom, out):
    out[0:COL_COEF, :] = cols[0:COL_COEF, :]
    lane, sub = lanes(PLANES), subl(PLANES)
    keep = column_keep(PLANES)
    for k, rows in enumerate((top, bottom)):
        line = rows[0:PLANES, :]
        at = COL_COEF + k * PLANES
        out[at : at + PLANES, :] = jnp.where(
            (lane == 4) | (lane == 5), pltpu.roll(line, 5, 1) * keep, cols[at : at + PLANES, :]
        )
        first = jnp.broadcast_to(line[:, 0:1], (PLANES, T))
        last = jnp.broadcast_to(line[:, T - 1 : T], (PLANES, T))
        spread = jnp.where(lane == 2 * sub, last, jnp.where(lane == 2 * sub + 1, first, 0.0))
        total = jnp.sum(spread * keep, axis=0, keepdims=True)
        at = COL_TOP + 8 * k
        out[at : at + 8, :] = jnp.broadcast_to(total, (8, T))


def with_corners(cols, top, bottom):
    return pl.pallas_call(
        corner_kernel,
        in_specs=[VMEM] * 3,
        out_specs=VMEM,
        out_shape=jax.ShapeDtypeStruct((COL_SIZE, T), f32),
        compiler_params=params(4 * MIB),
        cost_estimate=cost(1 << 16, 1 << 18),
        name="with_corners",
    )(cols, top, bottom)


def remap_kernel(
    dest_in, count_in, surf, weight, after, out, blocks, buffer, names, dest, count, used, label, sems
):
    del after
    rows = T // CHUNKS
    lists = [
        pltpu.make_async_copy(dest_in, dest, sems.at[CHUNKS]),
        pltpu.make_async_copy(count_in, count, sems.at[CHUNKS + 1]),
    ]
    for copy in lists:
        copy.start()

    def fetch(c):
        piece = pl.ds(c * rows, rows)
        return pltpu.make_async_copy(weight.at[0, piece, 0], blocks.at[piece], sems.at[c])

    for c in range(CHUNKS):
        fetch(c).start()
    buffer[...] = jnp.zeros_like(buffer)

    def clear(i, _):
        used[i] = 0
        for k in range(CAP):
            label[i * CAP + k] = 0
        return 0

    lax.fori_loop(0, PEERS, clear, 0)
    for copy in lists:
        copy.wait()
    sub = subl(8)

    def place_of(row, f):
        target = dest[f, row]
        peer = (lax.shift_right_logical(target, 7) & (PEERS - 1)) ^ MIRROR
        live = f < count[0, row]
        at = used[peer]
        used[peer] = at + jnp.where(live, 1, 0)
        label[jnp.where(live, peer * CAP + at, PEERS * CAP)] = (target & (T - 1)) + 1
        return jnp.where(live, peer * SIZE + at * NV, PEERS * SIZE)

    def chunk(c, _):
        fetch(c).wait()
        for r in range(0, rows, 2):
            row = c * rows + r
            places = [[place_of(row + q, f) for f in range(FAN)] for q in range(2)]
            pair = surf[pl.ds(pl.multiple_of(row * NV, 8), 8), :]
            pair = jnp.concatenate(
                [jnp.where(sub < NV, pair, 0.0), jnp.where(sub >= NV, pair, 0.0)], axis=1
            ).astype(bf16)
            for f in range(0, FAN, 2):
                block = jnp.concatenate(
                    [
                        jnp.concatenate([blocks[row + q, f], blocks[row + q, f + 1]], axis=1)
                        for q in range(2)
                    ],
                    axis=0,
                )
                product = jnp.dot(pair, block, preferred_element_type=f32)
                for q in range(2):
                    for g in range(2):
                        part = product[q * NV : (q + 1) * NV, g * T : (g + 1) * T]
                        buffer[pl.ds(places[q][f + g], NV), :] = part
        return 0

    lax.fori_loop(0, CHUNKS, chunk, 0)
    lane = lanes(1)

    def name(i, _):
        line = jnp.zeros((1, T), i32)
        for k in range(CAP):
            line = jnp.where(lane == k, label[i * CAP + k], line)
        names[pl.ds(i, 1), :] = line.astype(f32)
        return 0

    lax.fori_loop(0, PEERS, name, 0, unroll=8)
    lane = lanes(PEERS)
    rims = jnp.zeros((PEERS, T), f32)
    for j in range(CAP * NV):
        column = EDGE + 2 * j
        turned = pltpu.roll(buffer[pl.ds(j, PEERS, stride=SIZE), :], (column + 1) % T, 1)
        rims = jnp.where((lane >> 1) == column >> 1, turned, rims)
    lane, sub = lanes(8), subl(8)
    left_end, right_end = sub == MIRROR, sub == MIRROR - 1
    for b in range(PEERS // 8):
        own, rim = names[b * 8 : b * 8 + 8, :], rims[b * 8 : b * 8 + 8, :]
        left_name, left_rim = (jnp.where(left_end, 0.0, pltpu.roll(x, 1, 0)) for x in (own, rim))
        right_name, right_rim = (jnp.where(right_end, 0.0, pltpu.roll(x, 7, 0)) for x in (own, rim))
        line = own + pltpu.roll(left_name, CAP, 1) + pltpu.roll(right_name, 2 * CAP, 1)
        line = line + jnp.where((lane & 1) == 0, left_rim, right_rim)
        buffer[pl.ds(b * 8 * SIZE + SIZE - 1, 8, stride=SIZE), :] = line
    run([pltpu.make_async_copy(buffer.at[pl.ds(0, PEERS * SIZE)], out, sems.at[0])])


def remap(dest, count, surf, weight, after):
    return pl.pallas_call(
        remap_kernel,
        in_specs=[HBM, HBM, VMEM, HBM, HBM],
        out_specs=HBM,
        out_shape=jax.ShapeDtypeStruct((PEERS * SIZE, T), f32),
        scratch_shapes=[
            pltpu.VMEM((T, FAN, T, T), bf16),
            pltpu.VMEM((PEERS * SIZE + 8, T), f32),
            pltpu.VMEM((PEERS, T), f32),
            pltpu.SMEM((FAN, T), i32),
            pltpu.SMEM((1, T), i32),
            pltpu.SMEM((PEERS,), i32),
            pltpu.SMEM((PEERS * CAP + 8,), i32),
            pltpu.SemaphoreType.DMA((CHUNKS + 2,)),
        ],
        compiler_params=params(44 * MIB),
        cost_estimate=cost(67 << 20, 20 << 20),
        name="remap",
    )(dest, count, surf, weight, after)


def sealed(block, *after):
    def kernel(*refs):
        del refs

    return pl.pallas_call(
        kernel,
        in_specs=[HBM] * (1 + len(after)),
        out_specs=HBM,
        out_shape=jax.ShapeDtypeStruct(block.shape, block.dtype),
        input_output_aliases={0: 0},
        compiler_params=params(MIB),
        name="sealed",
    )(block, *after)


def merged(left, right, back=2):
    return jnp.where((lanes(left.shape[0]) & 1) == 0, left, pltpu.roll(right, T - back, 1))


def diffuse(u, up, down, side, rate):
    rows = u.shape[0]
    lane, sub = lanes(rows), subl(rows)
    north = jnp.where(sub == 0, up, pltpu.roll(u, 1, 0))
    south = jnp.where(sub == rows - 1, down, pltpu.roll(u, rows - 1, 0))
    west = jnp.where(lane == 0, side, pltpu.roll(u, 1, 1))
    east = jnp.where(lane == T - 1, side, pltpu.roll(u, T - 1, 1))
    return u + rate * ((north + south) + (west + east) - 4.0 * u)


def level_diffuse(u, top, bottom, side, rate, l, lo):
    up = top[l : l + 1, :] if lo == 0 else u[l, lo - 1 : lo, :]
    down = bottom[l : l + 1, :] if lo + HALF == T else u[l, lo + HALF : lo + HALF + 1, :]
    spin = side[lo : lo + HALF, :]
    if l:
        spin = pltpu.roll(spin, T - 2 * l, 1)
    return diffuse(u[l, lo : lo + HALF, :], up, down, spin, rate)


def halo_columns(rate, left, right, own):
    lane, sub = lanes(T), subl(T)
    here = merged(left[0:T, :], right[0:T, :])
    outer = merged(pltpu.roll(left[COL_NEXT : COL_NEXT + T, :], 1, 1), right[COL_NEXT : COL_NEXT + T, :], 3)
    inner = pltpu.roll(own[0:T, :], T - 1, 1)
    ends = [merged(left[at : at + 8, :], right[at : at + 8, :])[0:1, :] for at in (COL_TOP, COL_BOTTOM)]
    north = jnp.where(sub == 0, ends[0], pltpu.roll(here, 1, 0))
    south = jnp.where(sub == T - 1, ends[1], pltpu.roll(here, T - 1, 0))
    plane = ((lane + 1) >> 1) & (PLANES - 1)
    number = jnp.full((T, T), rate[0, 0], f32)
    for v in range(1, NV):
        number = jnp.where(plane // LEV == v, rate[0, v], number)
    h = here + number * ((north + south) + (outer + inner) - 4.0 * here)
    coef = jnp.where(
        (lane & 1) == 0,
        jnp.broadcast_to(left[COL_COEF : COL_COEF + T, 0:1], (T, T)),
        jnp.broadcast_to(right[COL_COEF : COL_COEF + T, 1:2], (T, T)),
    )
    level = plane % LEV
    above = jnp.where(level < LEV - 1, pltpu.roll(h, T - 2, 1) - h, 0.0)
    below = jnp.where(level > 0, pltpu.roll(h, 2, 1) - h, 0.0)
    return here, h + coef * (above + below)


def halo_rows(rate, rows, own, left, right, k, v):
    at = v * LEV
    lane, level = lanes(LEV), subl(LEV)
    here = rows[at : at + LEV, :]
    corner = COL_COEF + k * PLANES + at
    west = jnp.where(
        lane == 0, pltpu.roll(left[corner : corner + LEV, :], T - 4, 1), pltpu.roll(here, 1, 1)
    )
    east = jnp.where(
        lane == T - 1,
        pltpu.roll(right[corner : corner + LEV, :], T - 6, 1),
        pltpu.roll(here, T - 1, 1),
    )
    outer = rows[PLANES + at : PLANES + at + LEV, :]
    inner = own[at : at + LEV, :]
    h = here + rate[0, v] * ((outer + inner) + (west + east) - 4.0 * here)
    above = jnp.where(level < LEV - 1, pltpu.roll(h, LEV - 1, 0) - h, 0.0)
    below = jnp.where(level > 0, pltpu.roll(h, 1, 0) - h, 0.0)
    return h + rows[ROW_VERT : ROW_VERT + 1, :] * (above + below)


def step_kernel(
    rate, state, coef, sea, own, top, bottom, near, far,
    out, keep, u, w, stage, inner, top1, bottom1, top2, bottom2, side1, side2, turned, sems,
):
    def emit(v):
        levels = pl.ds(2, LEV - 2)
        return pltpu.make_async_copy(stage.at[v], out.at[0, v, levels], sems.at[v])

    loads = [pltpu.make_async_copy(state.at[0, v], u.at[v], sems.at[v]) for v in range(NV)]
    for load in loads:
        load.start()
    up, down, _, _ = inside()
    side1[...], side2[...] = halo_columns(rate, near, far, own)
    for v in range(NV):
        loads[v].wait()
        at = v * LEV
        for l in range(LEV):
            inner[0, at + l : at + l + 1, :] = u[v, l, 0:1, :] * up
            inner[1, at + l : at + l + 1, :] = u[v, l, T - 1 : T, :] * down
    for v in range(NV):
        at = v * LEV
        top1[v] = top[at : at + LEV, :]
        bottom1[v] = bottom[at : at + LEV, :]
        top2[v] = halo_rows(rate, top, inner.at[0], near, far, 0, v)
        bottom2[v] = halo_rows(rate, bottom, inner.at[1], near, far, 1, v)

    def first(v, _):
        number = rate[0, v]
        turned[...] = pltpu.roll(side1[...], lax.rem((NV - v) * 32, T), 1)
        source, result = u.at[v], w.at[v]
        for lo in range(0, T, HALF):
            mix = coef[lo : lo + HALF, :]
            at = lambda l: level_diffuse(source, top1.at[v], bottom1.at[v], turned, number, l, lo)
            before, here = None, at(0)
            for l in range(LEV):
                after = at(l + 1) if l + 1 < LEV else None
                if before is None:
                    term = after - here
                elif after is None:
                    term = before - here
                else:
                    term = (after - here) + (before - here)
                result[l, lo : lo + HALF, :] = here + mix * term
                before, here = here, after
        return 0

    lax.fori_loop(0, NV, first, 0)

    def second(v, _):
        number = rate[0, v]
        turned[...] = pltpu.roll(side2[...], lax.rem((NV - v) * 32, T), 1)
        source, result = w.at[v], stage.at[v]
        for lo in range(0, T, HALF):
            mix = coef[lo : lo + HALF, :]
            at = lambda l: level_diffuse(source, top2.at[v], bottom2.at[v], turned, number, l, lo)
            before, here = at(1), at(2)
            row = pl.multiple_of(v * T + lo, 8)
            keep[pl.ds(KEEP_BASE + row, HALF), :] = source[0, lo : lo + HALF, :]
            keep[pl.ds(KEEP_ONE + row, HALF), :] = before
            keep[pl.ds(KEEP_PART + row, HALF), :] = before + mix * ((here - before) - before)
            for l in range(2, LEV):
                after = at(l + 1) if l + 1 < LEV else None
                term = before - here
                if after is not None:
                    term = (after - here) + term
                result[l - 2, lo : lo + HALF, :] = here + mix * term
                before, here = here, after
        emit(v).start()
        return 0

    lax.fori_loop(0, NV, second, 0)
    keep[KEEP_VERT : KEEP_VERT + T, :] = coef[...]
    keep[KEEP_SEA : KEEP_SEA + T, :] = sea[...]
    keep[KEEP_SIDE : KEEP_SIDE + T, :] = side2[...]
    coefs = pl.ds(COL_COEF, T)
    keep[KEEP_SEA_SIDE : KEEP_SEA_SIDE + T, :] = jnp.where(
        lanes(T) == 0, pltpu.roll(near[coefs, :], T - 2, 1), pltpu.roll(far[coefs, :], T - 4, 1)
    )
    for k, (rows, line) in enumerate(((top2, top), (bottom2, bottom))):
        for v in range(NV):
            keep[KEEP_ENDS + 8 * k + v : KEEP_ENDS + 8 * k + v + 1, :] = rows[v, 0:1, :]
        keep[KEEP_ENDS + 8 * k + NV : KEEP_ENDS + 8 * k + 8, :] = line[ROW_SEA : ROW_SEA + NV, :]
    for v in range(NV):
        emit(v).wait()


def two_steps(rate, state, coef, sea, own, top, bottom, left, right):
    rows = pltpu.VMEM((NV, LEV, T), f32)
    square = pltpu.VMEM((T, T), f32)
    return pl.pallas_call(
        step_kernel,
        in_specs=[SMEM, HBM] + [VMEM] * 7,
        out_specs=[HBM, VMEM],
        out_shape=[
            jax.ShapeDtypeStruct(state.shape, f32),
            jax.ShapeDtypeStruct((KEEP_SIZE, T), f32),
        ],
        scratch_shapes=[
            pltpu.VMEM((NV, LEV, T, T), f32),
            pltpu.VMEM((NV, LEV, T, T), f32),
            pltpu.VMEM((NV, LEV - 2, T, T), f32),
            pltpu.VMEM((2, PLANES, T), f32),
            rows,
            rows,
            rows,
            rows,
            square,
            square,
            square,
            pltpu.SemaphoreType.DMA((NV,)),
        ],
        compiler_params=params(20 * MIB),
        cost_estimate=cost(48 << 20, 10 << 20),
        name="two_steps",
    )(rate, state, coef, sea, own, top, bottom, left, right)


def unpack_kernel(data, after, imp, first, last):
    del after
    sub = subl(T).astype(f32) + 1.0
    line = data[pl.ds(SIZE - 1, PEERS, stride=SIZE), :]
    fields = jnp.transpose(jnp.concatenate([line, jnp.zeros((T - PEERS, T), f32)], axis=0))

    def two(at, size):
        return fields[at : at + size, :] + pltpu.roll(fields[at + size : at + 2 * size, :], PEERS, 1)

    def split(x):
        high = x.astype(bf16)
        return high, (x - high.astype(f32)).astype(bf16)

    def picks(at):
        return jnp.concatenate(
            [(sub == two(at + k, 1)).astype(bf16) for k in range(0, CAP, 2)], axis=1
        )

    pick = picks(0)
    up, down, _, _ = inside()
    for v in range(NV):
        block = jnp.concatenate(
            [data[pl.ds(k * NV + v, PEERS, stride=SIZE), :] for k in range(CAP)], axis=0
        )
        high, low = split(block)
        total = jnp.dot(pick, high, preferred_element_type=f32)
        total = total + jnp.dot(pick, low, preferred_element_type=f32)
        imp[v * T : (v + 1) * T, :] = total
        for out, row, keep in ((first, 0, up), (last, T - 1, down)):
            out[v : v + 1, :] = total[row : row + 1, :] * keep
            out[NV + v : NV + v + 1, :] = total[row : row + 1, :] * keep
    rims = jnp.concatenate([two(EDGE + 8 * k, 8) for k in range(0, CAP, 2)], axis=1)
    sides = []
    for at in (CAP, 2 * CAP):
        pick = picks(at)
        high, low = (
            lax.dot_general(part, pick, (((1,), (1,)), ((), ())), preferred_element_type=f32)
            for part in split(rims)
        )
        sides.append(high + low)
    imp[NV * T : NV * T + 8, :] = jnp.where((subl(8) & 1) == 0, sides[0], sides[1])


def unpack(data, after):
    return pl.pallas_call(
        unpack_kernel,
        in_specs=[VMEM, HBM],
        out_specs=[VMEM] * 3,
        out_shape=[
            jax.ShapeDtypeStruct((NV * T + 8, T), f32),
            jax.ShapeDtypeStruct((2 * NV, T), f32),
            jax.ShapeDtypeStruct((2 * NV, T), f32),
        ],
        compiler_params=params(12 * MIB),
        cost_estimate=cost(200 << 20, 2 << 20),
        name="unpack",
    )(data, after)


def final_kernel(
    horiz, relax, mid, near, imp, imp_top, imp_bottom, out, stage, sems
):
    del mid
    ends = jnp.concatenate([imp[NV * T : NV * T + 8, :], jnp.zeros((T - 8, T), f32)], axis=0)
    side_new = jnp.transpose(ends)
    sea, sea_side = near[KEEP_SEA : KEEP_SEA + T, :], near[KEEP_SEA_SIDE : KEEP_SEA_SIDE + T, :]
    coef = near[KEEP_VERT : KEEP_VERT + T, :]
    side_base = near[KEEP_SIDE : KEEP_SIDE + T, :]
    lane = lanes(T)
    copies = []
    for v in range(NV):
        pull = relax[0, v]

        def relaxed(base, wet, new, pull=pull):
            return base + pull * wet * (new - base)

        ends = []
        for k, new in enumerate((imp_top, imp_bottom)):
            at = KEEP_ENDS + 8 * k
            ends.append(
                relaxed(near[at + v : at + v + 1, :], near[at + NV : at + NV + 1, :], new[v : v + 1, :])
            )
        turn = (T - 32 * v) % T
        base = pltpu.roll(side_base, turn, 1) if turn else side_base
        new = pltpu.roll(side_new, T - 2 * v, 1) if v else side_new
        new = jnp.where(lane == 0, new, pltpu.roll(side_new, T - 2 - 2 * v, 1))
        mine = imp[v * T : (v + 1) * T, :]
        u = relaxed(near[KEEP_BASE + v * T : KEEP_BASE + (v + 1) * T, :], sea, mine)
        h = diffuse(u, ends[0], ends[1], relaxed(base, sea_side, new), horiz[0, v])
        one = near[KEEP_ONE + v * T : KEEP_ONE + (v + 1) * T, :]
        stage[v, 0] = relaxed(h + coef * (one - h), sea, mine)
        stage[v, 1] = near[KEEP_PART + v * T : KEEP_PART + (v + 1) * T, :] + coef * h
        copies.append(
            pltpu.make_async_copy(stage.at[v], out.at[0, v, pl.ds(0, 2)], sems.at[v])
        )
        copies[-1].start()
    for copy in copies:
        copy.wait()


def final(horiz, relax, mid, keep, imp, imp_rows):
    return pl.pallas_call(
        final_kernel,
        in_specs=[SMEM, SMEM, HBM] + [VMEM] * 4,
        out_specs=HBM,
        out_shape=jax.ShapeDtypeStruct(mid.shape, f32),
        input_output_aliases={2: 0},
        scratch_shapes=[
            pltpu.VMEM((NV, 2, T, T), f32),
            pltpu.SemaphoreType.DMA((NV,)),
        ],
        compiler_params=params(6 * MIB),
        cost_estimate=cost(2 << 20, 3 << 20),
        name="final",
    )(horiz, relax, mid, keep, imp, *imp_rows)


def shifted(block, axis, by):
    count = lax.axis_size(axis)
    return lax.ppermute(block, axis, [(i, (i + by) % count) for i in range(count)])


def crossed(block, gx_by=0):
    size = lax.axis_size("gx"), lax.axis_size("gy")
    route = []
    for c in range(2):
        for i in range(size[0]):
            for j in range(size[1]):
                to = (1 - c) * size[0] + (i + gx_by) % size[0]
                route.append(((c * size[0] + i) * size[1] + j, to * size[1] + (j ^ MIRROR)))
    return lax.ppermute(block, ("comp", "gx", "gy"), route)


def local(
    state, horiz_coef, vert_coef, couple_rate, sea_mask, dest_block, entry_count, remap_weight
):
    head, tail = outer_rows(state, vert_coef, sea_mask)
    top, bottom = shifted(tail, "gx", 1), shifted(head, "gx", -1)
    cols, surf, coef, sea = outer_columns(state, vert_coef, sea_mask)
    cols = with_corners(cols, top, bottom)
    left, right = shifted(cols, "gy", 1), shifted(cols, "gy", -1)
    dest = dest_block.reshape(T, FAN).T
    packed = remap(dest, entry_count.reshape(1, T), surf, remap_weight, cols)
    packed = sealed(packed, left, right).reshape(PEERS, SIZE, 1, T)
    packed = lax.all_to_all(packed, ("gx", "gy"), split_axis=0, concat_axis=0, tiled=True)
    mid, keep = two_steps(horiz_coef, state, coef, sea, cols, top, bottom, left, right)
    new, first, last = unpack(packed.reshape(PEERS * SIZE, T), keep)
    imp = crossed(new)
    imp_rows = crossed(last, 1), crossed(first, -1)
    return final(horiz_coef, couple_rate, mid, keep, imp, imp_rows)


def solution(mesh):
    in_specs = (
        P("comp", None, None, "gx", "gy"),
        P("comp", None),
        P("comp", "gx", "gy"),
        P("comp", None),
        P("comp", "gx", "gy"),
        P("comp", "gx", "gy", None),
        P("comp", "gx", "gy"),
        P("comp", "gx", "gy", None, None, None),
    )
    out_specs = P("comp", None, None, "gx", "gy")
    return jax.shard_map(local, mesh=mesh, in_specs=in_specs, out_specs=out_specs, check_vma=False)
```

```python
import jax
import jax.numpy as jnp
from jax import lax
from jax.experimental import pallas as pl
from jax.experimental.pallas import tpu as pltpu
from jax.sharding import PartitionSpec as P

NV = 4
LEV = 16
PLANES = NV * LEV
T = 128
FAN = 4
CAP = 8
PEERS = 64
SIZE = CAP * NV + 1
EDGE = 32
HALF = 64
CHUNKS = 16
EARLY = 32
MIRROR = 4
MIB = 1024 * 1024
LIMIT = 58 * MIB
ROW_VERT = 2 * PLANES
ROW_SEA = ROW_VERT + 8
ROW_SIZE = ROW_SEA + 8
COL_NEXT = T
COL_COEF = 2 * T
COL_TOP = 3 * T
COL_BOTTOM = COL_TOP + 8
COL_SIZE = COL_BOTTOM + 8
KEEP_BASE = 0
KEEP_ONE = NV * T
KEEP_PART = 2 * NV * T
KEEP_VERT = 3 * NV * T
KEEP_SEA = KEEP_VERT + T
KEEP_SIDE = KEEP_SEA + T
KEEP_SEA_SIDE = KEEP_SIDE + T
KEEP_ENDS = KEEP_SEA_SIDE + T
KEEP_SIZE = KEEP_ENDS + 16

f32 = jnp.float32
i32 = jnp.int32
bf16 = jnp.bfloat16

SMEM = pl.BlockSpec(memory_space=pltpu.SMEM)
VMEM = pl.BlockSpec(memory_space=pltpu.VMEM)
HBM = pl.BlockSpec(memory_space=pl.ANY)


def params(limit=LIMIT):
    return pltpu.CompilerParams(vmem_limit_bytes=limit)


def cost(flops, size):
    return pl.CostEstimate(flops=flops, bytes_accessed=size, transcendentals=0)


def lanes(rows):
    return lax.broadcasted_iota(i32, (rows, T), 1)


def subl(rows):
    return lax.broadcasted_iota(i32, (rows, T), 0)


def inside():
    gx, gy = lax.axis_index("gx"), lax.axis_index("gy")
    one = lambda test: jnp.where(test, 1.0, 0.0).astype(f32)
    return (
        one(gx > 0),
        one(gx < lax.axis_size("gx") - 1),
        one(gy > 0),
        one(gy < lax.axis_size("gy") - 1),
    )


def column_keep(rows, later=0):
    _, _, before, after = inside()
    return jnp.where((lanes(rows) & 1) == later, after, before)


def run(copies):
    for copy in copies:
        copy.start()
    for copy in copies:
        copy.wait()


def row_kernel(state, vert, mask, head, tail, high, low, coef, sea, sems):
    ends = pl.ds(0, 8), pl.ds(T - 8, 8)
    copies = []
    for k, buffer in enumerate((high, low)):
        copies.append(pltpu.make_async_copy(state.at[0, :, :, ends[k]], buffer, sems.at[3 * k]))
        copies.append(pltpu.make_async_copy(vert.at[0, ends[k]], coef.at[k], sems.at[3 * k + 1]))
        copies.append(pltpu.make_async_copy(mask.at[0, ends[k]], sea.at[k], sems.at[3 * k + 2]))
    run(copies)
    up, down, _, _ = inside()
    for k, (out, buffer, keep) in enumerate(((head, high, up), (tail, low, down))):
        outer, following = (0, 1) if k == 0 else (7, 6)
        flat = buffer.reshape(PLANES * 8, T)
        out[0:PLANES, :] = flat[pl.ds(outer, PLANES, stride=8), :] * keep
        out[PLANES : 2 * PLANES, :] = flat[pl.ds(following, PLANES, stride=8), :] * keep
        line = coef[k, outer : outer + 1, :] * keep
        out[ROW_VERT : ROW_VERT + 8, :] = jnp.broadcast_to(line, (8, T))
        line = sea[k, outer : outer + 1, :].astype(f32) * keep
        out[ROW_SEA : ROW_SEA + 8, :] = jnp.broadcast_to(line, (8, T))


def outer_rows(state, vert, mask):
    return pl.pallas_call(
        row_kernel,
        in_specs=[HBM, HBM, HBM],
        out_specs=[VMEM, VMEM],
        out_shape=[jax.ShapeDtypeStruct((ROW_SIZE, T), f32)] * 2,
        scratch_shapes=[
            pltpu.VMEM((NV, LEV, 8, T), f32),
            pltpu.VMEM((NV, LEV, 8, T), f32),
            pltpu.VMEM((2, 8, T), f32),
            pltpu.VMEM((2, 8, T), i32),
            pltpu.SemaphoreType.DMA((6,)),
        ],
        compiler_params=params(),
        cost_estimate=cost(1 << 16, 1 << 19),
        name="outer_rows",
    )(state, vert, mask)


def column_kernel(state, vert, mask, weight, cols, surf, coef, wet, early, tile, sea, sems):
    loads = [pltpu.make_async_copy(state.at[0, v], tile.at[v], sems.at[v]) for v in range(NV)]
    loads.append(pltpu.make_async_copy(vert.at[0], coef, sems.at[NV]))
    loads.append(pltpu.make_async_copy(mask.at[0], sea, sems.at[NV + 1]))
    loads.append(pltpu.make_async_copy(weight.at[0, pl.ds(0, EARLY), 0], early, sems.at[NV + 2]))
    for load in loads:
        load.start()
    lane = lanes(HALF)
    keep = column_keep(HALF)
    keep2 = column_keep(HALF, 1)
    for v in range(NV):
        loads[v].wait()
        surf[pl.ds(v, T, stride=NV), :] = tile[v, 0]
        for lo in range(0, T, HALF):
            outer, following = pl.ds(lo, HALF), pl.ds(COL_NEXT + lo, HALF)
            acc = jnp.zeros((HALF, T), f32) if v == 0 else cols[outer, :]
            acc2 = jnp.zeros((HALF, T), f32) if v == 0 else cols[following, :]
            for l in range(LEV):
                p = v * LEV + l
                plane = tile[v, l, lo : lo + HALF, :]
                turned = pltpu.roll(plane, (2 * p + 1) % T, 1)
                acc = jnp.where((lane >> 1) == p, turned, acc)
                acc2 = jnp.where((lane == (2 * p - 1) % T) | (lane == (2 * p + 2) % T), turned, acc2)
            last = v == NV - 1
            cols[outer, :] = acc * keep if last else acc
            cols[following, :] = acc2 * keep2 if last else acc2
    loads[NV].wait()
    loads[NV + 1].wait()
    lane = lanes(T)
    wet[...] = sea[...].astype(f32)
    pair = jnp.where(lane < 2, pltpu.roll(coef[...], 1, 1), pltpu.roll(wet[...], 3, 1))
    cols[COL_COEF : COL_COEF + T, :] = pair * column_keep(T)
    loads[NV + 2].wait()


def outer_columns(state, vert, mask, weight):
    square = jax.ShapeDtypeStruct((T, T), f32)
    return pl.pallas_call(
        column_kernel,
        in_specs=[HBM] * 4,
        out_specs=[VMEM] * 5,
        out_shape=[
            jax.ShapeDtypeStruct((COL_TOP, T), f32),
            jax.ShapeDtypeStruct((T * NV, T), f32),
            square,
            square,
            jax.ShapeDtypeStruct((EARLY, FAN, T, T), bf16),
        ],
        scratch_shapes=[
            pltpu.VMEM((NV, LEV, T, T), f32),
            pltpu.VMEM((T, T), i32),
            pltpu.SemaphoreType.DMA((NV + 3,)),
        ],
        compiler_params=params(46 * MIB),
        cost_estimate=cost(6 << 20, 9 << 20),
        name="outer_columns",
    )(state, vert, mask, weight)


def corner_kernel(cols, top, bottom, out):
    out[0:COL_COEF, :] = cols[0:COL_COEF, :]
    lane, sub = lanes(PLANES), subl(PLANES)
    keep = column_keep(PLANES)
    for k, rows in enumerate((top, bottom)):
        line = rows[0:PLANES, :]
        at = COL_COEF + k * PLANES
        out[at : at + PLANES, :] = jnp.where(
            (lane == 4) | (lane == 5), pltpu.roll(line, 5, 1) * keep, cols[at : at + PLANES, :]
        )
        first = jnp.broadcast_to(line[:, 0:1], (PLANES, T))
        last = jnp.broadcast_to(line[:, T - 1 : T], (PLANES, T))
        spread = jnp.where(lane == 2 * sub, last, jnp.where(lane == 2 * sub + 1, first, 0.0))
        total = jnp.sum(spread * keep, axis=0, keepdims=True)
        at = COL_TOP + 8 * k
        out[at : at + 8, :] = jnp.broadcast_to(total, (8, T))


def with_corners(cols, top, bottom):
    return pl.pallas_call(
        corner_kernel,
        in_specs=[VMEM] * 3,
        out_specs=VMEM,
        out_shape=jax.ShapeDtypeStruct((COL_SIZE, T), f32),
        compiler_params=params(4 * MIB),
        cost_estimate=cost(1 << 16, 1 << 18),
        name="with_corners",
    )(cols, top, bottom)


def remap_kernel(
    dest_in, count_in, surf, weight, early, after, out, blocks, buffer, names, dest, count, used, label, sems
):
    del after
    rows = T // CHUNKS
    lists = [
        pltpu.make_async_copy(dest_in, dest, sems.at[CHUNKS]),
        pltpu.make_async_copy(count_in, count, sems.at[CHUNKS + 1]),
    ]
    for copy in lists:
        copy.start()

    def fetch(c):
        piece = pl.ds(c * rows, rows)
        there = pl.ds(c * rows - EARLY, rows)
        return pltpu.make_async_copy(weight.at[0, piece, 0], blocks.at[there], sems.at[c])

    for c in range(EARLY // rows, CHUNKS):
        fetch(c).start()
    buffer[...] = jnp.zeros_like(buffer)

    def clear(i, _):
        used[i] = 0
        for k in range(CAP):
            label[i * CAP + k] = 0
        return 0

    lax.fori_loop(0, PEERS, clear, 0)
    for copy in lists:
        copy.wait()
    sub = subl(8)

    def place_of(row, f):
        target = dest[f, row]
        peer = (lax.shift_right_logical(target, 7) & (PEERS - 1)) ^ MIRROR
        live = f < count[0, row]
        at = used[peer]
        used[peer] = at + jnp.where(live, 1, 0)
        label[jnp.where(live, peer * CAP + at, PEERS * CAP)] = (target & (T - 1)) + 1
        return jnp.where(live, peer * SIZE + at * NV, PEERS * SIZE)

    def chunk(c, given, skipped):
        for r in range(0, rows, 2):
            row = c * rows + r
            places = [[place_of(row + q, f) for f in range(FAN)] for q in range(2)]
            pair = surf[pl.ds(pl.multiple_of(row * NV, 8), 8), :]
            pair = jnp.concatenate(
                [jnp.where(sub < NV, pair, 0.0), jnp.where(sub >= NV, pair, 0.0)], axis=1
            ).astype(bf16)
            for f in range(0, FAN, 2):
                block = jnp.concatenate(
                    [
                        jnp.concatenate([given[row + q - skipped, f + g] for g in range(2)], axis=1)
                        for q in range(2)
                    ],
                    axis=0,
                )
                product = jnp.dot(pair, block, preferred_element_type=f32)
                for q in range(2):
                    for g in range(2):
                        part = product[q * NV : (q + 1) * NV, g * T : (g + 1) * T]
                        buffer[pl.ds(places[q][f + g], NV), :] = part

    def near(c, _):
        chunk(c, early, 0)
        return 0

    def far(c, _):
        fetch(c).wait()
        chunk(c, blocks, EARLY)
        return 0

    lax.fori_loop(0, EARLY // rows, near, 0)
    lax.fori_loop(EARLY // rows, CHUNKS, far, 0)
    lane = lanes(1)

    def name(i, _):
        line = jnp.zeros((1, T), i32)
        for k in range(CAP):
            line = jnp.where(lane == k, label[i * CAP + k], line)
        names[pl.ds(i, 1), :] = line.astype(f32)
        return 0

    lax.fori_loop(0, PEERS, name, 0, unroll=8)
    lane = lanes(PEERS)
    rims = jnp.zeros((PEERS, T), f32)
    for j in range(CAP * NV):
        column = EDGE + 2 * j
        turned = pltpu.roll(buffer[pl.ds(j, PEERS, stride=SIZE), :], (column + 1) % T, 1)
        rims = jnp.where((lane >> 1) == column >> 1, turned, rims)
    lane, sub = lanes(8), subl(8)
    left_end, right_end = sub == MIRROR, sub == MIRROR - 1
    for b in range(PEERS // 8):
        own, rim = names[b * 8 : b * 8 + 8, :], rims[b * 8 : b * 8 + 8, :]
        left_name, left_rim = (jnp.where(left_end, 0.0, pltpu.roll(x, 1, 0)) for x in (own, rim))
        right_name, right_rim = (jnp.where(right_end, 0.0, pltpu.roll(x, 7, 0)) for x in (own, rim))
        line = own + pltpu.roll(left_name, CAP, 1) + pltpu.roll(right_name, 2 * CAP, 1)
        line = line + jnp.where((lane & 1) == 0, left_rim, right_rim)
        buffer[pl.ds(b * 8 * SIZE + SIZE - 1, 8, stride=SIZE), :] = line
    run([pltpu.make_async_copy(buffer.at[pl.ds(0, PEERS * SIZE)], out, sems.at[0])])


def remap(dest, count, surf, weight, early, after):
    return pl.pallas_call(
        remap_kernel,
        in_specs=[HBM, HBM, VMEM, HBM, VMEM, HBM],
        out_specs=HBM,
        out_shape=jax.ShapeDtypeStruct((PEERS * SIZE, T), f32),
        scratch_shapes=[
            pltpu.VMEM((T - EARLY, FAN, T, T), bf16),
            pltpu.VMEM((PEERS * SIZE + 8, T), f32),
            pltpu.VMEM((PEERS, T), f32),
            pltpu.SMEM((FAN, T), i32),
            pltpu.SMEM((1, T), i32),
            pltpu.SMEM((PEERS,), i32),
            pltpu.SMEM((PEERS * CAP + 8,), i32),
            pltpu.SemaphoreType.DMA((CHUNKS + 2,)),
        ],
        compiler_params=params(44 * MIB),
        cost_estimate=cost(67 << 20, 20 << 20),
        name="remap",
    )(dest, count, surf, weight, early, after)


def sealed(block, *after):
    def kernel(*refs):
        del refs

    return pl.pallas_call(
        kernel,
        in_specs=[HBM] * (1 + len(after)),
        out_specs=HBM,
        out_shape=jax.ShapeDtypeStruct(block.shape, block.dtype),
        input_output_aliases={0: 0},
        compiler_params=params(MIB),
        name="sealed",
    )(block, *after)


def merged(left, right, back=2):
    return jnp.where((lanes(left.shape[0]) & 1) == 0, left, pltpu.roll(right, T - back, 1))


def diffuse(u, up, down, side, rate):
    rows = u.shape[0]
    lane, sub = lanes(rows), subl(rows)
    north = jnp.where(sub == 0, up, pltpu.roll(u, 1, 0))
    south = jnp.where(sub == rows - 1, down, pltpu.roll(u, rows - 1, 0))
    west = jnp.where(lane == 0, side, pltpu.roll(u, 1, 1))
    east = jnp.where(lane == T - 1, side, pltpu.roll(u, T - 1, 1))
    return u + rate * ((north + south) + (west + east) - 4.0 * u)


def level_diffuse(u, top, bottom, side, rate, l, lo):
    up = top[l : l + 1, :] if lo == 0 else u[l, lo - 1 : lo, :]
    down = bottom[l : l + 1, :] if lo + HALF == T else u[l, lo + HALF : lo + HALF + 1, :]
    spin = side[lo : lo + HALF, :]
    if l:
        spin = pltpu.roll(spin, T - 2 * l, 1)
    return diffuse(u[l, lo : lo + HALF, :], up, down, spin, rate)


def halo_columns(rate, left, right, own):
    lane, sub = lanes(T), subl(T)
    here = merged(left[0:T, :], right[0:T, :])
    outer = merged(pltpu.roll(left[COL_NEXT : COL_NEXT + T, :], 1, 1), right[COL_NEXT : COL_NEXT + T, :], 3)
    inner = pltpu.roll(own[0:T, :], T - 1, 1)
    ends = [merged(left[at : at + 8, :], right[at : at + 8, :])[0:1, :] for at in (COL_TOP, COL_BOTTOM)]
    north = jnp.where(sub == 0, ends[0], pltpu.roll(here, 1, 0))
    south = jnp.where(sub == T - 1, ends[1], pltpu.roll(here, T - 1, 0))
    plane = ((lane + 1) >> 1) & (PLANES - 1)
    number = jnp.full((T, T), rate[0, 0], f32)
    for v in range(1, NV):
        number = jnp.where(plane // LEV == v, rate[0, v], number)
    h = here + number * ((north + south) + (outer + inner) - 4.0 * here)
    coef = jnp.where(
        (lane & 1) == 0,
        jnp.broadcast_to(left[COL_COEF : COL_COEF + T, 0:1], (T, T)),
        jnp.broadcast_to(right[COL_COEF : COL_COEF + T, 1:2], (T, T)),
    )
    level = plane % LEV
    above = jnp.where(level < LEV - 1, pltpu.roll(h, T - 2, 1) - h, 0.0)
    below = jnp.where(level > 0, pltpu.roll(h, 2, 1) - h, 0.0)
    return here, h + coef * (above + below)


def halo_rows(rate, rows, own, left, right, k, v):
    at = v * LEV
    lane, level = lanes(LEV), subl(LEV)
    here = rows[at : at + LEV, :]
    corner = COL_COEF + k * PLANES + at
    west = jnp.where(
        lane == 0, pltpu.roll(left[corner : corner + LEV, :], T - 4, 1), pltpu.roll(here, 1, 1)
    )
    east = jnp.where(
        lane == T - 1,
        pltpu.roll(right[corner : corner + LEV, :], T - 6, 1),
        pltpu.roll(here, T - 1, 1),
    )
    outer = rows[PLANES + at : PLANES + at + LEV, :]
    inner = own[at : at + LEV, :]
    h = here + rate[0, v] * ((outer + inner) + (west + east) - 4.0 * here)
    above = jnp.where(level < LEV - 1, pltpu.roll(h, LEV - 1, 0) - h, 0.0)
    below = jnp.where(level > 0, pltpu.roll(h, 1, 0) - h, 0.0)
    return h + rows[ROW_VERT : ROW_VERT + 1, :] * (above + below)


def step_kernel(
    rate, state, coef, sea, own, top, bottom, near, far,
    out, keep, u, w, stage, inner, top1, bottom1, top2, bottom2, side1, side2, turned, sems,
):
    def emit(v):
        levels = pl.ds(2, LEV - 2)
        return pltpu.make_async_copy(stage.at[v], out.at[0, v, levels], sems.at[v])

    loads = [pltpu.make_async_copy(state.at[0, v], u.at[v], sems.at[v]) for v in range(NV)]
    for load in loads:
        load.start()
    up, down, _, _ = inside()
    side1[...], side2[...] = halo_columns(rate, near, far, own)
    for v in range(NV):
        loads[v].wait()
        at = v * LEV
        for l in range(LEV):
            inner[0, at + l : at + l + 1, :] = u[v, l, 0:1, :] * up
            inner[1, at + l : at + l + 1, :] = u[v, l, T - 1 : T, :] * down
    for v in range(NV):
        at = v * LEV
        top1[v] = top[at : at + LEV, :]
        bottom1[v] = bottom[at : at + LEV, :]
        top2[v] = halo_rows(rate, top, inner.at[0], near, far, 0, v)
        bottom2[v] = halo_rows(rate, bottom, inner.at[1], near, far, 1, v)

    def first(v, _):
        number = rate[0, v]
        turned[...] = pltpu.roll(side1[...], lax.rem((NV - v) * 32, T), 1)
        source, result = u.at[v], w.at[v]
        for lo in range(0, T, HALF):
            mix = coef[lo : lo + HALF, :]
            at = lambda l: level_diffuse(source, top1.at[v], bottom1.at[v], turned, number, l, lo)
            before, here = None, at(0)
            for l in range(LEV):
                after = at(l + 1) if l + 1 < LEV else None
                if before is None:
                    term = after - here
                elif after is None:
                    term = before - here
                else:
                    term = (after - here) + (before - here)
                result[l, lo : lo + HALF, :] = here + mix * term
                before, here = here, after
        return 0

    lax.fori_loop(0, NV, first, 0)

    def second(v, _):
        number = rate[0, v]
        turned[...] = pltpu.roll(side2[...], lax.rem((NV - v) * 32, T), 1)
        source, result = w.at[v], stage.at[v]
        for lo in range(0, T, HALF):
            mix = coef[lo : lo + HALF, :]
            at = lambda l: level_diffuse(source, top2.at[v], bottom2.at[v], turned, number, l, lo)
            before, here = at(1), at(2)
            row = pl.multiple_of(v * T + lo, 8)
            keep[pl.ds(KEEP_BASE + row, HALF), :] = source[0, lo : lo + HALF, :]
            keep[pl.ds(KEEP_ONE + row, HALF), :] = before
            keep[pl.ds(KEEP_PART + row, HALF), :] = before + mix * ((here - before) - before)
            for l in range(2, LEV):
                after = at(l + 1) if l + 1 < LEV else None
                term = before - here
                if after is not None:
                    term = (after - here) + term
                result[l - 2, lo : lo + HALF, :] = here + mix * term
                before, here = here, after
        emit(v).start()
        return 0

    lax.fori_loop(0, NV, second, 0)
    keep[KEEP_VERT : KEEP_VERT + T, :] = coef[...]
    keep[KEEP_SEA : KEEP_SEA + T, :] = sea[...]
    keep[KEEP_SIDE : KEEP_SIDE + T, :] = side2[...]
    coefs = pl.ds(COL_COEF, T)
    keep[KEEP_SEA_SIDE : KEEP_SEA_SIDE + T, :] = jnp.where(
        lanes(T) == 0, pltpu.roll(near[coefs, :], T - 2, 1), pltpu.roll(far[coefs, :], T - 4, 1)
    )
    for k, (rows, line) in enumerate(((top2, top), (bottom2, bottom))):
        for v in range(NV):
            keep[KEEP_ENDS + 8 * k + v : KEEP_ENDS + 8 * k + v + 1, :] = rows[v, 0:1, :]
        keep[KEEP_ENDS + 8 * k + NV : KEEP_ENDS + 8 * k + 8, :] = line[ROW_SEA : ROW_SEA + NV, :]
    for v in range(NV):
        emit(v).wait()


def two_steps(rate, state, coef, sea, own, top, bottom, left, right):
    rows = pltpu.VMEM((NV, LEV, T), f32)
    square = pltpu.VMEM((T, T), f32)
    return pl.pallas_call(
        step_kernel,
        in_specs=[SMEM, HBM] + [VMEM] * 7,
        out_specs=[HBM, VMEM],
        out_shape=[
            jax.ShapeDtypeStruct(state.shape, f32),
            jax.ShapeDtypeStruct((KEEP_SIZE, T), f32),
        ],
        scratch_shapes=[
            pltpu.VMEM((NV, LEV, T, T), f32),
            pltpu.VMEM((NV, LEV, T, T), f32),
            pltpu.VMEM((NV, LEV - 2, T, T), f32),
            pltpu.VMEM((2, PLANES, T), f32),
            rows,
            rows,
            rows,
            rows,
            square,
            square,
            square,
            pltpu.SemaphoreType.DMA((NV,)),
        ],
        compiler_params=params(20 * MIB),
        cost_estimate=cost(48 << 20, 10 << 20),
        name="two_steps",
    )(rate, state, coef, sea, own, top, bottom, left, right)


def unpack_kernel(data, after, imp, first, last):
    del after
    sub = subl(T).astype(f32) + 1.0
    line = data[pl.ds(SIZE - 1, PEERS, stride=SIZE), :]
    fields = jnp.transpose(jnp.concatenate([line, jnp.zeros((T - PEERS, T), f32)], axis=0))

    def two(at, size):
        return fields[at : at + size, :] + pltpu.roll(fields[at + size : at + 2 * size, :], PEERS, 1)

    def split(x):
        high = x.astype(bf16)
        return high, (x - high.astype(f32)).astype(bf16)

    def picks(at):
        return jnp.concatenate(
            [(sub == two(at + k, 1)).astype(bf16) for k in range(0, CAP, 2)], axis=1
        )

    pick = picks(0)
    up, down, _, _ = inside()
    for v in range(NV):
        block = jnp.concatenate(
            [data[pl.ds(k * NV + v, PEERS, stride=SIZE), :] for k in range(CAP)], axis=0
        )
        high, low = split(block)
        total = jnp.dot(pick, high, preferred_element_type=f32)
        total = total + jnp.dot(pick, low, preferred_element_type=f32)
        imp[v * T : (v + 1) * T, :] = total
        for out, row, keep in ((first, 0, up), (last, T - 1, down)):
            out[v : v + 1, :] = total[row : row + 1, :] * keep
            out[NV + v : NV + v + 1, :] = total[row : row + 1, :] * keep
    rims = jnp.concatenate([two(EDGE + 8 * k, 8) for k in range(0, CAP, 2)], axis=1)
    sides = []
    for at in (CAP, 2 * CAP):
        pick = picks(at)
        high, low = (
            lax.dot_general(part, pick, (((1,), (1,)), ((), ())), preferred_element_type=f32)
            for part in split(rims)
        )
        sides.append(high + low)
    imp[NV * T : NV * T + 8, :] = jnp.where((subl(8) & 1) == 0, sides[0], sides[1])


def unpack(data, after):
    return pl.pallas_call(
        unpack_kernel,
        in_specs=[VMEM, HBM],
        out_specs=[VMEM] * 3,
        out_shape=[
            jax.ShapeDtypeStruct((NV * T + 8, T), f32),
            jax.ShapeDtypeStruct((2 * NV, T), f32),
            jax.ShapeDtypeStruct((2 * NV, T), f32),
        ],
        compiler_params=params(12 * MIB),
        cost_estimate=cost(200 << 20, 2 << 20),
        name="unpack",
    )(data, after)


def final_kernel(
    horiz, relax, mid, near, imp, imp_top, imp_bottom, out, stage, sems
):
    del mid
    ends = jnp.concatenate([imp[NV * T : NV * T + 8, :], jnp.zeros((T - 8, T), f32)], axis=0)
    side_new = jnp.transpose(ends)
    sea, sea_side = near[KEEP_SEA : KEEP_SEA + T, :], near[KEEP_SEA_SIDE : KEEP_SEA_SIDE + T, :]
    coef = near[KEEP_VERT : KEEP_VERT + T, :]
    side_base = near[KEEP_SIDE : KEEP_SIDE + T, :]
    lane = lanes(T)
    copies = []
    for v in range(NV):
        pull = relax[0, v]

        def relaxed(base, wet, new, pull=pull):
            return base + pull * wet * (new - base)

        ends = []
        for k, new in enumerate((imp_top, imp_bottom)):
            at = KEEP_ENDS + 8 * k
            ends.append(
                relaxed(near[at + v : at + v + 1, :], near[at + NV : at + NV + 1, :], new[v : v + 1, :])
            )
        turn = (T - 32 * v) % T
        base = pltpu.roll(side_base, turn, 1) if turn else side_base
        new = pltpu.roll(side_new, T - 2 * v, 1) if v else side_new
        new = jnp.where(lane == 0, new, pltpu.roll(side_new, T - 2 - 2 * v, 1))
        mine = imp[v * T : (v + 1) * T, :]
        u = relaxed(near[KEEP_BASE + v * T : KEEP_BASE + (v + 1) * T, :], sea, mine)
        h = diffuse(u, ends[0], ends[1], relaxed(base, sea_side, new), horiz[0, v])
        one = near[KEEP_ONE + v * T : KEEP_ONE + (v + 1) * T, :]
        stage[v, 0] = relaxed(h + coef * (one - h), sea, mine)
        stage[v, 1] = near[KEEP_PART + v * T : KEEP_PART + (v + 1) * T, :] + coef * h
        copies.append(
            pltpu.make_async_copy(stage.at[v], out.at[0, v, pl.ds(0, 2)], sems.at[v])
        )
        copies[-1].start()
    for copy in copies:
        copy.wait()


def final(horiz, relax, mid, keep, imp, imp_rows):
    return pl.pallas_call(
        final_kernel,
        in_specs=[SMEM, SMEM, HBM] + [VMEM] * 4,
        out_specs=HBM,
        out_shape=jax.ShapeDtypeStruct(mid.shape, f32),
        input_output_aliases={2: 0},
        scratch_shapes=[
            pltpu.VMEM((NV, 2, T, T), f32),
            pltpu.SemaphoreType.DMA((NV,)),
        ],
        compiler_params=params(6 * MIB),
        cost_estimate=cost(2 << 20, 3 << 20),
        name="final",
    )(horiz, relax, mid, keep, imp, *imp_rows)


def shifted(block, axis, by):
    count = lax.axis_size(axis)
    return lax.ppermute(block, axis, [(i, (i + by) % count) for i in range(count)])


def crossed(block, gx_by=0):
    size = lax.axis_size("gx"), lax.axis_size("gy")
    route = []
    for c in range(2):
        for i in range(size[0]):
            for j in range(size[1]):
                to = (1 - c) * size[0] + (i + gx_by) % size[0]
                route.append(((c * size[0] + i) * size[1] + j, to * size[1] + (j ^ MIRROR)))
    return lax.ppermute(block, ("comp", "gx", "gy"), route)


def local(
    state, horiz_coef, vert_coef, couple_rate, sea_mask, dest_block, entry_count, remap_weight
):
    head, tail = outer_rows(state, vert_coef, sea_mask)
    top, bottom = shifted(tail, "gx", 1), shifted(head, "gx", -1)
    cols, surf, coef, sea, early = outer_columns(state, vert_coef, sea_mask, remap_weight)
    cols = with_corners(cols, top, bottom)
    left, right = shifted(cols, "gy", 1), shifted(cols, "gy", -1)
    dest = dest_block.reshape(T, FAN).T
    packed = remap(dest, entry_count.reshape(1, T), surf, remap_weight, early, cols)
    packed = sealed(packed, left, right).reshape(PEERS, SIZE, 1, T)
    packed = lax.all_to_all(packed, ("gx", "gy"), split_axis=0, concat_axis=0, tiled=True)
    mid, keep = two_steps(horiz_coef, state, coef, sea, cols, top, bottom, left, right)
    new, first, last = unpack(packed.reshape(PEERS * SIZE, T), keep)
    imp = crossed(new)
    imp_rows = crossed(last, 1), crossed(first, -1)
    return final(horiz_coef, couple_rate, mid, keep, imp, imp_rows)


def solution(mesh):
    in_specs = (
        P("comp", None, None, "gx", "gy"),
        P("comp", None),
        P("comp", "gx", "gy"),
        P("comp", None),
        P("comp", "gx", "gy"),
        P("comp", "gx", "gy", None),
        P("comp", "gx", "gy"),
        P("comp", "gx", "gy", None, None, None),
    )
    out_specs = P("comp", None, None, "gx", "gy")
    return jax.shard_map(local, mesh=mesh, in_specs=in_specs, out_specs=out_specs, check_vma=False)
```

```python
import jax
import jax.numpy as jnp
from jax import lax
from jax.experimental import pallas as pl
from jax.experimental.pallas import tpu as pltpu
from jax.sharding import PartitionSpec as P

NV = 4
LEV = 16
PLANES = NV * LEV
T = 128
FAN = 4
CAP = 8
PEERS = 64
SIZE = CAP * NV + 1
EDGE = 32
HALF = 64
CHUNKS = 16
MIRROR = 4
MIB = 1024 * 1024
LIMIT = 58 * MIB
ROW_VERT = 2 * PLANES
ROW_SEA = ROW_VERT + 8
ROW_SIZE = ROW_SEA + 8
COL_NEXT = T
COL_COEF = 2 * T
COL_TOP = 3 * T
COL_BOTTOM = COL_TOP + 8
COL_SIZE = COL_BOTTOM + 8
KEEP_BASE = 0
KEEP_ONE = NV * T
KEEP_PART = 2 * NV * T
KEEP_VERT = 3 * NV * T
KEEP_SEA = KEEP_VERT + T
KEEP_SIDE = KEEP_SEA + T
KEEP_SEA_SIDE = KEEP_SIDE + T
KEEP_ENDS = KEEP_SEA_SIDE + T
KEEP_SIZE = KEEP_ENDS + 16

f32 = jnp.float32
i32 = jnp.int32
bf16 = jnp.bfloat16

SMEM = pl.BlockSpec(memory_space=pltpu.SMEM)
VMEM = pl.BlockSpec(memory_space=pltpu.VMEM)
HBM = pl.BlockSpec(memory_space=pl.ANY)


def params(limit=LIMIT):
    return pltpu.CompilerParams(vmem_limit_bytes=limit)


def cost(flops, size):
    return pl.CostEstimate(flops=flops, bytes_accessed=size, transcendentals=0)


def lanes(rows):
    return lax.broadcasted_iota(i32, (rows, T), 1)


def subl(rows):
    return lax.broadcasted_iota(i32, (rows, T), 0)


def inside():
    gx, gy = lax.axis_index("gx"), lax.axis_index("gy")
    one = lambda test: jnp.where(test, 1.0, 0.0).astype(f32)
    return (
        one(gx > 0),
        one(gx < lax.axis_size("gx") - 1),
        one(gy > 0),
        one(gy < lax.axis_size("gy") - 1),
    )


def column_keep(rows, later=0):
    _, _, before, after = inside()
    return jnp.where((lanes(rows) & 1) == later, after, before)


def run(copies):
    for copy in copies:
        copy.start()
    for copy in copies:
        copy.wait()


def row_kernel(state, vert, mask, head, tail, high, low, coef, sea, sems):
    ends = pl.ds(0, 8), pl.ds(T - 8, 8)
    copies = []
    for k, buffer in enumerate((high, low)):
        copies.append(pltpu.make_async_copy(state.at[0, :, :, ends[k]], buffer, sems.at[3 * k]))
        copies.append(pltpu.make_async_copy(vert.at[0, ends[k]], coef.at[k], sems.at[3 * k + 1]))
        copies.append(pltpu.make_async_copy(mask.at[0, ends[k]], sea.at[k], sems.at[3 * k + 2]))
    run(copies)
    up, down, _, _ = inside()
    for k, (out, buffer, keep) in enumerate(((head, high, up), (tail, low, down))):
        outer, following = (0, 1) if k == 0 else (7, 6)
        flat = buffer.reshape(PLANES * 8, T)
        out[0:PLANES, :] = flat[pl.ds(outer, PLANES, stride=8), :] * keep
        out[PLANES : 2 * PLANES, :] = flat[pl.ds(following, PLANES, stride=8), :] * keep
        line = coef[k, outer : outer + 1, :] * keep
        out[ROW_VERT : ROW_VERT + 8, :] = jnp.broadcast_to(line, (8, T))
        line = sea[k, outer : outer + 1, :].astype(f32) * keep
        out[ROW_SEA : ROW_SEA + 8, :] = jnp.broadcast_to(line, (8, T))


def outer_rows(state, vert, mask):
    return pl.pallas_call(
        row_kernel,
        in_specs=[HBM, HBM, HBM],
        out_specs=[VMEM, VMEM],
        out_shape=[jax.ShapeDtypeStruct((ROW_SIZE, T), f32)] * 2,
        scratch_shapes=[
            pltpu.VMEM((NV, LEV, 8, T), f32),
            pltpu.VMEM((NV, LEV, 8, T), f32),
            pltpu.VMEM((2, 8, T), f32),
            pltpu.VMEM((2, 8, T), i32),
            pltpu.SemaphoreType.DMA((6,)),
        ],
        compiler_params=params(),
        cost_estimate=cost(1 << 16, 1 << 19),
        name="outer_rows",
    )(state, vert, mask)


def column_kernel(state, vert, mask, cols, surf, coef, wet, tile, sea, sems):
    loads = [pltpu.make_async_copy(state.at[0, v], tile.at[v], sems.at[v]) for v in range(NV)]
    loads.append(pltpu.make_async_copy(vert.at[0], coef, sems.at[NV]))
    loads.append(pltpu.make_async_copy(mask.at[0], sea, sems.at[NV + 1]))
    for load in loads:
        load.start()
    lane = lanes(HALF)
    keep = column_keep(HALF)
    keep2 = column_keep(HALF, 1)
    for v in range(NV):
        loads[v].wait()
        surf[pl.ds(v, T, stride=NV), :] = tile[v, 0]
        for lo in range(0, T, HALF):
            outer, following = pl.ds(lo, HALF), pl.ds(COL_NEXT + lo, HALF)
            acc = jnp.zeros((HALF, T), f32) if v == 0 else cols[outer, :]
            acc2 = jnp.zeros((HALF, T), f32) if v == 0 else cols[following, :]
            for l in range(LEV):
                p = v * LEV + l
                plane = tile[v, l, lo : lo + HALF, :]
                turned = pltpu.roll(plane, (2 * p + 1) % T, 1)
                acc = jnp.where((lane >> 1) == p, turned, acc)
                acc2 = jnp.where((lane == (2 * p - 1) % T) | (lane == (2 * p + 2) % T), turned, acc2)
            last = v == NV - 1
            cols[outer, :] = acc * keep if last else acc
            cols[following, :] = acc2 * keep2 if last else acc2
    loads[NV].wait()
    loads[NV + 1].wait()
    lane = lanes(T)
    wet[...] = sea[...].astype(f32)
    pair = jnp.where(lane < 2, pltpu.roll(coef[...], 1, 1), pltpu.roll(wet[...], 3, 1))
    cols[COL_COEF : COL_COEF + T, :] = pair * column_keep(T)


def outer_columns(state, vert, mask):
    square = jax.ShapeDtypeStruct((T, T), f32)
    return pl.pallas_call(
        column_kernel,
        in_specs=[HBM, HBM, HBM],
        out_specs=[VMEM] * 4,
        out_shape=[
            jax.ShapeDtypeStruct((COL_TOP, T), f32),
            jax.ShapeDtypeStruct((T * NV, T), f32),
            square,
            square,
        ],
        scratch_shapes=[
            pltpu.VMEM((NV, LEV, T, T), f32),
            pltpu.VMEM((T, T), i32),
            pltpu.SemaphoreType.DMA((NV + 2,)),
        ],
        compiler_params=params(51 * MIB),
        cost_estimate=cost(6 << 20, 9 << 20),
        name="outer_columns",
    )(state, vert, mask)


def corner_kernel(cols, top, bottom, out):
    out[0:COL_COEF, :] = cols[0:COL_COEF, :]
    lane, sub = lanes(PLANES), subl(PLANES)
    keep = column_keep(PLANES)
    for k, rows in enumerate((top, bottom)):
        line = rows[0:PLANES, :]
        at = COL_COEF + k * PLANES
        out[at : at + PLANES, :] = jnp.where(
            (lane == 4) | (lane == 5), pltpu.roll(line, 5, 1) * keep, cols[at : at + PLANES, :]
        )
        first = jnp.broadcast_to(line[:, 0:1], (PLANES, T))
        last = jnp.broadcast_to(line[:, T - 1 : T], (PLANES, T))
        spread = jnp.where(lane == 2 * sub, last, jnp.where(lane == 2 * sub + 1, first, 0.0))
        total = jnp.sum(spread * keep, axis=0, keepdims=True)
        at = COL_TOP + 8 * k
        out[at : at + 8, :] = jnp.broadcast_to(total, (8, T))


def with_corners(cols, top, bottom):
    return pl.pallas_call(
        corner_kernel,
        in_specs=[VMEM] * 3,
        out_specs=VMEM,
        out_shape=jax.ShapeDtypeStruct((COL_SIZE, T), f32),
        compiler_params=params(4 * MIB),
        cost_estimate=cost(1 << 16, 1 << 18),
        name="with_corners",
    )(cols, top, bottom)


def remap_kernel(
    dest_in, count_in, surf, weight, after, out, blocks, buffer, names, dest, count, used, label, sems
):
    del after
    rows = T // CHUNKS
    lists = [
        pltpu.make_async_copy(dest_in, dest, sems.at[CHUNKS]),
        pltpu.make_async_copy(count_in, count, sems.at[CHUNKS + 1]),
    ]
    for copy in lists:
        copy.start()

    def fetch(c):
        piece = pl.ds(c * rows, rows)
        return pltpu.make_async_copy(weight.at[0, piece, 0], blocks.at[piece], sems.at[c])

    for c in range(CHUNKS):
        fetch(c).start()
    buffer[...] = jnp.zeros_like(buffer)

    def clear(i, _):
        row = (i ^ MIRROR) * SIZE
        used[i] = row
        for k in range(CAP):
            label[row + k * NV] = 0
        return 0

    lax.fori_loop(0, PEERS, clear, 0)
    for copy in lists:
        copy.wait()
    sub = subl(8)

    def place_of(row, f):
        target = dest[f, row]
        device = lax.shift_right_logical(target, 7) & (PEERS - 1)
        live = f < count[0, row]
        at = used[device]
        used[device] = jnp.where(live, at + NV, at)
        place = jnp.where(live, at, PEERS * SIZE)
        label[place] = (target & (T - 1)) + 1
        return place

    def chunk(c, _):
        fetch(c).wait()
        for r in range(0, rows, 2):
            row = c * rows + r
            places = [[place_of(row + q, f) for f in range(FAN)] for q in range(2)]
            pair = surf[pl.ds(pl.multiple_of(row * NV, 8), 8), :]
            pair = jnp.concatenate(
                [jnp.where(sub < NV, pair, 0.0), jnp.where(sub >= NV, pair, 0.0)], axis=1
            ).astype(bf16)
            for f in range(0, FAN, 2):
                block = jnp.concatenate(
                    [
                        jnp.concatenate([blocks[row + q, f], blocks[row + q, f + 1]], axis=1)
                        for q in range(2)
                    ],
                    axis=0,
                )
                product = jnp.dot(pair, block, preferred_element_type=f32)
                for q in range(2):
                    for g in range(2):
                        part = product[q * NV : (q + 1) * NV, g * T : (g + 1) * T]
                        buffer[pl.ds(places[q][f + g], NV), :] = part
        return 0

    lax.fori_loop(0, CHUNKS, chunk, 0)
    lane = lanes(1)

    def name(i, _):
        line = jnp.zeros((1, T), i32)
        for k in range(CAP):
            line = jnp.where(lane == k, label[i * SIZE + k * NV], line)
        names[pl.ds(i, 1), :] = line.astype(f32)
        return 0

    lax.fori_loop(0, PEERS, name, 0, unroll=8)
    lane = lanes(PEERS)
    rims = jnp.zeros((PEERS, T), f32)
    for j in range(CAP * NV):
        column = EDGE + 2 * j
        turned = pltpu.roll(buffer[pl.ds(j, PEERS, stride=SIZE), :], (column + 1) % T, 1)
        rims = jnp.where((lane >> 1) == column >> 1, turned, rims)
    lane, sub = lanes(8), subl(8)
    left_end, right_end = sub == MIRROR, sub == MIRROR - 1
    for b in range(PEERS // 8):
        own, rim = names[b * 8 : b * 8 + 8, :], rims[b * 8 : b * 8 + 8, :]
        left_name, left_rim = (jnp.where(left_end, 0.0, pltpu.roll(x, 1, 0)) for x in (own, rim))
        right_name, right_rim = (jnp.where(right_end, 0.0, pltpu.roll(x, 7, 0)) for x in (own, rim))
        line = own + pltpu.roll(left_name, CAP, 1) + pltpu.roll(right_name, 2 * CAP, 1)
        line = line + jnp.where((lane & 1) == 0, left_rim, right_rim)
        buffer[pl.ds(b * 8 * SIZE + SIZE - 1, 8, stride=SIZE), :] = line
    run([pltpu.make_async_copy(buffer.at[pl.ds(0, PEERS * SIZE)], out, sems.at[0])])


def remap(dest, count, surf, weight, after):
    return pl.pallas_call(
        remap_kernel,
        in_specs=[HBM, HBM, VMEM, HBM, HBM],
        out_specs=HBM,
        out_shape=jax.ShapeDtypeStruct((PEERS * SIZE, T), f32),
        scratch_shapes=[
            pltpu.VMEM((T, FAN, T, T), bf16),
            pltpu.VMEM((PEERS * SIZE + 8, T), f32),
            pltpu.VMEM((PEERS, T), f32),
            pltpu.SMEM((FAN, T), i32),
            pltpu.SMEM((1, T), i32),
            pltpu.SMEM((PEERS,), i32),
            pltpu.SMEM((PEERS * SIZE + 8,), i32),
            pltpu.SemaphoreType.DMA((CHUNKS + 2,)),
        ],
        compiler_params=params(44 * MIB),
        cost_estimate=cost(67 << 20, 20 << 20),
        name="remap",
    )(dest, count, surf, weight, after)


def sealed(block, *after):
    def kernel(*refs):
        del refs

    return pl.pallas_call(
        kernel,
        in_specs=[HBM] * (1 + len(after)),
        out_specs=HBM,
        out_shape=jax.ShapeDtypeStruct(block.shape, block.dtype),
        input_output_aliases={0: 0},
        compiler_params=params(MIB),
        name="sealed",
    )(block, *after)


def merged(left, right, back=2):
    return jnp.where((lanes(left.shape[0]) & 1) == 0, left, pltpu.roll(right, T - back, 1))


def diffuse(u, up, down, side, rate):
    rows = u.shape[0]
    lane, sub = lanes(rows), subl(rows)
    north = jnp.where(sub == 0, up, pltpu.roll(u, 1, 0))
    south = jnp.where(sub == rows - 1, down, pltpu.roll(u, rows - 1, 0))
    west = jnp.where(lane == 0, side, pltpu.roll(u, 1, 1))
    east = jnp.where(lane == T - 1, side, pltpu.roll(u, T - 1, 1))
    return u + rate * ((north + south) + (west + east) - 4.0 * u)


def level_diffuse(u, top, bottom, side, rate, l, lo):
    up = top[l : l + 1, :] if lo == 0 else u[l, lo - 1 : lo, :]
    down = bottom[l : l + 1, :] if lo + HALF == T else u[l, lo + HALF : lo + HALF + 1, :]
    spin = side[lo : lo + HALF, :]
    if l:
        spin = pltpu.roll(spin, T - 2 * l, 1)
    return diffuse(u[l, lo : lo + HALF, :], up, down, spin, rate)


def halo_columns(rate, left, right, own):
    lane, sub = lanes(T), subl(T)
    here = merged(left[0:T, :], right[0:T, :])
    outer = merged(pltpu.roll(left[COL_NEXT : COL_NEXT + T, :], 1, 1), right[COL_NEXT : COL_NEXT + T, :], 3)
    inner = pltpu.roll(own[0:T, :], T - 1, 1)
    ends = [merged(left[at : at + 8, :], right[at : at + 8, :])[0:1, :] for at in (COL_TOP, COL_BOTTOM)]
    north = jnp.where(sub == 0, ends[0], pltpu.roll(here, 1, 0))
    south = jnp.where(sub == T - 1, ends[1], pltpu.roll(here, T - 1, 0))
    plane = ((lane + 1) >> 1) & (PLANES - 1)
    number = jnp.full((T, T), rate[0, 0], f32)
    for v in range(1, NV):
        number = jnp.where(plane // LEV == v, rate[0, v], number)
    h = here + number * ((north + south) + (outer + inner) - 4.0 * here)
    coef = jnp.where(
        (lane & 1) == 0,
        jnp.broadcast_to(left[COL_COEF : COL_COEF + T, 0:1], (T, T)),
        jnp.broadcast_to(right[COL_COEF : COL_COEF + T, 1:2], (T, T)),
    )
    level = plane % LEV
    above = jnp.where(level < LEV - 1, pltpu.roll(h, T - 2, 1) - h, 0.0)
    below = jnp.where(level > 0, pltpu.roll(h, 2, 1) - h, 0.0)
    return here, h + coef * (above + below)


def halo_rows(rate, rows, own, left, right, k, v):
    at = v * LEV
    lane, level = lanes(LEV), subl(LEV)
    here = rows[at : at + LEV, :]
    corner = COL_COEF + k * PLANES + at
    west = jnp.where(
        lane == 0, pltpu.roll(left[corner : corner + LEV, :], T - 4, 1), pltpu.roll(here, 1, 1)
    )
    east = jnp.where(
        lane == T - 1,
        pltpu.roll(right[corner : corner + LEV, :], T - 6, 1),
        pltpu.roll(here, T - 1, 1),
    )
    outer = rows[PLANES + at : PLANES + at + LEV, :]
    inner = own[at : at + LEV, :]
    h = here + rate[0, v] * ((outer + inner) + (west + east) - 4.0 * here)
    above = jnp.where(level < LEV - 1, pltpu.roll(h, LEV - 1, 0) - h, 0.0)
    below = jnp.where(level > 0, pltpu.roll(h, 1, 0) - h, 0.0)
    return h + rows[ROW_VERT : ROW_VERT + 1, :] * (above + below)


def step_kernel(
    rate, state, coef, sea, own, top, bottom, near, far,
    out, keep, u, w, stage, inner, top1, bottom1, top2, bottom2, side1, side2, turned, sems,
):
    def emit(v):
        levels = pl.ds(2, LEV - 2)
        return pltpu.make_async_copy(stage.at[v], out.at[0, v, levels], sems.at[v])

    loads = [pltpu.make_async_copy(state.at[0, v], u.at[v], sems.at[v]) for v in range(NV)]
    for load in loads:
        load.start()
    up, down, _, _ = inside()
    side1[...], side2[...] = halo_columns(rate, near, far, own)
    for v in range(NV):
        loads[v].wait()
        at = v * LEV
        for l in range(LEV):
            inner[0, at + l : at + l + 1, :] = u[v, l, 0:1, :] * up
            inner[1, at + l : at + l + 1, :] = u[v, l, T - 1 : T, :] * down
    for v in range(NV):
        at = v * LEV
        top1[v] = top[at : at + LEV, :]
        bottom1[v] = bottom[at : at + LEV, :]
        top2[v] = halo_rows(rate, top, inner.at[0], near, far, 0, v)
        bottom2[v] = halo_rows(rate, bottom, inner.at[1], near, far, 1, v)

    def first(v, _):
        number = rate[0, v]
        turned[...] = pltpu.roll(side1[...], lax.rem((NV - v) * 32, T), 1)
        source, result = u.at[v], w.at[v]
        for lo in range(0, T, HALF):
            mix = coef[lo : lo + HALF, :]
            at = lambda l: level_diffuse(source, top1.at[v], bottom1.at[v], turned, number, l, lo)
            before, here = None, at(0)
            for l in range(LEV):
                after = at(l + 1) if l + 1 < LEV else None
                if before is None:
                    term = after - here
                elif after is None:
                    term = before - here
                else:
                    term = (after - here) + (before - here)
                result[l, lo : lo + HALF, :] = here + mix * term
                before, here = here, after
        return 0

    lax.fori_loop(0, NV, first, 0)

    def second(v, _):
        number = rate[0, v]
        turned[...] = pltpu.roll(side2[...], lax.rem((NV - v) * 32, T), 1)
        source, result = w.at[v], stage.at[v]
        for lo in range(0, T, HALF):
            mix = coef[lo : lo + HALF, :]
            at = lambda l: level_diffuse(source, top2.at[v], bottom2.at[v], turned, number, l, lo)
            before, here = at(1), at(2)
            row = pl.multiple_of(v * T + lo, 8)
            keep[pl.ds(KEEP_BASE + row, HALF), :] = source[0, lo : lo + HALF, :]
            keep[pl.ds(KEEP_ONE + row, HALF), :] = before
            keep[pl.ds(KEEP_PART + row, HALF), :] = before + mix * ((here - before) - before)
            for l in range(2, LEV):
                after = at(l + 1) if l + 1 < LEV else None
                term = before - here
                if after is not None:
                    term = (after - here) + term
                result[l - 2, lo : lo + HALF, :] = here + mix * term
                before, here = here, after
        emit(v).start()
        return 0

    lax.fori_loop(0, NV, second, 0)
    keep[KEEP_VERT : KEEP_VERT + T, :] = coef[...]
    keep[KEEP_SEA : KEEP_SEA + T, :] = sea[...]
    keep[KEEP_SIDE : KEEP_SIDE + T, :] = side2[...]
    coefs = pl.ds(COL_COEF, T)
    keep[KEEP_SEA_SIDE : KEEP_SEA_SIDE + T, :] = jnp.where(
        lanes(T) == 0, pltpu.roll(near[coefs, :], T - 2, 1), pltpu.roll(far[coefs, :], T - 4, 1)
    )
    for k, (rows, line) in enumerate(((top2, top), (bottom2, bottom))):
        for v in range(NV):
            keep[KEEP_ENDS + 8 * k + v : KEEP_ENDS + 8 * k + v + 1, :] = rows[v, 0:1, :]
        keep[KEEP_ENDS + 8 * k + NV : KEEP_ENDS + 8 * k + 8, :] = line[ROW_SEA : ROW_SEA + NV, :]
    for v in range(NV):
        emit(v).wait()


def two_steps(rate, state, coef, sea, own, top, bottom, left, right):
    rows = pltpu.VMEM((NV, LEV, T), f32)
    square = pltpu.VMEM((T, T), f32)
    return pl.pallas_call(
        step_kernel,
        in_specs=[SMEM, HBM] + [VMEM] * 7,
        out_specs=[HBM, VMEM],
        out_shape=[
            jax.ShapeDtypeStruct(state.shape, f32),
            jax.ShapeDtypeStruct((KEEP_SIZE, T), f32),
        ],
        scratch_shapes=[
            pltpu.VMEM((NV, LEV, T, T), f32),
            pltpu.VMEM((NV, LEV, T, T), f32),
            pltpu.VMEM((NV, LEV - 2, T, T), f32),
            pltpu.VMEM((2, PLANES, T), f32),
            rows,
            rows,
            rows,
            rows,
            square,
            square,
            square,
            pltpu.SemaphoreType.DMA((NV,)),
        ],
        compiler_params=params(20 * MIB),
        cost_estimate=cost(48 << 20, 10 << 20),
        name="two_steps",
    )(rate, state, coef, sea, own, top, bottom, left, right)


def unpack_kernel(data, after, imp, first, last):
    del after
    sub = subl(T).astype(f32) + 1.0
    line = data[pl.ds(SIZE - 1, PEERS, stride=SIZE), :]
    fields = jnp.transpose(jnp.concatenate([line, jnp.zeros((T - PEERS, T), f32)], axis=0))

    def two(at, size):
        return fields[at : at + size, :] + pltpu.roll(fields[at + size : at + 2 * size, :], PEERS, 1)

    def split(x):
        high = x.astype(bf16)
        return high, (x - high.astype(f32)).astype(bf16)

    def picks(at):
        return jnp.concatenate(
            [(sub == two(at + k, 1)).astype(bf16) for k in range(0, CAP, 2)], axis=1
        )

    pick = picks(0)
    up, down, _, _ = inside()
    for v in range(NV):
        block = jnp.concatenate(
            [data[pl.ds(k * NV + v, PEERS, stride=SIZE), :] for k in range(CAP)], axis=0
        )
        high, low = split(block)
        total = jnp.dot(pick, high, preferred_element_type=f32)
        total = total + jnp.dot(pick, low, preferred_element_type=f32)
        imp[v * T : (v + 1) * T, :] = total
        for out, row, keep in ((first, 0, up), (last, T - 1, down)):
            out[v : v + 1, :] = total[row : row + 1, :] * keep
            out[NV + v : NV + v + 1, :] = total[row : row + 1, :] * keep
    rims = jnp.concatenate([two(EDGE + 8 * k, 8) for k in range(0, CAP, 2)], axis=1)
    sides = []
    for at in (CAP, 2 * CAP):
        pick = picks(at)
        high, low = (
            lax.dot_general(part, pick, (((1,), (1,)), ((), ())), preferred_element_type=f32)
            for part in split(rims)
        )
        sides.append(high + low)
    imp[NV * T : NV * T + 8, :] = jnp.where((subl(8) & 1) == 0, sides[0], sides[1])


def unpack(data, after):
    return pl.pallas_call(
        unpack_kernel,
        in_specs=[VMEM, HBM],
        out_specs=[VMEM] * 3,
        out_shape=[
            jax.ShapeDtypeStruct((NV * T + 8, T), f32),
            jax.ShapeDtypeStruct((2 * NV, T), f32),
            jax.ShapeDtypeStruct((2 * NV, T), f32),
        ],
        compiler_params=params(12 * MIB),
        cost_estimate=cost(200 << 20, 2 << 20),
        name="unpack",
    )(data, after)


def final_kernel(
    horiz, relax, mid, near, imp, imp_top, imp_bottom, out, stage, sems
):
    del mid
    ends = jnp.concatenate([imp[NV * T : NV * T + 8, :], jnp.zeros((T - 8, T), f32)], axis=0)
    side_new = jnp.transpose(ends)
    sea, sea_side = near[KEEP_SEA : KEEP_SEA + T, :], near[KEEP_SEA_SIDE : KEEP_SEA_SIDE + T, :]
    coef = near[KEEP_VERT : KEEP_VERT + T, :]
    side_base = near[KEEP_SIDE : KEEP_SIDE + T, :]
    lane = lanes(T)
    copies = []
    for v in range(NV):
        pull = relax[0, v]

        def relaxed(base, wet, new, pull=pull):
            return base + pull * wet * (new - base)

        ends = []
        for k, new in enumerate((imp_top, imp_bottom)):
            at = KEEP_ENDS + 8 * k
            ends.append(
                relaxed(near[at + v : at + v + 1, :], near[at + NV : at + NV + 1, :], new[v : v + 1, :])
            )
        turn = (T - 32 * v) % T
        base = pltpu.roll(side_base, turn, 1) if turn else side_base
        new = pltpu.roll(side_new, T - 2 * v, 1) if v else side_new
        new = jnp.where(lane == 0, new, pltpu.roll(side_new, T - 2 - 2 * v, 1))
        mine = imp[v * T : (v + 1) * T, :]
        u = relaxed(near[KEEP_BASE + v * T : KEEP_BASE + (v + 1) * T, :], sea, mine)
        h = diffuse(u, ends[0], ends[1], relaxed(base, sea_side, new), horiz[0, v])
        one = near[KEEP_ONE + v * T : KEEP_ONE + (v + 1) * T, :]
        stage[v, 0] = relaxed(h + coef * (one - h), sea, mine)
        stage[v, 1] = near[KEEP_PART + v * T : KEEP_PART + (v + 1) * T, :] + coef * h
        copies.append(
            pltpu.make_async_copy(stage.at[v], out.at[0, v, pl.ds(0, 2)], sems.at[v])
        )
        copies[-1].start()
    for copy in copies:
        copy.wait()


def final(horiz, relax, mid, keep, imp, imp_rows):
    return pl.pallas_call(
        final_kernel,
        in_specs=[SMEM, SMEM, HBM] + [VMEM] * 4,
        out_specs=HBM,
        out_shape=jax.ShapeDtypeStruct(mid.shape, f32),
        input_output_aliases={2: 0},
        scratch_shapes=[
            pltpu.VMEM((NV, 2, T, T), f32),
            pltpu.SemaphoreType.DMA((NV,)),
        ],
        compiler_params=params(6 * MIB),
        cost_estimate=cost(2 << 20, 3 << 20),
        name="final",
    )(horiz, relax, mid, keep, imp, *imp_rows)


def shifted(block, axis, by):
    count = lax.axis_size(axis)
    return lax.ppermute(block, axis, [(i, (i + by) % count) for i in range(count)])


def crossed(block, gx_by=0):
    size = lax.axis_size("gx"), lax.axis_size("gy")
    route = []
    for c in range(2):
        for i in range(size[0]):
            for j in range(size[1]):
                to = (1 - c) * size[0] + (i + gx_by) % size[0]
                route.append(((c * size[0] + i) * size[1] + j, to * size[1] + (j ^ MIRROR)))
    return lax.ppermute(block, ("comp", "gx", "gy"), route)


def local(
    state, horiz_coef, vert_coef, couple_rate, sea_mask, dest_block, entry_count, remap_weight
):
    head, tail = outer_rows(state, vert_coef, sea_mask)
    top, bottom = shifted(tail, "gx", 1), shifted(head, "gx", -1)
    cols, surf, coef, sea = outer_columns(state, vert_coef, sea_mask)
    cols = with_corners(cols, top, bottom)
    left, right = shifted(cols, "gy", 1), shifted(cols, "gy", -1)
    dest = dest_block.reshape(T, FAN).T
    packed = remap(dest, entry_count.reshape(1, T), surf, remap_weight, cols)
    packed = sealed(packed, left, right).reshape(PEERS, SIZE, 1, T)
    packed = lax.all_to_all(packed, ("gx", "gy"), split_axis=0, concat_axis=0, tiled=True)
    mid, keep = two_steps(horiz_coef, state, coef, sea, cols, top, bottom, left, right)
    new, first, last = unpack(packed.reshape(PEERS * SIZE, T), keep)
    imp = crossed(new)
    imp_rows = crossed(last, 1), crossed(first, -1)
    return final(horiz_coef, couple_rate, mid, keep, imp, imp_rows)


def solution(mesh):
    in_specs = (
        P("comp", None, None, "gx", "gy"),
        P("comp", None),
        P("comp", "gx", "gy"),
        P("comp", None),
        P("comp", "gx", "gy"),
        P("comp", "gx", "gy", None),
        P("comp", "gx", "gy"),
        P("comp", "gx", "gy", None, None, None),
    )
    out_specs = P("comp", None, None, "gx", "gy")
    return jax.shard_map(local, mesh=mesh, in_specs=in_specs, out_specs=out_specs, check_vma=False)
```

```python
import jax
import jax.numpy as jnp
from jax import lax
from jax.experimental import pallas as pl
from jax.experimental.pallas import tpu as pltpu
from jax.sharding import PartitionSpec as P

NV = 4
LEV = 16
PLANES = NV * LEV
T = 128
FAN = 4
CAP = 8
PEERS = 64
SIZE = CAP * NV + 1
EDGE = 32
HALF = 64
CHUNKS = 16
MIRROR = 4
MIB = 1024 * 1024
LIMIT = 58 * MIB
ROW_VERT = 2 * PLANES
ROW_SEA = ROW_VERT + 8
ROW_SIZE = ROW_SEA + 8
COL_NEXT = T
COL_COEF = 2 * T
COL_TOP = COL_COEF + 8
COL_BOTTOM = COL_TOP + 8
COL_SIZE = COL_BOTTOM + 8
KEEP_BASE = 0
KEEP_ONE = NV * T
KEEP_PART = 2 * NV * T
KEEP_VERT = 3 * NV * T
KEEP_SEA = KEEP_VERT + T
KEEP_SIDE = KEEP_SEA + T
KEEP_SEA_SIDE = KEEP_SIDE + T
KEEP_ENDS = KEEP_SEA_SIDE + T
KEEP_SIZE = KEEP_ENDS + 16

f32 = jnp.float32
i32 = jnp.int32
bf16 = jnp.bfloat16

SMEM = pl.BlockSpec(memory_space=pltpu.SMEM)
VMEM = pl.BlockSpec(memory_space=pltpu.VMEM)
HBM = pl.BlockSpec(memory_space=pl.ANY)


def params(limit=LIMIT):
    return pltpu.CompilerParams(vmem_limit_bytes=limit)


def cost(flops, size):
    return pl.CostEstimate(flops=flops, bytes_accessed=size, transcendentals=0)


def lanes(rows):
    return lax.broadcasted_iota(i32, (rows, T), 1)


def subl(rows):
    return lax.broadcasted_iota(i32, (rows, T), 0)


def inside():
    gx, gy = lax.axis_index("gx"), lax.axis_index("gy")
    one = lambda test: jnp.where(test, 1.0, 0.0).astype(f32)
    return (
        one(gx > 0),
        one(gx < lax.axis_size("gx") - 1),
        one(gy > 0),
        one(gy < lax.axis_size("gy") - 1),
    )


def column_keep(rows, later=0):
    _, _, before, after = inside()
    return jnp.where((lanes(rows) & 1) == later, after, before)


def run(copies):
    for copy in copies:
        copy.start()
    for copy in copies:
        copy.wait()


def row_kernel(state, vert, mask, head, tail, high, low, coef, sea, sems):
    ends = pl.ds(0, 8), pl.ds(T - 8, 8)
    copies = []
    for k, buffer in enumerate((high, low)):
        copies.append(pltpu.make_async_copy(state.at[0, :, :, ends[k]], buffer, sems.at[3 * k]))
        copies.append(pltpu.make_async_copy(vert.at[0, ends[k]], coef.at[k], sems.at[3 * k + 1]))
        copies.append(pltpu.make_async_copy(mask.at[0, ends[k]], sea.at[k], sems.at[3 * k + 2]))
    run(copies)
    up, down, _, _ = inside()
    for k, (out, buffer, keep) in enumerate(((head, high, up), (tail, low, down))):
        outer, following = (0, 1) if k == 0 else (7, 6)
        flat = buffer.reshape(PLANES * 8, T)
        out[0:PLANES, :] = flat[pl.ds(outer, PLANES, stride=8), :] * keep
        out[PLANES : 2 * PLANES, :] = flat[pl.ds(following, PLANES, stride=8), :] * keep
        line = coef[k, outer : outer + 1, :] * keep
        out[ROW_VERT : ROW_VERT + 8, :] = jnp.broadcast_to(line, (8, T))
        line = sea[k, outer : outer + 1, :].astype(f32) * keep
        out[ROW_SEA : ROW_SEA + 8, :] = jnp.broadcast_to(line, (8, T))


def outer_rows(state, vert, mask):
    return pl.pallas_call(
        row_kernel,
        in_specs=[HBM, HBM, HBM],
        out_specs=[VMEM, VMEM],
        out_shape=[jax.ShapeDtypeStruct((ROW_SIZE, T), f32)] * 2,
        scratch_shapes=[
            pltpu.VMEM((NV, LEV, 8, T), f32),
            pltpu.VMEM((NV, LEV, 8, T), f32),
            pltpu.VMEM((2, 8, T), f32),
            pltpu.VMEM((2, 8, T), i32),
            pltpu.SemaphoreType.DMA((6,)),
        ],
        compiler_params=params(),
        cost_estimate=cost(1 << 16, 1 << 19),
        name="outer_rows",
    )(state, vert, mask)


def column_kernel(state, vert, mask, cols, surf, coef, wet, tile, sea, sems):
    loads = [pltpu.make_async_copy(state.at[0, v], tile.at[v], sems.at[v]) for v in range(NV)]
    loads.append(pltpu.make_async_copy(vert.at[0], coef, sems.at[NV]))
    loads.append(pltpu.make_async_copy(mask.at[0], sea, sems.at[NV + 1]))
    for load in loads:
        load.start()
    lane = lanes(HALF)
    keep = column_keep(HALF)
    keep2 = column_keep(HALF, 1)
    for v in range(NV):
        loads[v].wait()
        surf[pl.ds(v, T, stride=NV), :] = tile[v, 0]
        for lo in range(0, T, HALF):
            outer, following = pl.ds(lo, HALF), pl.ds(COL_NEXT + lo, HALF)
            acc = jnp.zeros((HALF, T), f32) if v == 0 else cols[outer, :]
            acc2 = jnp.zeros((HALF, T), f32) if v == 0 else cols[following, :]
            for l in range(LEV):
                p = v * LEV + l
                plane = tile[v, l, lo : lo + HALF, :]
                turned = pltpu.roll(plane, (2 * p + 1) % T, 1)
                acc = jnp.where((lane >> 1) == p, turned, acc)
                acc2 = jnp.where((lane == (2 * p - 1) % T) | (lane == (2 * p + 2) % T), turned, acc2)
            last = v == NV - 1
            cols[outer, :] = acc * keep if last else acc
            cols[following, :] = acc2 * keep2 if last else acc2
    loads[NV].wait()
    loads[NV + 1].wait()
    lane = lanes(T)
    wet[...] = sea[...].astype(f32)
    pair = jnp.where(lane < 2, pltpu.roll(coef[...], 1, 1), pltpu.roll(wet[...], 3, 1))
    cols[COL_COEF : COL_COEF + 8, :] = jnp.transpose(pair * column_keep(T))[0:8, :]


def outer_columns(state, vert, mask):
    square = jax.ShapeDtypeStruct((T, T), f32)
    return pl.pallas_call(
        column_kernel,
        in_specs=[HBM, HBM, HBM],
        out_specs=[VMEM] * 4,
        out_shape=[
            jax.ShapeDtypeStruct((COL_TOP, T), f32),
            jax.ShapeDtypeStruct((T * NV, T), f32),
            square,
            square,
        ],
        scratch_shapes=[
            pltpu.VMEM((NV, LEV, T, T), f32),
            pltpu.VMEM((T, T), i32),
            pltpu.SemaphoreType.DMA((NV + 2,)),
        ],
        compiler_params=params(51 * MIB),
        cost_estimate=cost(6 << 20, 9 << 20),
        name="outer_columns",
    )(state, vert, mask)


def corner_kernel(cols, top, bottom, out):
    out[0:COL_TOP, :] = cols[...]
    lane, sub = lanes(PLANES), subl(PLANES)
    keep = column_keep(PLANES)
    for k, rows in enumerate((top, bottom)):
        line = rows[0:PLANES, :]
        first = jnp.broadcast_to(line[:, 0:1], (PLANES, T))
        last = jnp.broadcast_to(line[:, T - 1 : T], (PLANES, T))
        spread = jnp.where(lane == 2 * sub, last, jnp.where(lane == 2 * sub + 1, first, 0.0))
        total = jnp.sum(spread * keep, axis=0, keepdims=True)
        at = COL_TOP + 8 * k
        out[at : at + 8, :] = jnp.broadcast_to(total, (8, T))


def with_corners(cols, top, bottom):
    return pl.pallas_call(
        corner_kernel,
        in_specs=[VMEM] * 3,
        out_specs=VMEM,
        out_shape=jax.ShapeDtypeStruct((COL_SIZE, T), f32),
        compiler_params=params(4 * MIB),
        cost_estimate=cost(1 << 16, 1 << 18),
        name="with_corners",
    )(cols, top, bottom)


def remap_kernel(
    dest_in, count_in, surf, weight, after, out, blocks, buffer, names, dest, count, used, label, sems
):
    del after
    rows = T // CHUNKS
    lists = [
        pltpu.make_async_copy(dest_in, dest, sems.at[CHUNKS]),
        pltpu.make_async_copy(count_in, count, sems.at[CHUNKS + 1]),
    ]
    for copy in lists:
        copy.start()

    def fetch(c):
        piece = pl.ds(c * rows, rows)
        return pltpu.make_async_copy(weight.at[0, piece, 0], blocks.at[piece], sems.at[c])

    for c in range(CHUNKS):
        fetch(c).start()
    buffer[...] = jnp.zeros_like(buffer)

    def clear(i, _):
        row = (i ^ MIRROR) * SIZE
        used[i] = row
        for k in range(CAP):
            label[row + k * NV] = 0
        return 0

    lax.fori_loop(0, PEERS, clear, 0)
    for copy in lists:
        copy.wait()
    sub = subl(8)

    def place_of(row, f):
        target = dest[f, row]
        device = lax.shift_right_logical(target, 7) & (PEERS - 1)
        live = f < count[0, row]
        at = used[device]
        used[device] = jnp.where(live, at + NV, at)
        place = jnp.where(live, at, PEERS * SIZE)
        label[place] = (target & (T - 1)) + 1
        return place

    def chunk(c, _):
        fetch(c).wait()
        for r in range(0, rows, 2):
            row = c * rows + r
            places = [[place_of(row + q, f) for f in range(FAN)] for q in range(2)]
            pair = surf[pl.ds(pl.multiple_of(row * NV, 8), 8), :]
            pair = jnp.concatenate(
                [jnp.where(sub < NV, pair, 0.0), jnp.where(sub >= NV, pair, 0.0)], axis=1
            ).astype(bf16)
            for f in range(0, FAN, 2):
                block = jnp.concatenate(
                    [
                        jnp.concatenate([blocks[row + q, f], blocks[row + q, f + 1]], axis=1)
                        for q in range(2)
                    ],
                    axis=0,
                )
                product = jnp.dot(pair, block, preferred_element_type=f32)
                for q in range(2):
                    for g in range(2):
                        part = product[q * NV : (q + 1) * NV, g * T : (g + 1) * T]
                        buffer[pl.ds(places[q][f + g], NV), :] = part
        return 0

    lax.fori_loop(0, CHUNKS, chunk, 0)
    lane = lanes(1)

    def name(i, _):
        line = jnp.zeros((1, T), i32)
        for k in range(CAP):
            line = jnp.where(lane == k, label[i * SIZE + k * NV], line)
        names[pl.ds(i, 1), :] = line.astype(f32)
        return 0

    lax.fori_loop(0, PEERS, name, 0, unroll=8)
    lane = lanes(PEERS)
    rims = jnp.zeros((PEERS, T), f32)
    for j in range(CAP * NV):
        column = EDGE + 2 * j
        turned = pltpu.roll(buffer[pl.ds(j, PEERS, stride=SIZE), :], (column + 1) % T, 1)
        rims = jnp.where((lane >> 1) == column >> 1, turned, rims)
    lane, sub = lanes(8), subl(8)
    left_end, right_end = sub == MIRROR, sub == MIRROR - 1
    for b in range(PEERS // 8):
        own, rim = names[b * 8 : b * 8 + 8, :], rims[b * 8 : b * 8 + 8, :]
        left_name, left_rim = (jnp.where(left_end, 0.0, pltpu.roll(x, 1, 0)) for x in (own, rim))
        right_name, right_rim = (jnp.where(right_end, 0.0, pltpu.roll(x, 7, 0)) for x in (own, rim))
        line = own + pltpu.roll(left_name, CAP, 1) + pltpu.roll(right_name, 2 * CAP, 1)
        line = line + jnp.where((lane & 1) == 0, left_rim, right_rim)
        buffer[pl.ds(b * 8 * SIZE + SIZE - 1, 8, stride=SIZE), :] = line
    run([pltpu.make_async_copy(buffer.at[pl.ds(0, PEERS * SIZE)], out, sems.at[0])])


def remap(dest, count, surf, weight, after):
    return pl.pallas_call(
        remap_kernel,
        in_specs=[HBM, HBM, VMEM, HBM, HBM],
        out_specs=HBM,
        out_shape=jax.ShapeDtypeStruct((PEERS * SIZE, T), f32),
        scratch_shapes=[
            pltpu.VMEM((T, FAN, T, T), bf16),
            pltpu.VMEM((PEERS * SIZE + 8, T), f32),
            pltpu.VMEM((PEERS, T), f32),
            pltpu.SMEM((FAN, T), i32),
            pltpu.SMEM((1, T), i32),
            pltpu.SMEM((PEERS,), i32),
            pltpu.SMEM((PEERS * SIZE + 8,), i32),
            pltpu.SemaphoreType.DMA((CHUNKS + 2,)),
        ],
        compiler_params=params(44 * MIB),
        cost_estimate=cost(67 << 20, 20 << 20),
        name="remap",
    )(dest, count, surf, weight, after)


def sealed(block, *after):
    def kernel(*refs):
        del refs

    return pl.pallas_call(
        kernel,
        in_specs=[HBM] * (1 + len(after)),
        out_specs=HBM,
        out_shape=jax.ShapeDtypeStruct(block.shape, block.dtype),
        input_output_aliases={0: 0},
        compiler_params=params(MIB),
        name="sealed",
    )(block, *after)


def merged(left, right, back=2):
    return jnp.where((lanes(left.shape[0]) & 1) == 0, left, pltpu.roll(right, T - back, 1))


def diffuse(u, up, down, side, rate):
    rows = u.shape[0]
    lane, sub = lanes(rows), subl(rows)
    north = jnp.where(sub == 0, up, pltpu.roll(u, 1, 0))
    south = jnp.where(sub == rows - 1, down, pltpu.roll(u, rows - 1, 0))
    west = jnp.where(lane == 0, side, pltpu.roll(u, 1, 1))
    east = jnp.where(lane == T - 1, side, pltpu.roll(u, T - 1, 1))
    return u + rate * ((north + south) + (west + east) - 4.0 * u)


def level_diffuse(u, top, bottom, side, rate, l, lo):
    up = top[l : l + 1, :] if lo == 0 else u[l, lo - 1 : lo, :]
    down = bottom[l : l + 1, :] if lo + HALF == T else u[l, lo + HALF : lo + HALF + 1, :]
    spin = side[lo : lo + HALF, :]
    if l:
        spin = pltpu.roll(spin, T - 2 * l, 1)
    return diffuse(u[l, lo : lo + HALF, :], up, down, spin, rate)


def halo_columns(rate, left, right, sides, own):
    lane, sub = lanes(T), subl(T)
    here = merged(left[0:T, :], right[0:T, :])
    outer = merged(pltpu.roll(left[COL_NEXT : COL_NEXT + T, :], 1, 1), right[COL_NEXT : COL_NEXT + T, :], 3)
    inner = pltpu.roll(own[0:T, :], T - 1, 1)
    ends = [merged(left[at : at + 8, :], right[at : at + 8, :])[0:1, :] for at in (COL_TOP, COL_BOTTOM)]
    north = jnp.where(sub == 0, ends[0], pltpu.roll(here, 1, 0))
    south = jnp.where(sub == T - 1, ends[1], pltpu.roll(here, T - 1, 0))
    plane = ((lane + 1) >> 1) & (PLANES - 1)
    number = jnp.full((T, T), rate[0, 0], f32)
    for v in range(1, NV):
        number = jnp.where(plane // LEV == v, rate[0, v], number)
    h = here + number * ((north + south) + (outer + inner) - 4.0 * here)
    coef = jnp.where(
        (lane & 1) == 0,
        jnp.broadcast_to(sides[0][:, 0:1], (T, T)),
        jnp.broadcast_to(sides[1][:, 1:2], (T, T)),
    )
    level = plane % LEV
    above = jnp.where(level < LEV - 1, pltpu.roll(h, T - 2, 1) - h, 0.0)
    below = jnp.where(level > 0, pltpu.roll(h, 2, 1) - h, 0.0)
    return here, h + coef * (above + below)


def halo_rows(rate, rows, own, left, right, k, v):
    at = v * LEV
    lane, level = lanes(LEV), subl(LEV)
    here = rows[at : at + LEV, :]
    edge = COL_TOP + 8 * k

    def corner(message, later):
        line = jnp.broadcast_to(message[edge : edge + 1, :], (LEV, T))
        return jnp.sum(jnp.where(lane == 2 * (at + level) + later, line, 0.0), axis=1, keepdims=True)

    west = jnp.where(lane == 0, corner(left, 0), pltpu.roll(here, 1, 1))
    east = jnp.where(lane == T - 1, corner(right, 1), pltpu.roll(here, T - 1, 1))
    outer = rows[PLANES + at : PLANES + at + LEV, :]
    inner = own[at : at + LEV, :]
    h = here + rate[0, v] * ((outer + inner) + (west + east) - 4.0 * here)
    above = jnp.where(level < LEV - 1, pltpu.roll(h, LEV - 1, 0) - h, 0.0)
    below = jnp.where(level > 0, pltpu.roll(h, 1, 0) - h, 0.0)
    return h + rows[ROW_VERT : ROW_VERT + 1, :] * (above + below)


def step_kernel(
    rate, state, coef, sea, own, top, bottom, near, far,
    out, keep, u, w, stage, inner, top1, bottom1, top2, bottom2, side1, side2, turned, sems,
):
    def emit(v):
        levels = pl.ds(2, LEV - 2)
        return pltpu.make_async_copy(stage.at[v], out.at[0, v, levels], sems.at[v])

    loads = [pltpu.make_async_copy(state.at[0, v], u.at[v], sems.at[v]) for v in range(NV)]
    for load in loads:
        load.start()
    up, down, _, _ = inside()
    rest = jnp.zeros((T - 8, T), f32)
    sides = [
        jnp.transpose(jnp.concatenate([x[COL_COEF : COL_COEF + 8, :], rest], axis=0))
        for x in (near, far)
    ]
    side1[...], side2[...] = halo_columns(rate, near, far, sides, own)
    keep[KEEP_SEA_SIDE : KEEP_SEA_SIDE + T, :] = jnp.where(
        lanes(T) == 0, pltpu.roll(sides[0], T - 2, 1), pltpu.roll(sides[1], T - 4, 1)
    )
    for v in range(NV):
        loads[v].wait()
        at = v * LEV
        for l in range(LEV):
            inner[0, at + l : at + l + 1, :] = u[v, l, 0:1, :] * up
            inner[1, at + l : at + l + 1, :] = u[v, l, T - 1 : T, :] * down
    for v in range(NV):
        at = v * LEV
        top1[v] = top[at : at + LEV, :]
        bottom1[v] = bottom[at : at + LEV, :]
        top2[v] = halo_rows(rate, top, inner.at[0], near, far, 0, v)
        bottom2[v] = halo_rows(rate, bottom, inner.at[1], near, far, 1, v)

    def first(v, _):
        number = rate[0, v]
        turned[...] = pltpu.roll(side1[...], lax.rem((NV - v) * 32, T), 1)
        source, result = u.at[v], w.at[v]
        for lo in range(0, T, HALF):
            mix = coef[lo : lo + HALF, :]
            at = lambda l: level_diffuse(source, top1.at[v], bottom1.at[v], turned, number, l, lo)
            before, here = None, at(0)
            for l in range(LEV):
                after = at(l + 1) if l + 1 < LEV else None
                if before is None:
                    term = after - here
                elif after is None:
                    term = before - here
                else:
                    term = (after - here) + (before - here)
                result[l, lo : lo + HALF, :] = here + mix * term
                before, here = here, after
        return 0

    lax.fori_loop(0, NV, first, 0)

    def second(v, _):
        number = rate[0, v]
        turned[...] = pltpu.roll(side2[...], lax.rem((NV - v) * 32, T), 1)
        source, result = w.at[v], stage.at[v]
        for lo in range(0, T, HALF):
            mix = coef[lo : lo + HALF, :]
            at = lambda l: level_diffuse(source, top2.at[v], bottom2.at[v], turned, number, l, lo)
            before, here = at(1), at(2)
            row = pl.multiple_of(v * T + lo, 8)
            keep[pl.ds(KEEP_BASE + row, HALF), :] = source[0, lo : lo + HALF, :]
            keep[pl.ds(KEEP_ONE + row, HALF), :] = before
            keep[pl.ds(KEEP_PART + row, HALF), :] = before + mix * ((here - before) - before)
            for l in range(2, LEV):
                after = at(l + 1) if l + 1 < LEV else None
                term = before - here
                if after is not None:
                    term = (after - here) + term
                result[l - 2, lo : lo + HALF, :] = here + mix * term
                before, here = here, after
        emit(v).start()
        return 0

    lax.fori_loop(0, NV, second, 0)
    keep[KEEP_VERT : KEEP_VERT + T, :] = coef[...]
    keep[KEEP_SEA : KEEP_SEA + T, :] = sea[...]
    keep[KEEP_SIDE : KEEP_SIDE + T, :] = side2[...]
    for k, (rows, line) in enumerate(((top2, top), (bottom2, bottom))):
        for v in range(NV):
            keep[KEEP_ENDS + 8 * k + v : KEEP_ENDS + 8 * k + v + 1, :] = rows[v, 0:1, :]
        keep[KEEP_ENDS + 8 * k + NV : KEEP_ENDS + 8 * k + 8, :] = line[ROW_SEA : ROW_SEA + NV, :]
    for v in range(NV):
        emit(v).wait()


def two_steps(rate, state, coef, sea, own, top, bottom, left, right):
    rows = pltpu.VMEM((NV, LEV, T), f32)
    square = pltpu.VMEM((T, T), f32)
    return pl.pallas_call(
        step_kernel,
        in_specs=[SMEM, HBM] + [VMEM] * 7,
        out_specs=[HBM, VMEM],
        out_shape=[
            jax.ShapeDtypeStruct(state.shape, f32),
            jax.ShapeDtypeStruct((KEEP_SIZE, T), f32),
        ],
        scratch_shapes=[
            pltpu.VMEM((NV, LEV, T, T), f32),
            pltpu.VMEM((NV, LEV, T, T), f32),
            pltpu.VMEM((NV, LEV - 2, T, T), f32),
            pltpu.VMEM((2, PLANES, T), f32),
            rows,
            rows,
            rows,
            rows,
            square,
            square,
            square,
            pltpu.SemaphoreType.DMA((NV,)),
        ],
        compiler_params=params(20 * MIB),
        cost_estimate=cost(48 << 20, 10 << 20),
        name="two_steps",
    )(rate, state, coef, sea, own, top, bottom, left, right)


def unpack_kernel(data, after, imp, first, last):
    del after
    sub = subl(T).astype(f32) + 1.0
    line = data[pl.ds(SIZE - 1, PEERS, stride=SIZE), :]
    fields = jnp.transpose(jnp.concatenate([line, jnp.zeros((T - PEERS, T), f32)], axis=0))

    def two(at, size):
        return fields[at : at + size, :] + pltpu.roll(fields[at + size : at + 2 * size, :], PEERS, 1)

    def split(x):
        high = x.astype(bf16)
        return high, (x - high.astype(f32)).astype(bf16)

    def picks(at):
        return jnp.concatenate(
            [(sub == two(at + k, 1)).astype(bf16) for k in range(0, CAP, 2)], axis=1
        )

    pick = picks(0)
    up, down, _, _ = inside()
    for v in range(NV):
        block = jnp.concatenate(
            [data[pl.ds(k * NV + v, PEERS, stride=SIZE), :] for k in range(CAP)], axis=0
        )
        high, low = split(block)
        total = jnp.dot(pick, high, preferred_element_type=f32)
        total = total + jnp.dot(pick, low, preferred_element_type=f32)
        imp[v * T : (v + 1) * T, :] = total
        for out, row, keep in ((first, 0, up), (last, T - 1, down)):
            out[v : v + 1, :] = total[row : row + 1, :] * keep
            out[NV + v : NV + v + 1, :] = total[row : row + 1, :] * keep
    rims = jnp.concatenate([two(EDGE + 8 * k, 8) for k in range(0, CAP, 2)], axis=1)
    sides = []
    for at in (CAP, 2 * CAP):
        pick = picks(at)
        high, low = (
            lax.dot_general(part, pick, (((1,), (1,)), ((), ())), preferred_element_type=f32)
            for part in split(rims)
        )
        sides.append(high + low)
    imp[NV * T : NV * T + 8, :] = jnp.where((subl(8) & 1) == 0, sides[0], sides[1])


def unpack(data, after):
    return pl.pallas_call(
        unpack_kernel,
        in_specs=[VMEM, HBM],
        out_specs=[VMEM] * 3,
        out_shape=[
            jax.ShapeDtypeStruct((NV * T + 8, T), f32),
            jax.ShapeDtypeStruct((2 * NV, T), f32),
            jax.ShapeDtypeStruct((2 * NV, T), f32),
        ],
        compiler_params=params(12 * MIB),
        cost_estimate=cost(200 << 20, 2 << 20),
        name="unpack",
    )(data, after)


def final_kernel(
    horiz, relax, mid, near, imp, imp_top, imp_bottom, out, stage, sems
):
    del mid
    ends = jnp.concatenate([imp[NV * T : NV * T + 8, :], jnp.zeros((T - 8, T), f32)], axis=0)
    side_new = jnp.transpose(ends)
    sea, sea_side = near[KEEP_SEA : KEEP_SEA + T, :], near[KEEP_SEA_SIDE : KEEP_SEA_SIDE + T, :]
    coef = near[KEEP_VERT : KEEP_VERT + T, :]
    side_base = near[KEEP_SIDE : KEEP_SIDE + T, :]
    lane = lanes(T)
    copies = []
    for v in range(NV):
        pull = relax[0, v]

        def relaxed(base, wet, new, pull=pull):
            return base + pull * wet * (new - base)

        ends = []
        for k, new in enumerate((imp_top, imp_bottom)):
            at = KEEP_ENDS + 8 * k
            ends.append(
                relaxed(near[at + v : at + v + 1, :], near[at + NV : at + NV + 1, :], new[v : v + 1, :])
            )
        turn = (T - 32 * v) % T
        base = pltpu.roll(side_base, turn, 1) if turn else side_base
        new = pltpu.roll(side_new, T - 2 * v, 1) if v else side_new
        new = jnp.where(lane == 0, new, pltpu.roll(side_new, T - 2 - 2 * v, 1))
        mine = imp[v * T : (v + 1) * T, :]
        u = relaxed(near[KEEP_BASE + v * T : KEEP_BASE + (v + 1) * T, :], sea, mine)
        h = diffuse(u, ends[0], ends[1], relaxed(base, sea_side, new), horiz[0, v])
        one = near[KEEP_ONE + v * T : KEEP_ONE + (v + 1) * T, :]
        stage[v, 0] = relaxed(h + coef * (one - h), sea, mine)
        stage[v, 1] = near[KEEP_PART + v * T : KEEP_PART + (v + 1) * T, :] + coef * h
        copies.append(
            pltpu.make_async_copy(stage.at[v], out.at[0, v, pl.ds(0, 2)], sems.at[v])
        )
        copies[-1].start()
    for copy in copies:
        copy.wait()


def final(horiz, relax, mid, keep, imp, imp_rows):
    return pl.pallas_call(
        final_kernel,
        in_specs=[SMEM, SMEM, HBM] + [VMEM] * 4,
        out_specs=HBM,
        out_shape=jax.ShapeDtypeStruct(mid.shape, f32),
        input_output_aliases={2: 0},
        scratch_shapes=[
            pltpu.VMEM((NV, 2, T, T), f32),
            pltpu.SemaphoreType.DMA((NV,)),
        ],
        compiler_params=params(6 * MIB),
        cost_estimate=cost(2 << 20, 3 << 20),
        name="final",
    )(horiz, relax, mid, keep, imp, *imp_rows)


def shifted(block, axis, by):
    count = lax.axis_size(axis)
    return lax.ppermute(block, axis, [(i, (i + by) % count) for i in range(count)])


def crossed(block, gx_by=0):
    size = lax.axis_size("gx"), lax.axis_size("gy")
    route = []
    for c in range(2):
        for i in range(size[0]):
            for j in range(size[1]):
                to = (1 - c) * size[0] + (i + gx_by) % size[0]
                route.append(((c * size[0] + i) * size[1] + j, to * size[1] + (j ^ MIRROR)))
    return lax.ppermute(block, ("comp", "gx", "gy"), route)


def local(
    state, horiz_coef, vert_coef, couple_rate, sea_mask, dest_block, entry_count, remap_weight
):
    head, tail = outer_rows(state, vert_coef, sea_mask)
    top, bottom = shifted(tail, "gx", 1), shifted(head, "gx", -1)
    cols, surf, coef, sea = outer_columns(state, vert_coef, sea_mask)
    cols = with_corners(cols, top, bottom)
    left, right = shifted(cols, "gy", 1), shifted(cols, "gy", -1)
    dest = dest_block.reshape(T, FAN).T
    packed = remap(dest, entry_count.reshape(1, T), surf, remap_weight, cols)
    packed = sealed(packed, left, right).reshape(PEERS, SIZE, 1, T)
    packed = lax.all_to_all(packed, ("gx", "gy"), split_axis=0, concat_axis=0, tiled=True)
    mid, keep = two_steps(horiz_coef, state, coef, sea, cols, top, bottom, left, right)
    new, first, last = unpack(packed.reshape(PEERS * SIZE, T), keep)
    imp = crossed(new)
    imp_rows = crossed(last, 1), crossed(first, -1)
    return final(horiz_coef, couple_rate, mid, keep, imp, imp_rows)


def solution(mesh):
    in_specs = (
        P("comp", None, None, "gx", "gy"),
        P("comp", None),
        P("comp", "gx", "gy"),
        P("comp", None),
        P("comp", "gx", "gy"),
        P("comp", "gx", "gy", None),
        P("comp", "gx", "gy"),
        P("comp", "gx", "gy", None, None, None),
    )
    out_specs = P("comp", None, None, "gx", "gy")
    return jax.shard_map(local, mesh=mesh, in_specs=in_specs, out_specs=out_specs, check_vma=False)
```

```python
import jax
import jax.numpy as jnp
from jax import lax
from jax.experimental import pallas as pl
from jax.experimental.pallas import tpu as pltpu
from jax.sharding import PartitionSpec as P

NV = 4
LEV = 16
PLANES = NV * LEV
T = 128
FAN = 4
CAP = 8
PEERS = 64
SIZE = CAP * NV + 1
EDGE = 32
HALF = 64
CHUNKS = 16
EARLY = 32
MIRROR = 4
MIB = 1024 * 1024
LIMIT = 58 * MIB
ROW_VERT = 2 * PLANES
ROW_SEA = ROW_VERT + 8
ROW_SIZE = ROW_SEA + 8
COL_NEXT = T
COL_COEF = 2 * T
COL_TOP = 3 * T
COL_BOTTOM = COL_TOP + 8
COL_SIZE = COL_BOTTOM + 8
KEEP_BASE = 0
KEEP_ONE = NV * T
KEEP_PART = 2 * NV * T
KEEP_VERT = 3 * NV * T
KEEP_SEA = KEEP_VERT + T
KEEP_SIDE = KEEP_SEA + T
KEEP_SEA_SIDE = KEEP_SIDE + T
KEEP_ENDS = KEEP_SEA_SIDE + T
KEEP_SIZE = KEEP_ENDS + 16

f32 = jnp.float32
i32 = jnp.int32
bf16 = jnp.bfloat16

SMEM = pl.BlockSpec(memory_space=pltpu.SMEM)
VMEM = pl.BlockSpec(memory_space=pltpu.VMEM)
HBM = pl.BlockSpec(memory_space=pl.ANY)


def params(limit=LIMIT):
    return pltpu.CompilerParams(vmem_limit_bytes=limit)


def cost(flops, size):
    return pl.CostEstimate(flops=flops, bytes_accessed=size, transcendentals=0)


def lanes(rows):
    return lax.broadcasted_iota(i32, (rows, T), 1)


def subl(rows):
    return lax.broadcasted_iota(i32, (rows, T), 0)


def inside():
    gx, gy = lax.axis_index("gx"), lax.axis_index("gy")
    one = lambda test: jnp.where(test, 1.0, 0.0).astype(f32)
    return (
        one(gx > 0),
        one(gx < lax.axis_size("gx") - 1),
        one(gy > 0),
        one(gy < lax.axis_size("gy") - 1),
    )


def column_keep(rows, later=0):
    _, _, before, after = inside()
    return jnp.where((lanes(rows) & 1) == later, after, before)


def run(copies):
    for copy in copies:
        copy.start()
    for copy in copies:
        copy.wait()


def row_kernel(state, vert, mask, head, tail, high, low, coef, sea, sems):
    ends = pl.ds(0, 8), pl.ds(T - 8, 8)
    copies = []
    for k, buffer in enumerate((high, low)):
        copies.append(pltpu.make_async_copy(state.at[0, :, :, ends[k]], buffer, sems.at[3 * k]))
        copies.append(pltpu.make_async_copy(vert.at[0, ends[k]], coef.at[k], sems.at[3 * k + 1]))
        copies.append(pltpu.make_async_copy(mask.at[0, ends[k]], sea.at[k], sems.at[3 * k + 2]))
    run(copies)
    up, down, _, _ = inside()
    for k, (out, buffer, keep) in enumerate(((head, high, up), (tail, low, down))):
        outer, following = (0, 1) if k == 0 else (7, 6)
        flat = buffer.reshape(PLANES * 8, T)
        out[0:PLANES, :] = flat[pl.ds(outer, PLANES, stride=8), :] * keep
        out[PLANES : 2 * PLANES, :] = flat[pl.ds(following, PLANES, stride=8), :] * keep
        line = coef[k, outer : outer + 1, :] * keep
        out[ROW_VERT : ROW_VERT + 8, :] = jnp.broadcast_to(line, (8, T))
        line = sea[k, outer : outer + 1, :].astype(f32) * keep
        out[ROW_SEA : ROW_SEA + 8, :] = jnp.broadcast_to(line, (8, T))


def outer_rows(state, vert, mask):
    return pl.pallas_call(
        row_kernel,
        in_specs=[HBM, HBM, HBM],
        out_specs=[VMEM, VMEM],
        out_shape=[jax.ShapeDtypeStruct((ROW_SIZE, T), f32)] * 2,
        scratch_shapes=[
            pltpu.VMEM((NV, LEV, 8, T), f32),
            pltpu.VMEM((NV, LEV, 8, T), f32),
            pltpu.VMEM((2, 8, T), f32),
            pltpu.VMEM((2, 8, T), i32),
            pltpu.SemaphoreType.DMA((6,)),
        ],
        compiler_params=params(),
        cost_estimate=cost(1 << 16, 1 << 19),
        name="outer_rows",
    )(state, vert, mask)


def column_kernel(state, vert, mask, weight, cols, surf, coef, wet, early, tile, sea, sems):
    loads = [pltpu.make_async_copy(state.at[0, v], tile.at[v], sems.at[v]) for v in range(NV)]
    loads.append(pltpu.make_async_copy(vert.at[0], coef, sems.at[NV]))
    loads.append(pltpu.make_async_copy(mask.at[0], sea, sems.at[NV + 1]))
    loads.append(pltpu.make_async_copy(weight.at[0, pl.ds(0, EARLY), 0], early, sems.at[NV + 2]))
    for load in loads:
        load.start()
    lane = lanes(HALF)
    keep = column_keep(HALF)
    keep2 = column_keep(HALF, 1)
    for v in range(NV):
        loads[v].wait()
        surf[pl.ds(v, T, stride=NV), :] = tile[v, 0]
        for lo in range(0, T, HALF):
            outer, following = pl.ds(lo, HALF), pl.ds(COL_NEXT + lo, HALF)
            acc = jnp.zeros((HALF, T), f32) if v == 0 else cols[outer, :]
            acc2 = jnp.zeros((HALF, T), f32) if v == 0 else cols[following, :]
            for l in range(LEV):
                p = v * LEV + l
                plane = tile[v, l, lo : lo + HALF, :]
                turned = pltpu.roll(plane, (2 * p + 1) % T, 1)
                acc = jnp.where((lane >> 1) == p, turned, acc)
                acc2 = jnp.where((lane == (2 * p - 1) % T) | (lane == (2 * p + 2) % T), turned, acc2)
            last = v == NV - 1
            cols[outer, :] = acc * keep if last else acc
            cols[following, :] = acc2 * keep2 if last else acc2
    loads[NV].wait()
    loads[NV + 1].wait()
    lane = lanes(T)
    wet[...] = sea[...].astype(f32)
    pair = jnp.where(lane < 2, pltpu.roll(coef[...], 1, 1), pltpu.roll(wet[...], 3, 1))
    cols[COL_COEF : COL_COEF + T, :] = pair * column_keep(T)
    loads[NV + 2].wait()


def outer_columns(state, vert, mask, weight):
    square = jax.ShapeDtypeStruct((T, T), f32)
    return pl.pallas_call(
        column_kernel,
        in_specs=[HBM] * 4,
        out_specs=[VMEM] * 5,
        out_shape=[
            jax.ShapeDtypeStruct((COL_TOP, T), f32),
            jax.ShapeDtypeStruct((T * NV, T), f32),
            square,
            square,
            jax.ShapeDtypeStruct((EARLY, FAN, T, T), bf16),
        ],
        scratch_shapes=[
            pltpu.VMEM((NV, LEV, T, T), f32),
            pltpu.VMEM((T, T), i32),
            pltpu.SemaphoreType.DMA((NV + 3,)),
        ],
        compiler_params=params(46 * MIB),
        cost_estimate=cost(6 << 20, 9 << 20),
        name="outer_columns",
    )(state, vert, mask, weight)


def corner_kernel(cols, top, bottom, out):
    out[0:COL_COEF, :] = cols[0:COL_COEF, :]
    lane, sub = lanes(PLANES), subl(PLANES)
    keep = column_keep(PLANES)
    for k, rows in enumerate((top, bottom)):
        line = rows[0:PLANES, :]
        at = COL_COEF + k * PLANES
        out[at : at + PLANES, :] = jnp.where(
            (lane == 4) | (lane == 5), pltpu.roll(line, 5, 1) * keep, cols[at : at + PLANES, :]
        )
        first = jnp.broadcast_to(line[:, 0:1], (PLANES, T))
        last = jnp.broadcast_to(line[:, T - 1 : T], (PLANES, T))
        spread = jnp.where(lane == 2 * sub, last, jnp.where(lane == 2 * sub + 1, first, 0.0))
        total = jnp.sum(spread * keep, axis=0, keepdims=True)
        at = COL_TOP + 8 * k
        out[at : at + 8, :] = jnp.broadcast_to(total, (8, T))


def with_corners(cols, top, bottom):
    return pl.pallas_call(
        corner_kernel,
        in_specs=[VMEM] * 3,
        out_specs=VMEM,
        out_shape=jax.ShapeDtypeStruct((COL_SIZE, T), f32),
        compiler_params=params(4 * MIB),
        cost_estimate=cost(1 << 16, 1 << 18),
        name="with_corners",
    )(cols, top, bottom)


def remap_kernel(
    dest_in, count_in, surf, weight, early, after, out, blocks, buffer, names, dest, count, used, label, sems
):
    del after
    rows = T // CHUNKS
    lists = [
        pltpu.make_async_copy(dest_in, dest, sems.at[CHUNKS]),
        pltpu.make_async_copy(count_in, count, sems.at[CHUNKS + 1]),
    ]
    for copy in lists:
        copy.start()

    def fetch(c):
        piece = pl.ds(c * rows, rows)
        there = pl.ds(c * rows - EARLY, rows)
        return pltpu.make_async_copy(weight.at[0, piece, 0], blocks.at[there], sems.at[c])

    for c in range(EARLY // rows, CHUNKS):
        fetch(c).start()
    buffer[...] = jnp.zeros_like(buffer)

    def clear(i, _):
        row = (i ^ MIRROR) * SIZE
        used[i] = row
        for k in range(CAP):
            label[row + k * NV] = 0
        return 0

    lax.fori_loop(0, PEERS, clear, 0)
    for copy in lists:
        copy.wait()
    sub = subl(8)

    def place_of(row, f):
        target = dest[f, row]
        device = lax.shift_right_logical(target, 7) & (PEERS - 1)
        live = f < count[0, row]
        at = used[device]
        used[device] = jnp.where(live, at + NV, at)
        place = jnp.where(live, at, PEERS * SIZE)
        label[place] = (target & (T - 1)) + 1
        return place

    def chunk(c, given, skipped):
        for r in range(0, rows, 2):
            row = c * rows + r
            places = [[place_of(row + q, f) for f in range(FAN)] for q in range(2)]
            pair = surf[pl.ds(pl.multiple_of(row * NV, 8), 8), :]
            pair = jnp.concatenate(
                [jnp.where(sub < NV, pair, 0.0), jnp.where(sub >= NV, pair, 0.0)], axis=1
            ).astype(bf16)
            for f in range(0, FAN, 2):
                block = jnp.concatenate(
                    [
                        jnp.concatenate([given[row + q - skipped, f + g] for g in range(2)], axis=1)
                        for q in range(2)
                    ],
                    axis=0,
                )
                product = jnp.dot(pair, block, preferred_element_type=f32)
                for q in range(2):
                    for g in range(2):
                        part = product[q * NV : (q + 1) * NV, g * T : (g + 1) * T]
                        buffer[pl.ds(places[q][f + g], NV), :] = part

    def near(c, _):
        chunk(c, early, 0)
        return 0

    def far(c, _):
        fetch(c).wait()
        chunk(c, blocks, EARLY)
        return 0

    lax.fori_loop(0, EARLY // rows, near, 0)
    lax.fori_loop(EARLY // rows, CHUNKS, far, 0)
    lane = lanes(1)

    def name(i, _):
        line = jnp.zeros((1, T), i32)
        for k in range(CAP):
            line = jnp.where(lane == k, label[i * SIZE + k * NV], line)
        names[pl.ds(i, 1), :] = line.astype(f32)
        return 0

    lax.fori_loop(0, PEERS, name, 0, unroll=8)
    lane = lanes(PEERS)
    rims = jnp.zeros((PEERS, T), f32)
    for j in range(CAP * NV):
        column = EDGE + 2 * j
        turned = pltpu.roll(buffer[pl.ds(j, PEERS, stride=SIZE), :], (column + 1) % T, 1)
        rims = jnp.where((lane >> 1) == column >> 1, turned, rims)
    lane, sub = lanes(8), subl(8)
    left_end, right_end = sub == MIRROR, sub == MIRROR - 1
    for b in range(PEERS // 8):
        own, rim = names[b * 8 : b * 8 + 8, :], rims[b * 8 : b * 8 + 8, :]
        left_name, left_rim = (jnp.where(left_end, 0.0, pltpu.roll(x, 1, 0)) for x in (own, rim))
        right_name, right_rim = (jnp.where(right_end, 0.0, pltpu.roll(x, 7, 0)) for x in (own, rim))
        line = own + pltpu.roll(left_name, CAP, 1) + pltpu.roll(right_name, 2 * CAP, 1)
        line = line + jnp.where((lane & 1) == 0, left_rim, right_rim)
        buffer[pl.ds(b * 8 * SIZE + SIZE - 1, 8, stride=SIZE), :] = line
    run([pltpu.make_async_copy(buffer.at[pl.ds(0, PEERS * SIZE)], out, sems.at[0])])


def remap(dest, count, surf, weight, early, after):
    return pl.pallas_call(
        remap_kernel,
        in_specs=[HBM, HBM, VMEM, HBM, VMEM, HBM],
        out_specs=HBM,
        out_shape=jax.ShapeDtypeStruct((PEERS * SIZE, T), f32),
        scratch_shapes=[
            pltpu.VMEM((T - EARLY, FAN, T, T), bf16),
            pltpu.VMEM((PEERS * SIZE + 8, T), f32),
            pltpu.VMEM((PEERS, T), f32),
            pltpu.SMEM((FAN, T), i32),
            pltpu.SMEM((1, T), i32),
            pltpu.SMEM((PEERS,), i32),
            pltpu.SMEM((PEERS * SIZE + 8,), i32),
            pltpu.SemaphoreType.DMA((CHUNKS + 2,)),
        ],
        compiler_params=params(44 * MIB),
        cost_estimate=cost(67 << 20, 20 << 20),
        name="remap",
    )(dest, count, surf, weight, early, after)


def sealed(block, *after):
    def kernel(*refs):
        del refs

    return pl.pallas_call(
        kernel,
        in_specs=[HBM] * (1 + len(after)),
        out_specs=HBM,
        out_shape=jax.ShapeDtypeStruct(block.shape, block.dtype),
        input_output_aliases={0: 0},
        compiler_params=params(MIB),
        name="sealed",
    )(block, *after)


def merged(left, right, back=2):
    return jnp.where((lanes(left.shape[0]) & 1) == 0, left, pltpu.roll(right, T - back, 1))


def diffuse(u, up, down, side, rate):
    rows = u.shape[0]
    lane, sub = lanes(rows), subl(rows)
    north = jnp.where(sub == 0, up, pltpu.roll(u, 1, 0))
    south = jnp.where(sub == rows - 1, down, pltpu.roll(u, rows - 1, 0))
    west = jnp.where(lane == 0, side, pltpu.roll(u, 1, 1))
    east = jnp.where(lane == T - 1, side, pltpu.roll(u, T - 1, 1))
    return u + rate * ((north + south) + (west + east) - 4.0 * u)


def level_diffuse(u, top, bottom, side, rate, l, lo):
    up = top[l : l + 1, :] if lo == 0 else u[l, lo - 1 : lo, :]
    down = bottom[l : l + 1, :] if lo + HALF == T else u[l, lo + HALF : lo + HALF + 1, :]
    spin = side[lo : lo + HALF, :]
    if l:
        spin = pltpu.roll(spin, T - 2 * l, 1)
    return diffuse(u[l, lo : lo + HALF, :], up, down, spin, rate)


def halo_columns(rate, left, right, own):
    lane, sub = lanes(T), subl(T)
    here = merged(left[0:T, :], right[0:T, :])
    outer = merged(pltpu.roll(left[COL_NEXT : COL_NEXT + T, :], 1, 1), right[COL_NEXT : COL_NEXT + T, :], 3)
    inner = pltpu.roll(own[0:T, :], T - 1, 1)
    ends = [merged(left[at : at + 8, :], right[at : at + 8, :])[0:1, :] for at in (COL_TOP, COL_BOTTOM)]
    north = jnp.where(sub == 0, ends[0], pltpu.roll(here, 1, 0))
    south = jnp.where(sub == T - 1, ends[1], pltpu.roll(here, T - 1, 0))
    plane = ((lane + 1) >> 1) & (PLANES - 1)
    number = jnp.full((T, T), rate[0, 0], f32)
    for v in range(1, NV):
        number = jnp.where(plane // LEV == v, rate[0, v], number)
    h = here + number * ((north + south) + (outer + inner) - 4.0 * here)
    coef = jnp.where(
        (lane & 1) == 0,
        jnp.broadcast_to(left[COL_COEF : COL_COEF + T, 0:1], (T, T)),
        jnp.broadcast_to(right[COL_COEF : COL_COEF + T, 1:2], (T, T)),
    )
    level = plane % LEV
    above = jnp.where(level < LEV - 1, pltpu.roll(h, T - 2, 1) - h, 0.0)
    below = jnp.where(level > 0, pltpu.roll(h, 2, 1) - h, 0.0)
    return here, h + coef * (above + below)


def halo_rows(rate, rows, own, left, right, k, v):
    at = v * LEV
    lane, level = lanes(LEV), subl(LEV)
    here = rows[at : at + LEV, :]
    corner = COL_COEF + k * PLANES + at
    west = jnp.where(
        lane == 0, pltpu.roll(left[corner : corner + LEV, :], T - 4, 1), pltpu.roll(here, 1, 1)
    )
    east = jnp.where(
        lane == T - 1,
        pltpu.roll(right[corner : corner + LEV, :], T - 6, 1),
        pltpu.roll(here, T - 1, 1),
    )
    outer = rows[PLANES + at : PLANES + at + LEV, :]
    inner = own[at : at + LEV, :]
    h = here + rate[0, v] * ((outer + inner) + (west + east) - 4.0 * here)
    above = jnp.where(level < LEV - 1, pltpu.roll(h, LEV - 1, 0) - h, 0.0)
    below = jnp.where(level > 0, pltpu.roll(h, 1, 0) - h, 0.0)
    return h + rows[ROW_VERT : ROW_VERT + 1, :] * (above + below)


def step_kernel(
    rate, state, coef, sea, own, top, bottom, near, far,
    out, keep, u, w, stage, inner, top1, bottom1, top2, bottom2, side1, side2, turned, sems,
):
    def emit(v):
        levels = pl.ds(2, LEV - 2)
        return pltpu.make_async_copy(stage.at[v], out.at[0, v, levels], sems.at[v])

    loads = [pltpu.make_async_copy(state.at[0, v], u.at[v], sems.at[v]) for v in range(NV)]
    for load in loads:
        load.start()
    up, down, _, _ = inside()
    side1[...], side2[...] = halo_columns(rate, near, far, own)
    for v in range(NV):
        loads[v].wait()
        at = v * LEV
        for l in range(LEV):
            inner[0, at + l : at + l + 1, :] = u[v, l, 0:1, :] * up
            inner[1, at + l : at + l + 1, :] = u[v, l, T - 1 : T, :] * down
    for v in range(NV):
        at = v * LEV
        top1[v] = top[at : at + LEV, :]
        bottom1[v] = bottom[at : at + LEV, :]
        top2[v] = halo_rows(rate, top, inner.at[0], near, far, 0, v)
        bottom2[v] = halo_rows(rate, bottom, inner.at[1], near, far, 1, v)

    def first(v, _):
        number = rate[0, v]
        turned[...] = pltpu.roll(side1[...], lax.rem((NV - v) * 32, T), 1)
        source, result = u.at[v], w.at[v]
        for lo in range(0, T, HALF):
            mix = coef[lo : lo + HALF, :]
            at = lambda l: level_diffuse(source, top1.at[v], bottom1.at[v], turned, number, l, lo)
            before, here = None, at(0)
            for l in range(LEV):
                after = at(l + 1) if l + 1 < LEV else None
                if before is None:
                    term = after - here
                elif after is None:
                    term = before - here
                else:
                    term = (after - here) + (before - here)
                result[l, lo : lo + HALF, :] = here + mix * term
                before, here = here, after
        return 0

    lax.fori_loop(0, NV, first, 0)

    def second(v, _):
        number = rate[0, v]
        turned[...] = pltpu.roll(side2[...], lax.rem((NV - v) * 32, T), 1)
        source, result = w.at[v], stage.at[v]
        for lo in range(0, T, HALF):
            mix = coef[lo : lo + HALF, :]
            at = lambda l: level_diffuse(source, top2.at[v], bottom2.at[v], turned, number, l, lo)
            before, here = at(1), at(2)
            row = pl.multiple_of(v * T + lo, 8)
            keep[pl.ds(KEEP_BASE + row, HALF), :] = source[0, lo : lo + HALF, :]
            keep[pl.ds(KEEP_ONE + row, HALF), :] = before
            keep[pl.ds(KEEP_PART + row, HALF), :] = before + mix * ((here - before) - before)
            for l in range(2, LEV):
                after = at(l + 1) if l + 1 < LEV else None
                term = before - here
                if after is not None:
                    term = (after - here) + term
                result[l - 2, lo : lo + HALF, :] = here + mix * term
                before, here = here, after
        emit(v).start()
        return 0

    lax.fori_loop(0, NV, second, 0)
    keep[KEEP_VERT : KEEP_VERT + T, :] = coef[...]
    keep[KEEP_SEA : KEEP_SEA + T, :] = sea[...]
    keep[KEEP_SIDE : KEEP_SIDE + T, :] = side2[...]
    coefs = pl.ds(COL_COEF, T)
    keep[KEEP_SEA_SIDE : KEEP_SEA_SIDE + T, :] = jnp.where(
        lanes(T) == 0, pltpu.roll(near[coefs, :], T - 2, 1), pltpu.roll(far[coefs, :], T - 4, 1)
    )
    for k, (rows, line) in enumerate(((top2, top), (bottom2, bottom))):
        for v in range(NV):
            keep[KEEP_ENDS + 8 * k + v : KEEP_ENDS + 8 * k + v + 1, :] = rows[v, 0:1, :]
        keep[KEEP_ENDS + 8 * k + NV : KEEP_ENDS + 8 * k + 8, :] = line[ROW_SEA : ROW_SEA + NV, :]
    for v in range(NV):
        emit(v).wait()


def two_steps(rate, state, coef, sea, own, top, bottom, left, right):
    rows = pltpu.VMEM((NV, LEV, T), f32)
    square = pltpu.VMEM((T, T), f32)
    return pl.pallas_call(
        step_kernel,
        in_specs=[SMEM, HBM] + [VMEM] * 7,
        out_specs=[HBM, VMEM],
        out_shape=[
            jax.ShapeDtypeStruct(state.shape, f32),
            jax.ShapeDtypeStruct((KEEP_SIZE, T), f32),
        ],
        scratch_shapes=[
            pltpu.VMEM((NV, LEV, T, T), f32),
            pltpu.VMEM((NV, LEV, T, T), f32),
            pltpu.VMEM((NV, LEV - 2, T, T), f32),
            pltpu.VMEM((2, PLANES, T), f32),
            rows,
            rows,
            rows,
            rows,
            square,
            square,
            square,
            pltpu.SemaphoreType.DMA((NV,)),
        ],
        compiler_params=params(20 * MIB),
        cost_estimate=cost(48 << 20, 10 << 20),
        name="two_steps",
    )(rate, state, coef, sea, own, top, bottom, left, right)


def unpack_kernel(data, after, imp, first, last):
    del after
    sub = subl(T).astype(f32) + 1.0
    line = data[pl.ds(SIZE - 1, PEERS, stride=SIZE), :]
    fields = jnp.transpose(jnp.concatenate([line, jnp.zeros((T - PEERS, T), f32)], axis=0))

    def two(at, size):
        return fields[at : at + size, :] + pltpu.roll(fields[at + size : at + 2 * size, :], PEERS, 1)

    def split(x):
        high = x.astype(bf16)
        return high, (x - high.astype(f32)).astype(bf16)

    def picks(at):
        return jnp.concatenate(
            [(sub == two(at + k, 1)).astype(bf16) for k in range(0, CAP, 2)], axis=1
        )

    pick = picks(0)
    up, down, _, _ = inside()
    for v in range(NV):
        block = jnp.concatenate(
            [data[pl.ds(k * NV + v, PEERS, stride=SIZE), :] for k in range(CAP)], axis=0
        )
        high, low = split(block)
        total = jnp.dot(pick, high, preferred_element_type=f32)
        total = total + jnp.dot(pick, low, preferred_element_type=f32)
        imp[v * T : (v + 1) * T, :] = total
        for out, row, keep in ((first, 0, up), (last, T - 1, down)):
            out[v : v + 1, :] = total[row : row + 1, :] * keep
            out[NV + v : NV + v + 1, :] = total[row : row + 1, :] * keep
    rims = jnp.concatenate([two(EDGE + 8 * k, 8) for k in range(0, CAP, 2)], axis=1)
    sides = []
    for at in (CAP, 2 * CAP):
        pick = picks(at)
        high, low = (
            lax.dot_general(part, pick, (((1,), (1,)), ((), ())), preferred_element_type=f32)
            for part in split(rims)
        )
        sides.append(high + low)
    imp[NV * T : NV * T + 8, :] = jnp.where((subl(8) & 1) == 0, sides[0], sides[1])


def unpack(data, after):
    return pl.pallas_call(
        unpack_kernel,
        in_specs=[VMEM, HBM],
        out_specs=[VMEM] * 3,
        out_shape=[
            jax.ShapeDtypeStruct((NV * T + 8, T), f32),
            jax.ShapeDtypeStruct((2 * NV, T), f32),
            jax.ShapeDtypeStruct((2 * NV, T), f32),
        ],
        compiler_params=params(12 * MIB),
        cost_estimate=cost(200 << 20, 2 << 20),
        name="unpack",
    )(data, after)


def final_kernel(
    horiz, relax, mid, near, imp, imp_top, imp_bottom, out, stage, sems
):
    del mid
    ends = jnp.concatenate([imp[NV * T : NV * T + 8, :], jnp.zeros((T - 8, T), f32)], axis=0)
    side_new = jnp.transpose(ends)
    sea, sea_side = near[KEEP_SEA : KEEP_SEA + T, :], near[KEEP_SEA_SIDE : KEEP_SEA_SIDE + T, :]
    coef = near[KEEP_VERT : KEEP_VERT + T, :]
    side_base = near[KEEP_SIDE : KEEP_SIDE + T, :]
    lane = lanes(T)
    copies = []
    for v in range(NV):
        pull = relax[0, v]

        def relaxed(base, wet, new, pull=pull):
            return base + pull * wet * (new - base)

        ends = []
        for k, new in enumerate((imp_top, imp_bottom)):
            at = KEEP_ENDS + 8 * k
            ends.append(
                relaxed(near[at + v : at + v + 1, :], near[at + NV : at + NV + 1, :], new[v : v + 1, :])
            )
        turn = (T - 32 * v) % T
        base = pltpu.roll(side_base, turn, 1) if turn else side_base
        new = pltpu.roll(side_new, T - 2 * v, 1) if v else side_new
        new = jnp.where(lane == 0, new, pltpu.roll(side_new, T - 2 - 2 * v, 1))
        mine = imp[v * T : (v + 1) * T, :]
        u = relaxed(near[KEEP_BASE + v * T : KEEP_BASE + (v + 1) * T, :], sea, mine)
        h = diffuse(u, ends[0], ends[1], relaxed(base, sea_side, new), horiz[0, v])
        one = near[KEEP_ONE + v * T : KEEP_ONE + (v + 1) * T, :]
        stage[v, 0] = relaxed(h + coef * (one - h), sea, mine)
        stage[v, 1] = near[KEEP_PART + v * T : KEEP_PART + (v + 1) * T, :] + coef * h
        copies.append(
            pltpu.make_async_copy(stage.at[v], out.at[0, v, pl.ds(0, 2)], sems.at[v])
        )
        copies[-1].start()
    for copy in copies:
        copy.wait()


def final(horiz, relax, mid, keep, imp, imp_rows):
    return pl.pallas_call(
        final_kernel,
        in_specs=[SMEM, SMEM, HBM] + [VMEM] * 4,
        out_specs=HBM,
        out_shape=jax.ShapeDtypeStruct(mid.shape, f32),
        input_output_aliases={2: 0},
        scratch_shapes=[
            pltpu.VMEM((NV, 2, T, T), f32),
            pltpu.SemaphoreType.DMA((NV,)),
        ],
        compiler_params=params(6 * MIB),
        cost_estimate=cost(2 << 20, 3 << 20),
        name="final",
    )(horiz, relax, mid, keep, imp, *imp_rows)


def shifted(block, axis, by):
    count = lax.axis_size(axis)
    return lax.ppermute(block, axis, [(i, (i + by) % count) for i in range(count)])


def crossed(block, gx_by=0):
    size = lax.axis_size("gx"), lax.axis_size("gy")
    route = []
    for c in range(2):
        for i in range(size[0]):
            for j in range(size[1]):
                to = (1 - c) * size[0] + (i + gx_by) % size[0]
                route.append(((c * size[0] + i) * size[1] + j, to * size[1] + (j ^ MIRROR)))
    return lax.ppermute(block, ("comp", "gx", "gy"), route)


def local(
    state, horiz_coef, vert_coef, couple_rate, sea_mask, dest_block, entry_count, remap_weight
):
    head, tail = outer_rows(state, vert_coef, sea_mask)
    top, bottom = shifted(tail, "gx", 1), shifted(head, "gx", -1)
    cols, surf, coef, sea, early = outer_columns(state, vert_coef, sea_mask, remap_weight)
    cols = with_corners(cols, top, bottom)
    left, right = shifted(cols, "gy", 1), shifted(cols, "gy", -1)
    dest = dest_block.reshape(T, FAN).T
    packed = remap(dest, entry_count.reshape(1, T), surf, remap_weight, early, cols)
    packed = sealed(packed, left, right).reshape(PEERS, SIZE, 1, T)
    packed = lax.all_to_all(packed, ("gx", "gy"), split_axis=0, concat_axis=0, tiled=True)
    mid, keep = two_steps(horiz_coef, state, coef, sea, cols, top, bottom, left, right)
    new, first, last = unpack(packed.reshape(PEERS * SIZE, T), keep)
    imp = crossed(new)
    imp_rows = crossed(last, 1), crossed(first, -1)
    return final(horiz_coef, couple_rate, mid, keep, imp, imp_rows)


def solution(mesh):
    in_specs = (
        P("comp", None, None, "gx", "gy"),
        P("comp", None),
        P("comp", "gx", "gy"),
        P("comp", None),
        P("comp", "gx", "gy"),
        P("comp", "gx", "gy", None),
        P("comp", "gx", "gy"),
        P("comp", "gx", "gy", None, None, None),
    )
    out_specs = P("comp", None, None, "gx", "gy")
    return jax.shard_map(local, mesh=mesh, in_specs=in_specs, out_specs=out_specs, check_vma=False)
```

```python
import jax
import jax.numpy as jnp
from jax import lax
from jax.experimental import pallas as pl
from jax.experimental.pallas import tpu as pltpu
from jax.sharding import PartitionSpec as P

NV = 4
LEV = 16
PLANES = NV * LEV
T = 128
FAN = 4
CAP = 8
PEERS = 64
SIZE = CAP * NV + 1
EDGE = 32
HALF = 64
CHUNKS = 16
EARLY = 32
MIRROR = 4
MIB = 1024 * 1024
LIMIT = 58 * MIB
ROW_VERT = 2 * PLANES
ROW_SEA = ROW_VERT + 8
ROW_SIZE = ROW_SEA + 8
COL_NEXT = T
COL_COEF = 2 * T
COL_TOP = COL_COEF + 8
COL_BOTTOM = COL_TOP + 8
COL_SIZE = COL_BOTTOM + 8
KEEP_BASE = 0
KEEP_ONE = NV * T
KEEP_PART = 2 * NV * T
KEEP_VERT = 3 * NV * T
KEEP_SEA = KEEP_VERT + T
KEEP_SIDE = KEEP_SEA + T
KEEP_SEA_SIDE = KEEP_SIDE + T
KEEP_ENDS = KEEP_SEA_SIDE + T
KEEP_SIZE = KEEP_ENDS + 16

f32 = jnp.float32
i32 = jnp.int32
bf16 = jnp.bfloat16

SMEM = pl.BlockSpec(memory_space=pltpu.SMEM)
VMEM = pl.BlockSpec(memory_space=pltpu.VMEM)
HBM = pl.BlockSpec(memory_space=pl.ANY)


def params(limit=LIMIT):
    return pltpu.CompilerParams(vmem_limit_bytes=limit)


def cost(flops, size):
    return pl.CostEstimate(flops=flops, bytes_accessed=size, transcendentals=0)


def lanes(rows):
    return lax.broadcasted_iota(i32, (rows, T), 1)


def subl(rows):
    return lax.broadcasted_iota(i32, (rows, T), 0)


def inside():
    gx, gy = lax.axis_index("gx"), lax.axis_index("gy")
    one = lambda test: jnp.where(test, 1.0, 0.0).astype(f32)
    return (
        one(gx > 0),
        one(gx < lax.axis_size("gx") - 1),
        one(gy > 0),
        one(gy < lax.axis_size("gy") - 1),
    )


def column_keep(rows, later=0):
    _, _, before, after = inside()
    return jnp.where((lanes(rows) & 1) == later, after, before)


def run(copies):
    for copy in copies:
        copy.start()
    for copy in copies:
        copy.wait()


def row_kernel(state, vert, mask, head, tail, high, low, coef, sea, sems):
    ends = pl.ds(0, 8), pl.ds(T - 8, 8)
    copies = []
    for k, buffer in enumerate((high, low)):
        copies.append(pltpu.make_async_copy(state.at[0, :, :, ends[k]], buffer, sems.at[3 * k]))
        copies.append(pltpu.make_async_copy(vert.at[0, ends[k]], coef.at[k], sems.at[3 * k + 1]))
        copies.append(pltpu.make_async_copy(mask.at[0, ends[k]], sea.at[k], sems.at[3 * k + 2]))
    run(copies)
    up, down, _, _ = inside()
    for k, (out, buffer, keep) in enumerate(((head, high, up), (tail, low, down))):
        outer, following = (0, 1) if k == 0 else (7, 6)
        flat = buffer.reshape(PLANES * 8, T)
        out[0:PLANES, :] = flat[pl.ds(outer, PLANES, stride=8), :] * keep
        out[PLANES : 2 * PLANES, :] = flat[pl.ds(following, PLANES, stride=8), :] * keep
        line = coef[k, outer : outer + 1, :] * keep
        out[ROW_VERT : ROW_VERT + 8, :] = jnp.broadcast_to(line, (8, T))
        line = sea[k, outer : outer + 1, :].astype(f32) * keep
        out[ROW_SEA : ROW_SEA + 8, :] = jnp.broadcast_to(line, (8, T))


def outer_rows(state, vert, mask):
    return pl.pallas_call(
        row_kernel,
        in_specs=[HBM, HBM, HBM],
        out_specs=[VMEM, VMEM],
        out_shape=[jax.ShapeDtypeStruct((ROW_SIZE, T), f32)] * 2,
        scratch_shapes=[
            pltpu.VMEM((NV, LEV, 8, T), f32),
            pltpu.VMEM((NV, LEV, 8, T), f32),
            pltpu.VMEM((2, 8, T), f32),
            pltpu.VMEM((2, 8, T), i32),
            pltpu.SemaphoreType.DMA((6,)),
        ],
        compiler_params=params(),
        cost_estimate=cost(1 << 16, 1 << 19),
        name="outer_rows",
    )(state, vert, mask)


def column_kernel(state, vert, mask, weight, cols, surf, coef, wet, early, tile, sea, sems):
    loads = [pltpu.make_async_copy(state.at[0, v], tile.at[v], sems.at[v]) for v in range(NV)]
    loads.append(pltpu.make_async_copy(vert.at[0], coef, sems.at[NV]))
    loads.append(pltpu.make_async_copy(mask.at[0], sea, sems.at[NV + 1]))
    loads.append(pltpu.make_async_copy(weight.at[0, pl.ds(0, EARLY), 0], early, sems.at[NV + 2]))
    for load in loads:
        load.start()
    lane = lanes(HALF)
    keep = column_keep(HALF)
    keep2 = column_keep(HALF, 1)
    for v in range(NV):
        loads[v].wait()
        surf[pl.ds(v, T, stride=NV), :] = tile[v, 0]
        for lo in range(0, T, HALF):
            outer, following = pl.ds(lo, HALF), pl.ds(COL_NEXT + lo, HALF)
            acc = jnp.zeros((HALF, T), f32) if v == 0 else cols[outer, :]
            acc2 = jnp.zeros((HALF, T), f32) if v == 0 else cols[following, :]
            for l in range(LEV):
                p = v * LEV + l
                plane = tile[v, l, lo : lo + HALF, :]
                turned = pltpu.roll(plane, (2 * p + 1) % T, 1)
                acc = jnp.where((lane >> 1) == p, turned, acc)
                acc2 = jnp.where((lane == (2 * p - 1) % T) | (lane == (2 * p + 2) % T), turned, acc2)
            last = v == NV - 1
            cols[outer, :] = acc * keep if last else acc
            cols[following, :] = acc2 * keep2 if last else acc2
    loads[NV].wait()
    loads[NV + 1].wait()
    lane = lanes(T)
    wet[...] = sea[...].astype(f32)
    pair = jnp.where(lane < 2, pltpu.roll(coef[...], 1, 1), pltpu.roll(wet[...], 3, 1))
    cols[COL_COEF : COL_COEF + 8, :] = jnp.transpose(pair * column_keep(T))[0:8, :]
    loads[NV + 2].wait()


def outer_columns(state, vert, mask, weight):
    square = jax.ShapeDtypeStruct((T, T), f32)
    return pl.pallas_call(
        column_kernel,
        in_specs=[HBM] * 4,
        out_specs=[VMEM] * 5,
        out_shape=[
            jax.ShapeDtypeStruct((COL_TOP, T), f32),
            jax.ShapeDtypeStruct((T * NV, T), f32),
            square,
            square,
            jax.ShapeDtypeStruct((EARLY, FAN, T, T), bf16),
        ],
        scratch_shapes=[
            pltpu.VMEM((NV, LEV, T, T), f32),
            pltpu.VMEM((T, T), i32),
            pltpu.SemaphoreType.DMA((NV + 3,)),
        ],
        compiler_params=params(46 * MIB),
        cost_estimate=cost(6 << 20, 9 << 20),
        name="outer_columns",
    )(state, vert, mask, weight)


def corner_kernel(cols, top, bottom, out):
    out[0:COL_TOP, :] = cols[...]
    lane, sub = lanes(PLANES), subl(PLANES)
    keep = column_keep(PLANES)
    for k, rows in enumerate((top, bottom)):
        line = rows[0:PLANES, :]
        first = jnp.broadcast_to(line[:, 0:1], (PLANES, T))
        last = jnp.broadcast_to(line[:, T - 1 : T], (PLANES, T))
        spread = jnp.where(lane == 2 * sub, last, jnp.where(lane == 2 * sub + 1, first, 0.0))
        total = jnp.sum(spread * keep, axis=0, keepdims=True)
        at = COL_TOP + 8 * k
        out[at : at + 8, :] = jnp.broadcast_to(total, (8, T))


def with_corners(cols, top, bottom):
    return pl.pallas_call(
        corner_kernel,
        in_specs=[VMEM] * 3,
        out_specs=VMEM,
        out_shape=jax.ShapeDtypeStruct((COL_SIZE, T), f32),
        compiler_params=params(4 * MIB),
        cost_estimate=cost(1 << 16, 1 << 18),
        name="with_corners",
    )(cols, top, bottom)


def remap_kernel(
    dest_in, count_in, surf, weight, early, after, out, blocks, buffer, names, dest, count, used, label, sems
):
    del after
    rows = T // CHUNKS
    lists = [
        pltpu.make_async_copy(dest_in, dest, sems.at[CHUNKS]),
        pltpu.make_async_copy(count_in, count, sems.at[CHUNKS + 1]),
    ]
    for copy in lists:
        copy.start()

    def fetch(c):
        piece = pl.ds(c * rows, rows)
        there = pl.ds(c * rows - EARLY, rows)
        return pltpu.make_async_copy(weight.at[0, piece, 0], blocks.at[there], sems.at[c])

    for c in range(EARLY // rows, CHUNKS):
        fetch(c).start()
    buffer[...] = jnp.zeros_like(buffer)

    def clear(i, _):
        row = (i ^ MIRROR) * SIZE
        used[i] = row
        for k in range(CAP):
            label[row + k * NV] = 0
        return 0

    lax.fori_loop(0, PEERS, clear, 0)
    for copy in lists:
        copy.wait()
    sub = subl(8)

    def place_of(row, f):
        target = dest[f, row]
        device = lax.shift_right_logical(target, 7) & (PEERS - 1)
        live = f < count[0, row]
        at = used[device]
        used[device] = jnp.where(live, at + NV, at)
        place = jnp.where(live, at, PEERS * SIZE)
        label[place] = (target & (T - 1)) + 1
        return place

    def chunk(c, given, skipped):
        for r in range(0, rows, 2):
            row = c * rows + r
            places = [[place_of(row + q, f) for f in range(FAN)] for q in range(2)]
            pair = surf[pl.ds(pl.multiple_of(row * NV, 8), 8), :]
            pair = jnp.concatenate(
                [jnp.where(sub < NV, pair, 0.0), jnp.where(sub >= NV, pair, 0.0)], axis=1
            ).astype(bf16)
            for f in range(0, FAN, 2):
                block = jnp.concatenate(
                    [
                        jnp.concatenate([given[row + q - skipped, f + g] for g in range(2)], axis=1)
                        for q in range(2)
                    ],
                    axis=0,
                )
                product = jnp.dot(pair, block, preferred_element_type=f32)
                for q in range(2):
                    for g in range(2):
                        part = product[q * NV : (q + 1) * NV, g * T : (g + 1) * T]
                        buffer[pl.ds(places[q][f + g], NV), :] = part

    def near(c, _):
        chunk(c, early, 0)
        return 0

    def far(c, _):
        fetch(c).wait()
        chunk(c, blocks, EARLY)
        return 0

    lax.fori_loop(0, EARLY // rows, near, 0)
    lax.fori_loop(EARLY // rows, CHUNKS, far, 0)
    lane = lanes(1)

    def name(i, _):
        line = jnp.zeros((1, T), i32)
        for k in range(CAP):
            line = jnp.where(lane == k, label[i * SIZE + k * NV], line)
        names[pl.ds(i, 1), :] = line.astype(f32)
        return 0

    lax.fori_loop(0, PEERS, name, 0, unroll=8)
    lane = lanes(PEERS)
    rims = jnp.zeros((PEERS, T), f32)
    for j in range(CAP * NV):
        column = EDGE + 2 * j
        turned = pltpu.roll(buffer[pl.ds(j, PEERS, stride=SIZE), :], (column + 1) % T, 1)
        rims = jnp.where((lane >> 1) == column >> 1, turned, rims)
    lane, sub = lanes(8), subl(8)
    left_end, right_end = sub == MIRROR, sub == MIRROR - 1
    for b in range(PEERS // 8):
        own, rim = names[b * 8 : b * 8 + 8, :], rims[b * 8 : b * 8 + 8, :]
        left_name, left_rim = (jnp.where(left_end, 0.0, pltpu.roll(x, 1, 0)) for x in (own, rim))
        right_name, right_rim = (jnp.where(right_end, 0.0, pltpu.roll(x, 7, 0)) for x in (own, rim))
        line = own + pltpu.roll(left_name, CAP, 1) + pltpu.roll(right_name, 2 * CAP, 1)
        line = line + jnp.where((lane & 1) == 0, left_rim, right_rim)
        buffer[pl.ds(b * 8 * SIZE + SIZE - 1, 8, stride=SIZE), :] = line
    run([pltpu.make_async_copy(buffer.at[pl.ds(0, PEERS * SIZE)], out, sems.at[0])])


def remap(dest, count, surf, weight, early, after):
    return pl.pallas_call(
        remap_kernel,
        in_specs=[HBM, HBM, VMEM, HBM, VMEM, HBM],
        out_specs=HBM,
        out_shape=jax.ShapeDtypeStruct((PEERS * SIZE, T), f32),
        scratch_shapes=[
            pltpu.VMEM((T - EARLY, FAN, T, T), bf16),
            pltpu.VMEM((PEERS * SIZE + 8, T), f32),
            pltpu.VMEM((PEERS, T), f32),
            pltpu.SMEM((FAN, T), i32),
            pltpu.SMEM((1, T), i32),
            pltpu.SMEM((PEERS,), i32),
            pltpu.SMEM((PEERS * SIZE + 8,), i32),
            pltpu.SemaphoreType.DMA((CHUNKS + 2,)),
        ],
        compiler_params=params(44 * MIB),
        cost_estimate=cost(67 << 20, 20 << 20),
        name="remap",
    )(dest, count, surf, weight, early, after)


def sealed(block, *after):
    def kernel(*refs):
        del refs

    return pl.pallas_call(
        kernel,
        in_specs=[HBM] * (1 + len(after)),
        out_specs=HBM,
        out_shape=jax.ShapeDtypeStruct(block.shape, block.dtype),
        input_output_aliases={0: 0},
        compiler_params=params(MIB),
        name="sealed",
    )(block, *after)


def merged(left, right, back=2):
    return jnp.where((lanes(left.shape[0]) & 1) == 0, left, pltpu.roll(right, T - back, 1))


def diffuse(u, up, down, side, rate):
    rows = u.shape[0]
    lane, sub = lanes(rows), subl(rows)
    north = jnp.where(sub == 0, up, pltpu.roll(u, 1, 0))
    south = jnp.where(sub == rows - 1, down, pltpu.roll(u, rows - 1, 0))
    west = jnp.where(lane == 0, side, pltpu.roll(u, 1, 1))
    east = jnp.where(lane == T - 1, side, pltpu.roll(u, T - 1, 1))
    return u + rate * ((north + south) + (west + east) - 4.0 * u)


def level_diffuse(u, top, bottom, side, rate, l, lo):
    up = top[l : l + 1, :] if lo == 0 else u[l, lo - 1 : lo, :]
    down = bottom[l : l + 1, :] if lo + HALF == T else u[l, lo + HALF : lo + HALF + 1, :]
    spin = side[lo : lo + HALF, :]
    if l:
        spin = pltpu.roll(spin, T - 2 * l, 1)
    return diffuse(u[l, lo : lo + HALF, :], up, down, spin, rate)


def halo_columns(rate, left, right, sides, own):
    lane, sub = lanes(T), subl(T)
    here = merged(left[0:T, :], right[0:T, :])
    outer = merged(pltpu.roll(left[COL_NEXT : COL_NEXT + T, :], 1, 1), right[COL_NEXT : COL_NEXT + T, :], 3)
    inner = pltpu.roll(own[0:T, :], T - 1, 1)
    ends = [merged(left[at : at + 8, :], right[at : at + 8, :])[0:1, :] for at in (COL_TOP, COL_BOTTOM)]
    north = jnp.where(sub == 0, ends[0], pltpu.roll(here, 1, 0))
    south = jnp.where(sub == T - 1, ends[1], pltpu.roll(here, T - 1, 0))
    plane = ((lane + 1) >> 1) & (PLANES - 1)
    number = jnp.full((T, T), rate[0, 0], f32)
    for v in range(1, NV):
        number = jnp.where(plane // LEV == v, rate[0, v], number)
    h = here + number * ((north + south) + (outer + inner) - 4.0 * here)
    coef = jnp.where(
        (lane & 1) == 0,
        jnp.broadcast_to(sides[0][:, 0:1], (T, T)),
        jnp.broadcast_to(sides[1][:, 1:2], (T, T)),
    )
    level = plane % LEV
    above = jnp.where(level < LEV - 1, pltpu.roll(h, T - 2, 1) - h, 0.0)
    below = jnp.where(level > 0, pltpu.roll(h, 2, 1) - h, 0.0)
    return here, h + coef * (above + below)


def halo_rows(rate, rows, own, left, right, k, v):
    at = v * LEV
    lane, level = lanes(LEV), subl(LEV)
    here = rows[at : at + LEV, :]
    edge = COL_TOP + 8 * k

    def corner(message, later):
        line = jnp.broadcast_to(message[edge : edge + 1, :], (LEV, T))
        return jnp.sum(jnp.where(lane == 2 * (at + level) + later, line, 0.0), axis=1, keepdims=True)

    west = jnp.where(lane == 0, corner(left, 0), pltpu.roll(here, 1, 1))
    east = jnp.where(lane == T - 1, corner(right, 1), pltpu.roll(here, T - 1, 1))
    outer = rows[PLANES + at : PLANES + at + LEV, :]
    inner = own[at : at + LEV, :]
    h = here + rate[0, v] * ((outer + inner) + (west + east) - 4.0 * here)
    above = jnp.where(level < LEV - 1, pltpu.roll(h, LEV - 1, 0) - h, 0.0)
    below = jnp.where(level > 0, pltpu.roll(h, 1, 0) - h, 0.0)
    return h + rows[ROW_VERT : ROW_VERT + 1, :] * (above + below)


def step_kernel(
    rate, state, coef, sea, own, top, bottom, near, far,
    out, keep, u, w, stage, inner, top1, bottom1, top2, bottom2, side1, side2, turned, sems,
):
    def emit(v):
        levels = pl.ds(2, LEV - 2)
        return pltpu.make_async_copy(stage.at[v], out.at[0, v, levels], sems.at[v])

    loads = [pltpu.make_async_copy(state.at[0, v], u.at[v], sems.at[v]) for v in range(NV)]
    for load in loads:
        load.start()
    up, down, _, _ = inside()
    rest = jnp.zeros((T - 8, T), f32)
    sides = [
        jnp.transpose(jnp.concatenate([x[COL_COEF : COL_COEF + 8, :], rest], axis=0))
        for x in (near, far)
    ]
    side1[...], side2[...] = halo_columns(rate, near, far, sides, own)
    keep[KEEP_SEA_SIDE : KEEP_SEA_SIDE + T, :] = jnp.where(
        lanes(T) == 0, pltpu.roll(sides[0], T - 2, 1), pltpu.roll(sides[1], T - 4, 1)
    )
    for v in range(NV):
        loads[v].wait()
        at = v * LEV
        for l in range(LEV):
            inner[0, at + l : at + l + 1, :] = u[v, l, 0:1, :] * up
            inner[1, at + l : at + l + 1, :] = u[v, l, T - 1 : T, :] * down
    for v in range(NV):
        at = v * LEV
        top1[v] = top[at : at + LEV, :]
        bottom1[v] = bottom[at : at + LEV, :]
        top2[v] = halo_rows(rate, top, inner.at[0], near, far, 0, v)
        bottom2[v] = halo_rows(rate, bottom, inner.at[1], near, far, 1, v)

    def first(v, _):
        number = rate[0, v]
        turned[...] = pltpu.roll(side1[...], lax.rem((NV - v) * 32, T), 1)
        source, result = u.at[v], w.at[v]
        for lo in range(0, T, HALF):
            mix = coef[lo : lo + HALF, :]
            at = lambda l: level_diffuse(source, top1.at[v], bottom1.at[v], turned, number, l, lo)
            before, here = None, at(0)
            for l in range(LEV):
                after = at(l + 1) if l + 1 < LEV else None
                if before is None:
                    term = after - here
                elif after is None:
                    term = before - here
                else:
                    term = (after - here) + (before - here)
                result[l, lo : lo + HALF, :] = here + mix * term
                before, here = here, after
        return 0

    lax.fori_loop(0, NV, first, 0)

    def second(v, _):
        number = rate[0, v]
        turned[...] = pltpu.roll(side2[...], lax.rem((NV - v) * 32, T), 1)
        source, result = w.at[v], stage.at[v]
        for lo in range(0, T, HALF):
            mix = coef[lo : lo + HALF, :]
            at = lambda l: level_diffuse(source, top2.at[v], bottom2.at[v], turned, number, l, lo)
            before, here = at(1), at(2)
            row = pl.multiple_of(v * T + lo, 8)
            keep[pl.ds(KEEP_BASE + row, HALF), :] = source[0, lo : lo + HALF, :]
            keep[pl.ds(KEEP_ONE + row, HALF), :] = before
            keep[pl.ds(KEEP_PART + row, HALF), :] = before + mix * ((here - before) - before)
            for l in range(2, LEV):
                after = at(l + 1) if l + 1 < LEV else None
                term = before - here
                if after is not None:
                    term = (after - here) + term
                result[l - 2, lo : lo + HALF, :] = here + mix * term
                before, here = here, after
        emit(v).start()
        return 0

    lax.fori_loop(0, NV, second, 0)
    keep[KEEP_VERT : KEEP_VERT + T, :] = coef[...]
    keep[KEEP_SEA : KEEP_SEA + T, :] = sea[...]
    keep[KEEP_SIDE : KEEP_SIDE + T, :] = side2[...]
    for k, (rows, line) in enumerate(((top2, top), (bottom2, bottom))):
        for v in range(NV):
            keep[KEEP_ENDS + 8 * k + v : KEEP_ENDS + 8 * k + v + 1, :] = rows[v, 0:1, :]
        keep[KEEP_ENDS + 8 * k + NV : KEEP_ENDS + 8 * k + 8, :] = line[ROW_SEA : ROW_SEA + NV, :]
    for v in range(NV):
        emit(v).wait()


def two_steps(rate, state, coef, sea, own, top, bottom, left, right):
    rows = pltpu.VMEM((NV, LEV, T), f32)
    square = pltpu.VMEM((T, T), f32)
    return pl.pallas_call(
        step_kernel,
        in_specs=[SMEM, HBM] + [VMEM] * 7,
        out_specs=[HBM, VMEM],
        out_shape=[
            jax.ShapeDtypeStruct(state.shape, f32),
            jax.ShapeDtypeStruct((KEEP_SIZE, T), f32),
        ],
        scratch_shapes=[
            pltpu.VMEM((NV, LEV, T, T), f32),
            pltpu.VMEM((NV, LEV, T, T), f32),
            pltpu.VMEM((NV, LEV - 2, T, T), f32),
            pltpu.VMEM((2, PLANES, T), f32),
            rows,
            rows,
            rows,
            rows,
            square,
            square,
            square,
            pltpu.SemaphoreType.DMA((NV,)),
        ],
        compiler_params=params(20 * MIB),
        cost_estimate=cost(48 << 20, 10 << 20),
        name="two_steps",
    )(rate, state, coef, sea, own, top, bottom, left, right)


def unpack_kernel(data, after, imp, first, last):
    del after
    sub = subl(T).astype(f32) + 1.0
    line = data[pl.ds(SIZE - 1, PEERS, stride=SIZE), :]
    fields = jnp.transpose(jnp.concatenate([line, jnp.zeros((T - PEERS, T), f32)], axis=0))

    def two(at, size):
        return fields[at : at + size, :] + pltpu.roll(fields[at + size : at + 2 * size, :], PEERS, 1)

    def split(x):
        high = x.astype(bf16)
        return high, (x - high.astype(f32)).astype(bf16)

    def picks(at):
        return jnp.concatenate(
            [(sub == two(at + k, 1)).astype(bf16) for k in range(0, CAP, 2)], axis=1
        )

    pick = picks(0)
    up, down, _, _ = inside()
    for v in range(NV):
        block = jnp.concatenate(
            [data[pl.ds(k * NV + v, PEERS, stride=SIZE), :] for k in range(CAP)], axis=0
        )
        high, low = split(block)
        total = jnp.dot(pick, high, preferred_element_type=f32)
        total = total + jnp.dot(pick, low, preferred_element_type=f32)
        imp[v * T : (v + 1) * T, :] = total
        for out, row, keep in ((first, 0, up), (last, T - 1, down)):
            out[v : v + 1, :] = total[row : row + 1, :] * keep
            out[NV + v : NV + v + 1, :] = total[row : row + 1, :] * keep
    rims = jnp.concatenate([two(EDGE + 8 * k, 8) for k in range(0, CAP, 2)], axis=1)
    sides = []
    for at in (CAP, 2 * CAP):
        pick = picks(at)
        high, low = (
            lax.dot_general(part, pick, (((1,), (1,)), ((), ())), preferred_element_type=f32)
            for part in split(rims)
        )
        sides.append(high + low)
    imp[NV * T : NV * T + 8, :] = jnp.where((subl(8) & 1) == 0, sides[0], sides[1])


def unpack(data, after):
    return pl.pallas_call(
        unpack_kernel,
        in_specs=[VMEM, HBM],
        out_specs=[VMEM] * 3,
        out_shape=[
            jax.ShapeDtypeStruct((NV * T + 8, T), f32),
            jax.ShapeDtypeStruct((2 * NV, T), f32),
            jax.ShapeDtypeStruct((2 * NV, T), f32),
        ],
        compiler_params=params(12 * MIB),
        cost_estimate=cost(200 << 20, 2 << 20),
        name="unpack",
    )(data, after)


def final_kernel(
    horiz, relax, mid, near, imp, imp_top, imp_bottom, out, stage, sems
):
    del mid
    ends = jnp.concatenate([imp[NV * T : NV * T + 8, :], jnp.zeros((T - 8, T), f32)], axis=0)
    side_new = jnp.transpose(ends)
    sea, sea_side = near[KEEP_SEA : KEEP_SEA + T, :], near[KEEP_SEA_SIDE : KEEP_SEA_SIDE + T, :]
    coef = near[KEEP_VERT : KEEP_VERT + T, :]
    side_base = near[KEEP_SIDE : KEEP_SIDE + T, :]
    lane = lanes(T)
    copies = []
    for v in range(NV):
        pull = relax[0, v]

        def relaxed(base, wet, new, pull=pull):
            return base + pull * wet * (new - base)

        ends = []
        for k, new in enumerate((imp_top, imp_bottom)):
            at = KEEP_ENDS + 8 * k
            ends.append(
                relaxed(near[at + v : at + v + 1, :], near[at + NV : at + NV + 1, :], new[v : v + 1, :])
            )
        turn = (T - 32 * v) % T
        base = pltpu.roll(side_base, turn, 1) if turn else side_base
        new = pltpu.roll(side_new, T - 2 * v, 1) if v else side_new
        new = jnp.where(lane == 0, new, pltpu.roll(side_new, T - 2 - 2 * v, 1))
        mine = imp[v * T : (v + 1) * T, :]
        u = relaxed(near[KEEP_BASE + v * T : KEEP_BASE + (v + 1) * T, :], sea, mine)
        h = diffuse(u, ends[0], ends[1], relaxed(base, sea_side, new), horiz[0, v])
        one = near[KEEP_ONE + v * T : KEEP_ONE + (v + 1) * T, :]
        stage[v, 0] = relaxed(h + coef * (one - h), sea, mine)
        stage[v, 1] = near[KEEP_PART + v * T : KEEP_PART + (v + 1) * T, :] + coef * h
        copies.append(
            pltpu.make_async_copy(stage.at[v], out.at[0, v, pl.ds(0, 2)], sems.at[v])
        )
        copies[-1].start()
    for copy in copies:
        copy.wait()


def final(horiz, relax, mid, keep, imp, imp_rows):
    return pl.pallas_call(
        final_kernel,
        in_specs=[SMEM, SMEM, HBM] + [VMEM] * 4,
        out_specs=HBM,
        out_shape=jax.ShapeDtypeStruct(mid.shape, f32),
        input_output_aliases={2: 0},
        scratch_shapes=[
            pltpu.VMEM((NV, 2, T, T), f32),
            pltpu.SemaphoreType.DMA((NV,)),
        ],
        compiler_params=params(6 * MIB),
        cost_estimate=cost(2 << 20, 3 << 20),
        name="final",
    )(horiz, relax, mid, keep, imp, *imp_rows)


def shifted(block, axis, by):
    count = lax.axis_size(axis)
    return lax.ppermute(block, axis, [(i, (i + by) % count) for i in range(count)])


def crossed(block, gx_by=0):
    size = lax.axis_size("gx"), lax.axis_size("gy")
    route = []
    for c in range(2):
        for i in range(size[0]):
            for j in range(size[1]):
                to = (1 - c) * size[0] + (i + gx_by) % size[0]
                route.append(((c * size[0] + i) * size[1] + j, to * size[1] + (j ^ MIRROR)))
    return lax.ppermute(block, ("comp", "gx", "gy"), route)


def local(
    state, horiz_coef, vert_coef, couple_rate, sea_mask, dest_block, entry_count, remap_weight
):
    head, tail = outer_rows(state, vert_coef, sea_mask)
    top, bottom = shifted(tail, "gx", 1), shifted(head, "gx", -1)
    cols, surf, coef, sea, early = outer_columns(state, vert_coef, sea_mask, remap_weight)
    cols = with_corners(cols, top, bottom)
    left, right = shifted(cols, "gy", 1), shifted(cols, "gy", -1)
    dest = dest_block.reshape(T, FAN).T
    packed = remap(dest, entry_count.reshape(1, T), surf, remap_weight, early, cols)
    packed = sealed(packed, left, right).reshape(PEERS, SIZE, 1, T)
    packed = lax.all_to_all(packed, ("gx", "gy"), split_axis=0, concat_axis=0, tiled=True)
    mid, keep = two_steps(horiz_coef, state, coef, sea, cols, top, bottom, left, right)
    new, first, last = unpack(packed.reshape(PEERS * SIZE, T), keep)
    imp = crossed(new)
    imp_rows = crossed(last, 1), crossed(first, -1)
    return final(horiz_coef, couple_rate, mid, keep, imp, imp_rows)


def solution(mesh):
    in_specs = (
        P("comp", None, None, "gx", "gy"),
        P("comp", None),
        P("comp", "gx", "gy"),
        P("comp", None),
        P("comp", "gx", "gy"),
        P("comp", "gx", "gy", None),
        P("comp", "gx", "gy"),
        P("comp", "gx", "gy", None, None, None),
    )
    out_specs = P("comp", None, None, "gx", "gy")
    return jax.shard_map(local, mesh=mesh, in_specs=in_specs, out_specs=out_specs, check_vma=False)
```
